32 devices in a mesh: groups: 2 (over y), gz: 4 (over z), view: 2 (over x), gy: 2 (over core).
Axes of the slice: x: 2, y: 2, z: 4, core: 2. Of those that a mesh axis runs over, the one named last changes fastest.
Arguments:
- camera: float32 [2, 256, 3, 128, 128], P('view', ('groups', 'gz'), None, 'gy'), parts along dimension 1, may hold values from 0 to 4
- background: int32 [2, 2, 8], P('view', 'gy', ('groups', 'gz')), parts along dimension 2, may hold values from 0 to 2
- destination: int32 [2, 2, 256, 1], P('view', 'gy', ('groups', 'gz')), parts along dimension 2, may hold values from 0 to 3; in each aligned block of 32 rows (0 to 31, 32 to 63, ..., all dimensions but the last counted through in order) at most 16 rows name the same one
- offsets: int32 [2, 2, 256], P('view', 'gy', ('groups', 'gz')), parts along dimension 2, may hold values from 0 to 6
- shift_frac: float32 [2, 3], P('view'), may hold values from 0.15 to 0.85
- psf_taps: float32 [2, 3, 9], P('view'), may hold values from 0.05 to 1
Outputs:
- estimate: float32 [64, 128, 128], P(('groups', 'gz'), 'gy'), parts along dimension 0
- joined_views: float32 [2, 64, 128, 128], P('view', ('groups', 'gz'), 'gy'), parts along dimension 1
The draws below stay inside these ranges and needn't reach their ends.
There are 2 independent parts, one for each index of `groups`. The reference program is written for one: setup_inputs(seed, part) draws one part's arguments, and reference() takes and returns one part's arrays. A program takes and returns all parts, laid end to end along the dimension named above; an argument that names none is the same for every part. Nothing has to cross between parts.
Inputs may be any that keep to these rules, and one draw needn't show every extreme that they name: `destination`: within the 32 block rows of one tile, no slab is named more than 16 times; some tile names one slab exactly 16 times.
All inputs are finite; a program needn't handle non-finite values.
Results may differ from the reference program's by a relative error of at most 0.0001.
Values sent between devices are 32-bit elements; how exact they have to be, the bound alone decides.
No kernel may reach another device: no remote copies, remote signals or barrier semaphores. Data moves between devices by JAX's collectives and lax.ppermute only.
A program may use at most 64 MiB of HBM per device.

```python
import math
import jax
import jax.numpy as jnp
import numpy as np
from jax import lax

CZ = 8
CY = 64
CX = 128
NB = 32
BZ = 3
TAPS = 9
ITERS = 2
VIEWS = 2
MOST = 16
NZ = 32
NY = 128
NBLK = 128
N_GZ = 4
N_GY = 2


def touch_ends(values, own_key, low, largest):
    index_at = [jax.random.randint(jax.random.fold_in(own_key, axis), (), 0, length) for axis, length in enumerate(values.shape)]
    widest = values.shape.index(max(values.shape))
    beside = index_at[:widest] + [(index_at[widest] + 1) % values.shape[widest]] + index_at[widest + 1:]
    return values.at[tuple(index_at)].set(low).at[tuple(beside)].set(largest)


def block_scale(stream_key, extent, cuts, least, largest):
    factor_of = 1.0
    for axis_at, shards_of in cuts:
        steps = jax.random.uniform(jax.random.fold_in(jax.random.fold_in(stream_key, 6), axis_at), (shards_of,), jnp.float32, least / len(cuts), largest / len(cuts))
        factor_of = factor_of * jnp.repeat(jnp.exp(steps), extent[axis_at] // shards_of).reshape((-1,) + (1,) * (len(extent) - 1 - axis_at))
    return factor_of


def shared_out(rng, own, number, rows, count, top, bound, slope):
    ranking = jax.random.permutation(rng, count)
    crowded, usual = load_shares(count, rows * top, bound, slope, True), load_shares(count, rows * top, bound, slope, False)
    places = jnp.arange(count)

    def named(tallies, turn):
        used = int((tallies > 0).sum())
        fixed = max(1, used // 4)
        shifted = fixed + (places - fixed + turn * (used - fixed)) % max(1, count - fixed)
        return jnp.zeros((count,), jnp.int32).at[ranking[jnp.where(places < fixed, places, shifted)]].set(jnp.asarray(tallies, jnp.int32))

    tallies = jnp.where(number % 4 == 0, named(crowded, number // 4), named(usual, number - number // 4 - 1))
    mixed = jax.random.permutation(jax.random.fold_in(own, 3), count)
    giver, receiver = mixed[0:count // 2 * 2:2], mixed[1:count // 2 * 2:2]
    room = jnp.minimum(tallies[giver] - 1, bound - tallies[receiver]) // 2
    room = jnp.where((giver == ranking[0]) | (receiver == ranking[0]) | (tallies[receiver] == 0), 0, jnp.maximum(room, 0))
    shifted = jax.random.randint(jax.random.fold_in(own, 4), (count // 2,), 0, 1 << 20) % (room + 1)
    tallies = tallies.at[giver].add(-shifted).at[receiver].add(shifted)
    members = jnp.searchsorted(jnp.cumsum(tallies), jnp.arange(rows * top), side="right").astype(jnp.int32)
    listing = members.reshape(top, rows).T
    listing = listing[jax.random.permutation(jax.random.fold_in(own, 1), rows)]
    turn = jax.random.randint(jax.random.fold_in(own, 2), (rows, 1), 0, top)
    return jnp.take_along_axis(listing, (jnp.arange(top)[None, :] + turn) % top, axis=1)


def load_shares(amount, total, reach, lean, full):
    loads = [(1 << 20) // math.isqrt(rank ** lean) + 1 for rank in range(1, amount + 1)]
    largest = reach if full else min(reach, max(-(-total // amount), total * loads[0] // sum(loads)))
    least = 1 if total - largest >= amount - 1 else 0
    holding, spare = [largest] + [least] * (amount - 1), total - largest - least * (amount - 1)
    while spare > 0:
        free = [i for i in range(1, amount) if holding[i] < largest] or [i for i in range(1, amount) if holding[i] < reach]
        whole, budget = sum([loads[i] for i in free]), spare
        for i in free:
            extra = min(reach - holding[i], max(1, budget * loads[i] // whole), spare)
            holding[i] = holding[i] + extra
            spare = spare - extra
    return np.array(holding)


def setup_inputs(seed: int = 0, part: int = 0) -> dict:
    seeds = jax.random.split(jax.random.key(seed), 7)
    own_keys = jax.random.split(jax.random.fold_in(seeds[6], part), 7)
    camera = jnp.clip(4.0 * jax.random.uniform(own_keys[0], (VIEWS, NBLK, BZ, NY, CX), jnp.float32) ** block_scale(own_keys[0], (VIEWS, NBLK, BZ, NY, CX), ((0, 2), (1, 4), (3, 2)), -0.2, 0.2), 0.0, 4.0)
    background = touch_ends(jax.random.randint(own_keys[1], (VIEWS, N_GY, N_GZ), 0, 3), jax.random.fold_in(own_keys[1], 1), 0, 2).astype(jnp.int32)
    destination_keys = jax.random.split(jax.random.fold_in(own_keys[2], 1), VIEWS * N_GY * NBLK // NB)
    destination_turns = jax.random.permutation(jax.random.fold_in(own_keys[2], 3), VIEWS * N_GY * NBLK // NB)
    destination = jax.vmap(lambda own, number: shared_out(jax.random.fold_in(own_keys[2], 2), own, number, NB, N_GZ, 1, MOST, 2))(destination_keys, destination_turns).reshape((VIEWS, N_GY, NBLK, 1))
    offsets = touch_ends(jax.random.randint(own_keys[3], (VIEWS, N_GY, NBLK), 0, CZ - 1), jax.random.fold_in(own_keys[3], 1), 0, (CZ - 1) - 1).astype(jnp.int32)
    shift_frac = jnp.clip(0.15 + 0.70000002 * jax.random.uniform(seeds[4], (VIEWS, 3), jnp.float32) ** block_scale(seeds[4], (VIEWS, 3), ((0, 2),), -0.2, 0.2), 0.15, 0.85)
    psf_taps = jnp.clip(jnp.exp(math.log(1.0) - 2.9957323 * jax.random.uniform(seeds[5], (VIEWS, 3, TAPS), jnp.float32) ** block_scale(seeds[5], (VIEWS, 3, TAPS), ((0, 2),), -0.2, 0.2)), 0.05, 1.0)
    return {"camera": camera, "background": background, "destination": destination, "offsets": offsets, "shift_frac": shift_frac, "psf_taps": psf_taps}


DATA_FLOOR = 0.25
PRECISE = lax.Precision.HIGHEST


def interp_matrix(length, fraction):
    places = jnp.arange(length, dtype=jnp.int32)
    follow = jnp.minimum(places + 1, length - 1)
    same_row = (places[:, None] == places[None, :]).astype(jnp.float32)
    next_row = (follow[:, None] == places[None, :]).astype(jnp.float32)
    return (1.0 - fraction) * same_row + fraction * next_row


def interp_blocks(blocks, fraction_z, y_matrix, x_matrix):
    lower = blocks[..., :-1, :, :]
    upper = blocks[..., 1:, :, :]
    planes = (1.0 - fraction_z) * lower + fraction_z * upper
    planes = jnp.einsum("ry,...yx->...rx", y_matrix, planes, precision=PRECISE)
    return jnp.einsum("...rx,cx->...rc", planes, x_matrix, precision=PRECISE)


def along_last(volume, weights):
    margin = weights.shape[0] // 2
    span_cells = volume.shape[-1]
    padded = jnp.pad(volume, [(0, 0)] * (volume.ndim - 1) + [(margin, margin)])
    result = weights[0] * padded[..., 0:span_cells]
    for offset in range(1, weights.shape[0]):
        result = result + weights[offset] * padded[..., offset:offset + span_cells]
    return result


def valid_pass(padded, weights, out_len, along_axis):
    result = weights[0] * lax.slice_in_dim(padded, 0, out_len, axis=along_axis)
    for offset in range(1, weights.shape[0]):
        result = result + weights[offset] * lax.slice_in_dim(padded, offset, offset + out_len, axis=along_axis)
    return result


def apply_passes(padded, kernel, planes_out, rows_out):
    x_done = along_last(padded, kernel[2])
    y_done = valid_pass(x_done, kernel[1], rows_out, 1)
    return valid_pass(y_done, kernel[0], planes_out, 0)


def blur_whole(volume, kernel):
    margin = kernel.shape[1] // 2
    padded = jnp.pad(volume, ((margin, margin), (margin, margin), (0, 0)))
    return apply_passes(padded, kernel, volume.shape[0], volume.shape[1])


def reference(camera, background, destination, offsets, shift_frac, psf_taps):
    joined_list = []
    for view_idx in range(VIEWS):
        fraction = shift_frac[view_idx]
        y_matrix = interp_matrix(CY, fraction[1])
        x_matrix = interp_matrix(CX, fraction[2])
        columns = []
        for row_idx in range(N_GY):
            tiles = camera[view_idx, :, :, row_idx * CY:(row_idx + 1) * CY, :]
            levels = jnp.repeat(background[view_idx, row_idx], NB).astype(jnp.float32)
            blocks = tiles - levels[:, None, None, None]
            planes = interp_blocks(blocks, fraction[0], y_matrix, x_matrix)
            start_plane = destination[view_idx, row_idx, :, 0] * CZ + offsets[view_idx, row_idx]
            target = (start_plane[:, None] + jnp.arange(BZ - 1, dtype=jnp.int32)[None, :]).reshape(-1).astype(jnp.int32)
            total = jax.ops.segment_sum(planes.reshape(-1, CY, CX), target, num_segments=NZ)
            covered = jax.ops.segment_sum(jnp.ones(target.shape, jnp.float32), target, num_segments=NZ)
            columns.append(jnp.maximum(total / (covered[:, None, None] + 1.0), DATA_FLOOR))
        joined_list.append(jnp.concatenate(columns, axis=1))
    joined_views = jnp.stack(joined_list)
    kernels = psf_taps / jnp.sum(psf_taps, axis=-1, keepdims=True)
    estimate = jnp.sum(joined_views, axis=0) / VIEWS
    for iteration in range(ITERS):
        log_total = jnp.zeros(estimate.shape, jnp.float32)
        for view_idx in range(VIEWS):
            blurred = blur_whole(estimate, kernels[view_idx])
            ratio = joined_views[view_idx] / blurred
            correction = blur_whole(ratio, kernels[view_idx][:, ::-1])
            log_total = log_total + jnp.log(correction)
        estimate = estimate * jnp.exp(log_total / VIEWS)
    return estimate, joined_views
```

```python
import functools

import jax
import jax.numpy as jnp
from jax import lax
from jax.experimental import pallas as pl
from jax.experimental.pallas import tpu as pltpu
from jax.sharding import PartitionSpec as P

CZ = 8
ITERS = 2


DATA_FLOOR = 0.25
PRECISE = lax.Precision.HIGHEST
F32 = jnp.float32
SUB = 8
SMEM = pl.BlockSpec(memory_space=pltpu.SMEM)
VMEM = pl.BlockSpec(memory_space=pltpu.VMEM)
VMEM_BYTES = 48 * 1024 * 1024


def bit_count(count):
    bits = count.bit_length() - 1
    assert count == 1 << bits
    return bits


def reversed_bits(value, bits):
    result = 0
    for bit in range(bits):
        result = result | (((value >> bit) & 1) << (bits - 1 - bit))
    return result


def deposit_kernel(place_ref, target_ref, first_ref, level_ref, fraction_ref, camera_ref, out_ref, *, bits, section):
    per_step, planes, rows, cols = camera_ref.shape
    step = pl.program_id(0)

    @pl.when(step == 0)
    def _():
        out_ref[...] = jnp.zeros(out_ref.shape, F32)

    level = level_ref[0].astype(F32)
    fraction = fraction_ref[0]
    keep = 1.0 - fraction
    plane_at = lax.broadcasted_iota(jnp.int32, (CZ, cols), 0)

    def one(index, carry):
        block = step * per_step + index
        slab = reversed_bits(target_ref[block] ^ place_ref[0], bits)
        first = first_ref[block]
        start = pl.multiple_of(slab * section, SUB)
        base = pl.multiple_of(start + first * rows, SUB)
        lower = camera_ref[index, 0] - level
        for plane in range(planes - 1):
            upper = camera_ref[index, plane + 1] - level
            here = pl.ds(pl.multiple_of(base + plane * rows, SUB), rows)
            out_ref[here, :] += keep * lower + fraction * upper
            lower = upper
        counts = pl.ds(pl.multiple_of(start + CZ * rows, SUB), CZ)
        landed = (plane_at >= first) & (plane_at < first + planes - 1)
        out_ref[counts, :] += landed.astype(F32)
        return carry

    lax.fori_loop(0, per_step, one, 0)


def deposit(camera, target, first, level, fraction, place, slabs):
    blocks, planes, rows, cols = camera.shape
    section = CZ * rows + CZ
    per_step = SUB if blocks % SUB == 0 else 1
    return pl.pallas_call(
        functools.partial(deposit_kernel, bits=bit_count(slabs), section=section),
        grid=(blocks // per_step,),
        in_specs=[SMEM] * 5 + [pl.BlockSpec((per_step, planes, rows, cols), lambda i: (i, 0, 0, 0))],
        out_specs=pl.BlockSpec((slabs * section, cols), lambda i: (0, 0)),
        out_shape=jax.ShapeDtypeStruct((slabs * section, cols), F32),
        compiler_params=pltpu.CompilerParams(vmem_limit_bytes=VMEM_BYTES),
        name="deposit",
    )(place, target, first, level, fraction, camera)


def butterfly(sums, slabs, section):
    bits = bit_count(slabs)
    own = sums
    count = slabs
    late = None
    for bit in range(bits):
        half = count // 2
        pairs = [(i, i ^ (1 << bit)) for i in range(slabs)]
        keep, send = own[: half * section], own[half * section :]
        if late is not None:
            send = send + late[1]
            keep = keep + late[0]
        if half > 1:
            cut = half // 2 * section
            onward = lax.ppermute(send[cut:], "gz", pairs)
            stays = lax.ppermute(send[:cut], "gz", pairs)
            late = (stays, onward)
            next_half = half // 2
            own = keep
        else:
            arrived = lax.ppermute(send, "gz", pairs)
            return keep, arrived
        count = half
    return own, jnp.zeros_like(own)


def join_kernel(fraction_ref, kept_ref, arrived_ref, taps_ref, joined_ref, message_ref, *, rows):
    cols = kept_ref.shape[1]
    total = kept_ref[...] + arrived_ref[...]
    planes = total[: CZ * rows].reshape(CZ, rows, cols)
    counts = total[CZ * rows :]
    fy, fx = fraction_ref[1], fraction_ref[2]
    row_at = lax.broadcasted_iota(jnp.int32, (rows, cols), 0)
    col_at = lax.broadcasted_iota(jnp.int32, (rows, cols), 1)
    for plane in range(CZ):
        part = planes[plane]
        follow = jnp.where(row_at == rows - 1, part, pltpu.roll(part, rows - 1, 0))
        part = (1.0 - fy) * part + fy * follow
        follow = jnp.where(col_at == cols - 1, part, pltpu.roll(part, cols - 1, 1))
        part = (1.0 - fx) * part + fx * follow
        part = jnp.maximum(part / (counts[plane : plane + 1] + 1.0), DATA_FLOOR)
        joined_ref[plane] = part
        message_ref[plane * rows : (plane + 1) * rows] = part
    message_ref[CZ * rows :] = taps_ref[...]


def join(kept, arrived, fraction, taps, rows):
    cols = kept.shape[1]
    return pl.pallas_call(
        functools.partial(join_kernel, rows=rows),
        in_specs=[SMEM, VMEM, VMEM, VMEM],
        out_specs=[VMEM, VMEM],
        out_shape=[jax.ShapeDtypeStruct((CZ, rows, cols), F32), jax.ShapeDtypeStruct(kept.shape, F32)],
        compiler_params=pltpu.CompilerParams(vmem_limit_bytes=VMEM_BYTES),
        name="join",
    )(fraction, kept, arrived, taps)


def taps_sum(values, weights):
    result = weights[0] * values[0]
    for offset in range(1, len(weights)):
        result = result + weights[offset] * values[offset]
    return result


def update_kernel(
    flag_ref, taps_ref, band_ref, own_ref, below_ref, above_ref, low_rows_ref, high_rows_ref, *rest, views, margin, first
):
    if first:
        out_ref, *scratch = rest
    else:
        est_ref, est_below_ref, est_above_ref, est_low_ref, est_high_ref, out_ref, *scratch = rest
    estimate, joined, first_pass, second_pass, ratio, back_first, back_second = scratch
    _, planes, rows, cols = own_ref.shape
    wide = 2 * margin
    flag_low, flag_high = flag_ref[0], flag_ref[1]
    low, body, high = slice(0, wide), slice(wide, wide + rows), slice(wide + rows, 2 * wide + rows)

    def spread_rows(ref, part):
        return [(body, part[0], part[1], None), (low, part[2], part[3], flag_low), (high, part[4], part[3], flag_high)]

    below_at = 0
    above_at = below_ref.shape[0]
    own_at = 2 * above_at
    for view in range(views):
        pieces = (
            (0, margin, below_ref, view * margin, below_at + view * margin),
            (margin, planes, own_ref.at[view], 0, own_at + view * planes),
            (margin + planes, margin, above_ref, view * margin, above_at + view * margin),
        )
        for to, length, source, at, edge_at in pieces:
            joined[view, to : to + length, body] = source[at : at + length]
            joined[view, to : to + length, low] = low_rows_ref[edge_at : edge_at + length] * flag_low
            joined[view, to : to + length, high] = high_rows_ref[edge_at : edge_at + length] * flag_high
    if first:
        inner = joined[0]
        for view in range(1, views):
            inner = inner + joined[view]
        estimate[margin : margin + planes + 2 * margin] = inner / views
        at = views * margin
        for to, source, edge_at in ((0, below_ref, below_at + at), (planes + 3 * margin, above_ref, above_at + at)):
            estimate[to : to + margin, body] = source[at : at + margin]
            estimate[to : to + margin, low] = low_rows_ref[edge_at : edge_at + margin] * flag_low
            estimate[to : to + margin, high] = high_rows_ref[edge_at : edge_at + margin] * flag_high
    else:
        for to, source, edge_at in ((0, est_below_ref, 0), (planes, est_ref, planes), (2 * planes, est_above_ref, 2 * planes)):
            estimate[to : to + planes, body] = source[...]
            estimate[to : to + planes, low] = est_low_ref[edge_at : edge_at + planes] * flag_low
            estimate[to : to + planes, high] = est_high_ref[edge_at : edge_at + planes] * flag_high

    taps = 2 * margin + 1
    mid_planes, mid_rows = planes + 2 * margin, rows + 2 * margin
    weights = [[[taps_ref[(view * 3 + dim) * taps + tap] for tap in range(taps)] for dim in range(3)] for view in range(views)]

    def along_z(tile, carry):
        here = pl.ds(pl.multiple_of(tile * SUB, SUB), SUB)
        values = [estimate[plane, here, :] for plane in range(planes + 4 * margin)]
        for view in range(views):
            for plane in range(mid_planes):
                first_pass[view, plane, here, :] = taps_sum(values[plane : plane + taps], weights[view][0])
        return carry

    lax.fori_loop(0, (rows + 4 * margin) // SUB, along_z, 0)

    def along_y(plane, carry):
        for view in range(views):
            values = [first_pass[view, plane, tap : tap + mid_rows, :] for tap in range(taps)]
            second_pass[view, plane] = taps_sum(values, weights[view][1])
        return carry

    lax.fori_loop(0, mid_planes, along_y, 0)

    per = 4
    for view in range(views):
        def along_x(index, carry, view=view):
            here = pl.ds(index * per, per)
            values = second_pass[view, here].reshape(per * mid_rows, cols)
            blurred = jnp.dot(values, band_ref[view, 0], precision=PRECISE, preferred_element_type=F32)
            ratio[view, here] = joined[view, here, margin : margin + mid_rows, :] / blurred.reshape(per, mid_rows, cols)
            return carry

        lax.fori_loop(0, mid_planes // per, along_x, 0)

    def back_z(tile, carry):
        here = pl.ds(pl.multiple_of(tile * SUB, SUB), SUB)
        for view in range(views):
            values = [ratio[view, plane, here, :] for plane in range(mid_planes)]
            for plane in range(planes):
                back_first[view, plane, here, :] = taps_sum(values[plane : plane + taps], weights[view][0][::-1])
        return carry

    lax.fori_loop(0, mid_rows // SUB, back_z, 0)

    def back_y(plane, carry):
        for view in range(views):
            values = [back_first[view, plane, tap : tap + rows, :] for tap in range(taps)]
            back_second[view, plane] = taps_sum(values, weights[view][1][::-1])
        return carry

    lax.fori_loop(0, planes, back_y, 0)

    def back_x(index, carry):
        here = pl.ds(index * per, per)
        logs = None
        for view in range(views):
            values = back_second[view, here].reshape(per * rows, cols)
            correction = jnp.dot(values, band_ref[view, 1], precision=PRECISE, preferred_element_type=F32)
            one = jnp.log(correction)
            logs = one if logs is None else logs + one
        old = estimate[pl.ds(2 * margin + index * per, per), body, :]
        out_ref[here] = old * jnp.exp(logs / views).reshape(per, rows, cols)
        return carry

    lax.fori_loop(0, planes // per, back_x, 0)


def update(flags, taps, bands, own, below, above, low_rows, high_rows, later, margin):
    views, planes, rows, cols = own.shape
    arrays = [flags, taps, bands, own, below, above, low_rows, high_rows] + list(later)
    mid_planes, mid_rows = planes + 2 * margin, rows + 2 * margin
    scratch = [
        (planes + 4 * margin, rows + 4 * margin),
        (views, mid_planes, rows + 4 * margin),
        (views, mid_planes, rows + 4 * margin),
        (views, mid_planes, mid_rows),
        (views, mid_planes, mid_rows),
        (views, planes, mid_rows),
        (views, planes, rows),
    ]
    return pl.pallas_call(
        functools.partial(update_kernel, views=views, margin=margin, first=not later),
        in_specs=[SMEM, SMEM] + [VMEM] * (len(arrays) - 2),
        out_specs=VMEM,
        out_shape=jax.ShapeDtypeStruct((planes, rows, cols), F32),
        scratch_shapes=[pltpu.VMEM(shape + (cols,), F32) for shape in scratch],
        compiler_params=pltpu.CompilerParams(vmem_limit_bytes=VMEM_BYTES),
        name="update",
    )(*arrays)


def from_beside(axis, upward, downward):
    count = lax.axis_size(axis)
    up = [(i, i + 1) for i in range(count - 1)]
    down = [(target, source) for source, target in up]
    return lax.ppermute(upward, axis, up), lax.ppermute(downward, axis, down)


def edge_rows(pieces, width):
    count = lax.axis_size("gy")
    rows = pieces[0].shape[-2]
    if count == 2:
        at = jnp.where(lax.axis_index("gy") == 0, rows - width, 0)
        parts = [lax.dynamic_slice_in_dim(piece, at, width, axis=1) for piece in pieces]
        arrived = lax.ppermute(jnp.concatenate(parts), "gy", [(0, 1), (1, 0)])
        return arrived, arrived
    upward = jnp.concatenate([piece[:, rows - width :] for piece in pieces])
    downward = jnp.concatenate([piece[:, :width] for piece in pieces])
    return from_beside("gy", upward, downward)


def from_views(message):
    count = lax.axis_size("view")
    if count == 2:
        return jnp.stack([message, lax.ppermute(message, "view", [(0, 1), (1, 0)])])
    return lax.all_gather(message, "view")


def on_device(camera, background, destination, offsets, shift_frac, psf_taps):
    slabs = lax.axis_size("gz")
    views = lax.axis_size("view")
    _, blocks, _, rows, cols = camera.shape
    taps = psf_taps.shape[-1]
    margin = taps // 2
    section = CZ * rows + CZ
    place = lax.axis_index("gz").astype(jnp.int32).reshape(1)
    fraction = shift_frac[0]
    sums = deposit(
        camera[0], destination.reshape(blocks), offsets.reshape(blocks), background.reshape(1), fraction, place, slabs
    )
    kept, arrived = butterfly(sums, slabs, section)
    own_taps = jnp.pad(psf_taps[0], ((0, CZ - 3), (0, cols - taps)))
    joined, message = join(kept, arrived, fraction, own_taps, rows)

    messages = from_views(message)
    all_joined = messages[:, : CZ * rows].reshape(views, CZ, rows, cols)
    all_taps = messages[:, CZ * rows : CZ * rows + 3, :taps]
    kernels = all_taps / jnp.sum(all_taps, axis=-1, keepdims=True)
    places = jnp.arange(cols, dtype=jnp.int32)
    shift = places[:, None] - places[None, :] + margin
    band = sum(jnp.where(shift == tap, kernels[:, 2, tap, None, None], 0.0) for tap in range(taps))
    bands = jnp.stack([band, jnp.swapaxes(band, 1, 2)], axis=1)
    flat_taps = kernels.reshape(-1)

    estimate = jnp.sum(all_joined, axis=0) / views
    upward = jnp.concatenate([all_joined[:, CZ - margin :].reshape(views * margin, rows, cols), estimate[: CZ - margin]])
    downward = jnp.concatenate([all_joined[:, :margin].reshape(views * margin, rows, cols), estimate[margin:]])
    below, above = from_beside("gz", upward, downward)
    wide = 2 * margin
    low_rows, high_rows = edge_rows([below, above, all_joined.reshape(views * CZ, rows, cols)], wide)
    row_band = lax.axis_index("gy")
    flags = jnp.stack([row_band > 0, row_band < lax.axis_size("gy") - 1]).astype(F32)

    later = ()
    for iteration in range(ITERS):
        if iteration:
            est_below, est_above = from_beside("gz", estimate, estimate)
            later = (estimate, est_below, est_above) + edge_rows([est_below, estimate, est_above], wide)
        estimate = update(flags, flat_taps, bands, all_joined, below, above, low_rows, high_rows, later, margin)
    return (estimate, joined[None])


def solution(mesh):
    return jax.shard_map(
        on_device,
        mesh=mesh,
        in_specs=(
            P("view", ("groups", "gz"), None, "gy", None),
            P("view", "gy", ("groups", "gz")),
            P("view", "gy", ("groups", "gz"), None),
            P("view", "gy", ("groups", "gz")),
            P("view", None),
            P("view", None, None),
        ),
        out_specs=(P(("groups", "gz"), "gy", None), P("view", ("groups", "gz"), "gy", None)),
        check_vma=False,
    )
```

```python
import functools

import jax
import jax.numpy as jnp
from jax import lax
from jax.experimental import pallas as pl
from jax.experimental.pallas import tpu as pltpu
from jax.sharding import PartitionSpec as P

CZ = 8
ITERS = 2


DATA_FLOOR = 0.25
PRECISE = lax.Precision.HIGHEST
F32 = jnp.float32
SUB = 8
VMEM = pl.BlockSpec(memory_space=pltpu.VMEM)
HBM = pl.BlockSpec(memory_space=pltpu.HBM)
VMEM_BYTES = 48 * 1024 * 1024
DEPOSIT_VMEM_BYTES = 60 * 1024 * 1024


def bit_count(count):
    bits = count.bit_length() - 1
    assert count == 1 << bits
    return bits


def reversed_bits(value, bits):
    result = 0
    for bit in range(bits):
        result = result | (((value >> bit) & 1) << (bits - 1 - bit))
    return result


def deposit_kernel(
    target_hbm, first_hbm, level_hbm, fraction_hbm, camera_hbm, out_ref, target, first, level, fraction, camera,
    small_sems, camera_sems, *, bits, section, chunk
):
    blocks, planes, rows, cols = camera.shape
    sources = ((target_hbm, target), (first_hbm, first), (level_hbm, level), (fraction_hbm, fraction))
    smalls = [pltpu.make_async_copy(*pair, small_sems.at[i]) for i, pair in enumerate(sources)]
    parts = []
    for i in range(blocks // chunk):
        here = pl.ds(i * chunk, chunk)
        parts.append(pltpu.make_async_copy(camera_hbm.at[here], camera.at[here], camera_sems.at[i]))
    for copy in smalls + parts:
        copy.start()
    out_ref[...] = jnp.zeros(out_ref.shape, F32)
    for copy in smalls:
        copy.wait()
    place = lax.axis_index("gz").astype(jnp.int32)
    base_level = level[0].astype(F32)
    upper_share = fraction[0]
    lower_share = 1.0 - upper_share
    plane_at = lax.broadcasted_iota(jnp.int32, (CZ, cols), 0)

    def one(block, carry):
        slab = reversed_bits(target[block] ^ place, bits)
        at = first[block]
        start = pl.multiple_of(slab * section, SUB)
        base = pl.multiple_of(start + at * rows, SUB)
        lower = camera[block, 0] - base_level
        for plane in range(planes - 1):
            upper = camera[block, plane + 1] - base_level
            here = pl.ds(pl.multiple_of(base + plane * rows, SUB), rows)
            out_ref[here, :] += lower_share * lower + upper_share * upper
            lower = upper
        counts = pl.ds(pl.multiple_of(start + CZ * rows, SUB), CZ)
        out_ref[counts, :] += ((plane_at >= at) & (plane_at < at + planes - 1)).astype(F32)
        return carry

    for i, copy in enumerate(parts):
        copy.wait()
        lax.fori_loop(i * chunk, (i + 1) * chunk, one, 0, unroll=True)


def deposit(camera, target, first, level, fraction, slabs):
    blocks, planes, rows, cols = camera.shape
    section = CZ * rows + CZ
    chunk = SUB if blocks % SUB == 0 else blocks
    return pl.pallas_call(
        functools.partial(deposit_kernel, bits=bit_count(slabs), section=section, chunk=chunk),
        in_specs=[HBM] * 5,
        out_specs=VMEM,
        out_shape=jax.ShapeDtypeStruct((slabs * section, cols), F32),
        scratch_shapes=[
            pltpu.SMEM(target.shape, jnp.int32),
            pltpu.SMEM(first.shape, jnp.int32),
            pltpu.SMEM(level.shape, jnp.int32),
            pltpu.SMEM(fraction.shape, F32),
            pltpu.VMEM(camera.shape, F32),
            pltpu.SemaphoreType.DMA((4,)),
            pltpu.SemaphoreType.DMA((blocks // chunk,)),
        ],
        compiler_params=pltpu.CompilerParams(vmem_limit_bytes=DEPOSIT_VMEM_BYTES),
        name="deposit",
    )(target, first, level, fraction, camera)


def butterfly(sums, slabs, section):
    bits = bit_count(slabs)
    own = sums
    count = slabs
    late = None
    for bit in range(bits):
        half = count // 2
        pairs = [(i, i ^ (1 << bit)) for i in range(slabs)]
        keep, send = own[: half * section], own[half * section :]
        if late is not None:
            send = send + late[1]
            keep = keep + late[0]
        if half > 1:
            cut = half // 2 * section
            onward = lax.ppermute(send[cut:], "gz", pairs)
            stays = lax.ppermute(send[:cut], "gz", pairs)
            late = (stays, onward)
            next_half = half // 2
            own = keep
        else:
            arrived = lax.ppermute(send, "gz", pairs)
            return keep, arrived
        count = half
    return own, jnp.zeros_like(own)


def join_kernel(small_ref, kept_ref, arrived_ref, message_ref, *, rows):
    cols = kept_ref.shape[1]
    total = kept_ref[...] + arrived_ref[...]
    planes = total[: CZ * rows].reshape(CZ, rows, cols)
    counts = total[CZ * rows :]
    fy, fx = small_ref[3:4], small_ref[4:5]
    row_at = lax.broadcasted_iota(jnp.int32, (rows, cols), 0)
    col_at = lax.broadcasted_iota(jnp.int32, (rows, cols), 1)
    for plane in range(CZ):
        part = planes[plane]
        follow = jnp.where(row_at == rows - 1, part, pltpu.roll(part, rows - 1, 0))
        part = (1.0 - fy) * part + fy * follow
        follow = jnp.where(col_at == cols - 1, part, pltpu.roll(part, cols - 1, 1))
        part = (1.0 - fx) * part + fx * follow
        part = jnp.maximum(part / (counts[plane : plane + 1] + 1.0), DATA_FLOOR)
        message_ref[plane * rows : (plane + 1) * rows] = part
    message_ref[CZ * rows :] = small_ref[...]


def join(small, kept, arrived, rows):
    return pl.pallas_call(
        functools.partial(join_kernel, rows=rows),
        in_specs=[VMEM] * 3,
        out_specs=VMEM,
        out_shape=jax.ShapeDtypeStruct(kept.shape, F32),
        compiler_params=pltpu.CompilerParams(vmem_limit_bytes=VMEM_BYTES),
        name="join",
    )(small, kept, arrived)


def taps_sum(values, weights):
    result = weights[0] * values[0]
    for offset in range(1, len(weights)):
        result = result + weights[offset] * values[offset]
    return result


def band_dot(values, high_part, low_part):
    cols = values.shape[1]
    top = values.astype(jnp.bfloat16)
    rest = (values - top.astype(F32)).astype(jnp.bfloat16)
    both = jnp.dot(top, jnp.concatenate([high_part, low_part], axis=1), preferred_element_type=F32)
    return both[:, :cols] + both[:, cols:] + jnp.dot(rest, high_part, preferred_element_type=F32)


def update_kernel(
    weight_ref, high_band_ref, low_band_ref, own_ref, below_ref, above_ref, low_rows_ref, high_rows_ref, *rest,
    views, margin, first
):
    if first:
        message_ref, out_ref, copied_hbm, *scratch, copied_sem = rest
        copied = pltpu.make_async_copy(message_ref.at[pl.ds(0, copied_hbm.shape[0])], copied_hbm, copied_sem)
        copied.start()
    else:
        est_ref, est_below_ref, est_above_ref, est_low_ref, est_high_ref, out_ref, *scratch = rest
    estimate, joined, first_pass, ratio, back_first = scratch
    _, planes, rows, cols = own_ref.shape
    taps = 2 * margin + 1
    wide = 2 * margin
    flag_low, flag_high = weight_ref[views * 3 * taps], weight_ref[views * 3 * taps + 1]
    low, body, high = slice(0, wide), slice(wide, wide + rows), slice(wide + rows, 2 * wide + rows)

    above_at = below_ref.shape[0]
    own_at = 2 * above_at
    for view in range(views):
        pieces = (
            (0, margin, below_ref, view * margin, view * margin),
            (margin, planes, own_ref.at[view], 0, own_at + view * planes),
            (margin + planes, margin, above_ref, view * margin, above_at + view * margin),
        )
        for to, length, source, at, edge_at in pieces:
            joined[view, to : to + length, body] = source[at : at + length]
            joined[view, to : to + length, low] = low_rows_ref[edge_at : edge_at + length] * flag_low
            joined[view, to : to + length, high] = high_rows_ref[edge_at : edge_at + length] * flag_high
    if first:
        inner = joined[0]
        for view in range(1, views):
            inner = inner + joined[view]
        estimate[margin : planes + 3 * margin] = inner / views
        at = views * margin
        for to, source, edge_at in ((0, below_ref, at), (planes + 3 * margin, above_ref, above_at + at)):
            estimate[to : to + margin, body] = source[at : at + margin]
            estimate[to : to + margin, low] = low_rows_ref[edge_at : edge_at + margin] * flag_low
            estimate[to : to + margin, high] = high_rows_ref[edge_at : edge_at + margin] * flag_high
    else:
        for index, source in enumerate((est_below_ref, est_ref, est_above_ref)):
            here = slice(index * planes, (index + 1) * planes)
            estimate[here, body] = source[...]
            estimate[here, low] = est_low_ref[here] * flag_low
            estimate[here, high] = est_high_ref[here] * flag_high

    mid_planes, mid_rows = planes + 2 * margin, rows + 2 * margin
    weights = [
        [[weight_ref[(view * 3 + dim) * taps + tap] for tap in range(taps)] for dim in range(3)] for view in range(views)
    ]

    def along_z(tile, carry):
        here = pl.ds(pl.multiple_of(tile * SUB, SUB), SUB)
        values = [estimate[plane, here, :] for plane in range(planes + 4 * margin)]
        for view in range(views):
            for plane in range(mid_planes):
                first_pass[view, plane, here, :] = taps_sum(values[plane : plane + taps], weights[view][0])
        return carry

    lax.fori_loop(0, (rows + 4 * margin) // SUB, along_z, 0)

    for view in range(views):
        values = [first_pass[view, :, tap : tap + mid_rows, :].reshape(-1, SUB, cols) for tap in range(taps)]
        blurred = band_dot(
            taps_sum(values, weights[view][1]).reshape(-1, cols), high_band_ref[view, 0], low_band_ref[view, 0]
        )
        ratio[view] = joined[view, :, margin : margin + mid_rows, :] / blurred.reshape(mid_planes, mid_rows, cols)

    def back_z(tile, carry):
        here = pl.ds(pl.multiple_of(tile * SUB, SUB), SUB)
        for view in range(views):
            values = [ratio[view, plane, here, :] for plane in range(mid_planes)]
            for plane in range(planes):
                back_first[view, plane, here, :] = taps_sum(values[plane : plane + taps], weights[view][0][::-1])
        return carry

    lax.fori_loop(0, mid_rows // SUB, back_z, 0)

    logs = None
    for view in range(views):
        values = [back_first[view, :, tap : tap + rows, :].reshape(-1, SUB, cols) for tap in range(taps)]
        correction = band_dot(
            taps_sum(values, weights[view][1][::-1]).reshape(-1, cols), high_band_ref[view, 1], low_band_ref[view, 1]
        )
        one = jnp.log(correction)
        logs = one if logs is None else logs + one
    out_ref[...] = estimate[wide : wide + planes, body] * jnp.exp(logs / views).reshape(planes, rows, cols)
    if first:
        copied.wait()


def update(weights, bands, own, below, above, low_rows, high_rows, message, later, margin):
    views, planes, rows, cols = own.shape
    first = not later
    arrays = [weights, *bands, own, below, above, low_rows, high_rows] + ([message] if first else list(later))
    mid_planes, mid_rows = planes + 2 * margin, rows + 2 * margin
    scratch = [
        (planes + 4 * margin, rows + 4 * margin),
        (views, mid_planes, rows + 4 * margin),
        (views, mid_planes, rows + 4 * margin),
        (views, mid_planes, mid_rows),
        (views, planes, mid_rows),
    ]
    out_shape = jax.ShapeDtypeStruct((planes, rows, cols), F32)
    copy_shape = jax.ShapeDtypeStruct((planes * rows, cols), F32)
    return pl.pallas_call(
        functools.partial(update_kernel, views=views, margin=margin, first=first),
        in_specs=[VMEM] * len(arrays),
        out_specs=[VMEM, HBM] if first else VMEM,
        out_shape=[out_shape, copy_shape] if first else out_shape,
        scratch_shapes=[pltpu.VMEM(shape + (cols,), F32) for shape in scratch] + [pltpu.SemaphoreType.DMA] * first,
        compiler_params=pltpu.CompilerParams(vmem_limit_bytes=VMEM_BYTES),
        name="update",
    )(*arrays)


def from_beside(axis, upward, downward):
    count = lax.axis_size(axis)
    up = [(i, i + 1) for i in range(count - 1)]
    down = [(target, source) for source, target in up]
    return lax.ppermute(upward, axis, up), lax.ppermute(downward, axis, down)


def edge_rows(pieces, width):
    count = lax.axis_size("gy")
    rows = pieces[0].shape[-2]
    if count == 2:
        at = jnp.where(lax.axis_index("gy") == 0, rows - width, 0)
        parts = [lax.dynamic_slice_in_dim(piece, at, width, axis=1) for piece in pieces]
        arrived = lax.ppermute(jnp.concatenate(parts), "gy", [(0, 1), (1, 0)])
        return arrived, arrived
    upward = jnp.concatenate([piece[:, rows - width :] for piece in pieces])
    downward = jnp.concatenate([piece[:, :width] for piece in pieces])
    return from_beside("gy", upward, downward)


def from_views(message):
    count = lax.axis_size("view")
    if count == 2:
        return jnp.stack([message, lax.ppermute(message, "view", [(0, 1), (1, 0)])])
    return lax.all_gather(message, "view")


def on_device(camera, background, destination, offsets, shift_frac, psf_taps):
    slabs = lax.axis_size("gz")
    views = lax.axis_size("view")
    _, blocks, _, rows, cols = camera.shape
    taps = psf_taps.shape[-1]
    margin = taps // 2
    section = CZ * rows + CZ
    fraction = shift_frac[0]
    sums = deposit(
        camera[0], destination.reshape(blocks), offsets.reshape(blocks), background.reshape(1), fraction, slabs
    )
    kept, arrived = butterfly(sums, slabs, section)
    small = jnp.concatenate(
        [
            jnp.pad(psf_taps[0], ((0, 0), (0, cols - taps))),
            jnp.broadcast_to(fraction[1:, None], (2, cols)),
            jnp.zeros((CZ - 5, cols), F32),
        ]
    )
    message = join(small, kept, arrived, rows)

    messages = from_views(message)
    all_joined = messages[:, : CZ * rows].reshape(views, CZ, rows, cols)
    estimate = jnp.sum(all_joined, axis=0) / views
    upward = jnp.concatenate([all_joined[:, CZ - margin :].reshape(views * margin, rows, cols), estimate[: CZ - margin]])
    downward = jnp.concatenate([all_joined[:, :margin].reshape(views * margin, rows, cols), estimate[margin:]])
    below, above = from_beside("gz", upward, downward)
    wide = 2 * margin
    low_rows, high_rows = edge_rows([below, above, all_joined.reshape(views * CZ, rows, cols)], wide)

    all_taps = messages[:, CZ * rows : CZ * rows + 3, :taps]
    kernels = all_taps / jnp.sum(all_taps, axis=-1, keepdims=True)
    places = jnp.arange(cols, dtype=jnp.int32)
    shift = places[:, None] - places[None, :] + margin
    band = sum(jnp.where(shift == tap, kernels[:, 2, tap, None, None], 0.0) for tap in range(taps))
    band = jnp.stack([band, jnp.swapaxes(band, 1, 2)], axis=1)
    high_part = lax.reduce_precision(band, 8, 7)
    bands = (high_part.astype(jnp.bfloat16), (band - high_part).astype(jnp.bfloat16))
    row_band = lax.axis_index("gy")
    flags = jnp.stack([row_band > 0, row_band < lax.axis_size("gy") - 1]).astype(F32)
    weights = jnp.broadcast_to(jnp.concatenate([kernels.reshape(-1), flags])[:, None, None], (views * 3 * taps + 2, SUB, cols))

    later = ()
    for iteration in range(ITERS):
        if iteration:
            est_below, est_above = from_beside("gz", estimate, estimate)
            later = (estimate, est_below, est_above) + edge_rows([est_below, estimate, est_above], wide)
        result = update(weights, bands, all_joined, below, above, low_rows, high_rows, message, later, margin)
        estimate = result if later else result[0]
        joined = joined if later else result[1]
    return (estimate, joined.reshape(1, CZ, rows, cols))


def solution(mesh):
    return jax.shard_map(
        on_device,
        mesh=mesh,
        in_specs=(
            P("view", ("groups", "gz"), None, "gy", None),
            P("view", "gy", ("groups", "gz")),
            P("view", "gy", ("groups", "gz"), None),
            P("view", "gy", ("groups", "gz")),
            P("view", None),
            P("view", None, None),
        ),
        out_specs=(P(("groups", "gz"), "gy", None), P("view", ("groups", "gz"), "gy", None)),
        check_vma=False,
    )
```

```python
import functools

import jax
import jax.numpy as jnp
from jax import lax
from jax.experimental import pallas as pl
from jax.experimental.pallas import tpu as pltpu
from jax.sharding import PartitionSpec as P

CZ = 8
ITERS = 2


DATA_FLOOR = 0.25
PRECISE = lax.Precision.HIGHEST
F32 = jnp.float32
SUB = 8
VMEM = pl.BlockSpec(memory_space=pltpu.VMEM)
HBM = pl.BlockSpec(memory_space=pltpu.HBM)
VMEM_BYTES = 48 * 1024 * 1024
DEPOSIT_VMEM_BYTES = 60 * 1024 * 1024
LATE_BYTES = 4 * 1024 * 1024


def bit_count(count):
    bits = count.bit_length() - 1
    assert count == 1 << bits
    return bits


def step_bits(slabs, odd):
    order = list(range(bit_count(slabs)))
    if odd and len(order) > 1:
        order[:2] = [1, 0]
    return order


def section_of(value, order):
    result = 0
    for step, bit in enumerate(order):
        result = result | (((value >> bit) & 1) << (len(order) - 1 - step))
    return result


def deposit_kernel(
    target_hbm, first_hbm, level_hbm, fraction_hbm, camera_hbm, *rest, slabs, section, chunk
):
    *out_refs, sums_ref, target, first, level, fraction, camera, small_sems, camera_sems = rest
    blocks, planes, rows, cols = camera.shape
    sources = ((target_hbm, target), (first_hbm, first), (level_hbm, level), (fraction_hbm, fraction))
    smalls = [pltpu.make_async_copy(*pair, small_sems.at[i]) for i, pair in enumerate(sources)]
    parts = []
    for i in range(blocks // chunk):
        here = pl.ds(i * chunk, chunk)
        parts.append(pltpu.make_async_copy(camera_hbm.at[here], camera.at[here], camera_sems.at[i]))
    for copy in smalls + parts:
        copy.start()
    sums_ref[...] = jnp.zeros(sums_ref.shape, F32)
    for copy in smalls:
        copy.wait()
    place = lax.axis_index("gz").astype(jnp.int32)
    odd = lax.axis_index("gy") % 2 == 1
    base_level = level[0].astype(F32)
    upper_share = fraction[0]
    lower_share = 1.0 - upper_share
    plane_at = lax.broadcasted_iota(jnp.int32, (CZ, cols), 0)

    def one(block, carry):
        away = target[block] ^ place
        slab = jnp.where(odd, section_of(away, step_bits(slabs, True)), section_of(away, step_bits(slabs, False)))
        at = first[block]
        start = pl.multiple_of(slab * section, SUB)
        base = pl.multiple_of(start + at * rows, SUB)
        lower = camera[block, 0] - base_level
        for plane in range(planes - 1):
            upper = camera[block, plane + 1] - base_level
            here = pl.ds(pl.multiple_of(base + plane * rows, SUB), rows)
            sums_ref[here, :] += lower_share * lower + upper_share * upper
            lower = upper
        counts = pl.ds(pl.multiple_of(start + CZ * rows, SUB), CZ)
        sums_ref[counts, :] += ((plane_at >= at) & (plane_at < at + planes - 1)).astype(F32)
        return carry

    for i, copy in enumerate(parts):
        copy.wait()
        lax.fori_loop(i * chunk, (i + 1) * chunk, one, 0, unroll=True)
    at = 0
    for out_ref in out_refs:
        out_ref[...] = sums_ref[at : at + out_ref.shape[0]]
        at += out_ref.shape[0]


def deposit(camera, target, first, level, fraction, slabs, shares):
    blocks, planes, rows, cols = camera.shape
    section = CZ * rows + CZ
    chunk = SUB if blocks % SUB == 0 else blocks
    return pl.pallas_call(
        functools.partial(deposit_kernel, slabs=slabs, section=section, chunk=chunk),
        in_specs=[HBM] * 5,
        out_specs=[VMEM] * len(shares),
        out_shape=[jax.ShapeDtypeStruct((share * section, cols), F32) for share in shares],
        scratch_shapes=[
            pltpu.VMEM((slabs * section, cols), F32),
            pltpu.SMEM(target.shape, jnp.int32),
            pltpu.SMEM(first.shape, jnp.int32),
            pltpu.SMEM(level.shape, jnp.int32),
            pltpu.SMEM(fraction.shape, F32),
            pltpu.VMEM(camera.shape, F32),
            pltpu.SemaphoreType.DMA((4,)),
            pltpu.SemaphoreType.DMA((blocks // chunk,)),
        ],
        compiler_params=pltpu.CompilerParams(vmem_limit_bytes=DEPOSIT_VMEM_BYTES),
        name="deposit",
    )(target, first, level, fraction, camera)


def gz_pairs(partner):
    count, bands = lax.axis_size("gz"), lax.axis_size("gy")
    pairs = []
    for place in range(count):
        for band in range(bands):
            other = partner(place, band % 2 == 1)
            if 0 <= other < count:
                pairs.append((place * bands + band, other * bands + band))
    return pairs


def first_shares(slabs):
    if slabs <= 2:
        return [1] * slabs
    return [slabs // 4] * 4


def fetch_kernel(*refs):
    sources, targets, sems = refs[: len(refs) // 2], refs[len(refs) // 2 : -1], refs[-1]
    copies = [pltpu.make_async_copy(*pair, sems.at[i]) for i, pair in enumerate(zip(sources, targets))]
    for copy in copies:
        copy.start()
    for copy in copies:
        copy.wait()


def fetch(*arrays):
    return pl.pallas_call(
        fetch_kernel,
        in_specs=[HBM] * len(arrays),
        out_specs=[VMEM] * len(arrays),
        out_shape=[jax.ShapeDtypeStruct(array.shape, array.dtype) for array in arrays],
        scratch_shapes=[pltpu.SemaphoreType.DMA((len(arrays),))],
        compiler_params=pltpu.CompilerParams(vmem_limit_bytes=VMEM_BYTES),
        name="fetch",
    )(*arrays)


def add_kernel(left_ref, right_ref, out_ref):
    out_ref[...] = left_ref[...] + right_ref[...]


def add(left, right, cost=None):
    return pl.pallas_call(
        add_kernel,
        in_specs=[VMEM] * 2,
        out_specs=VMEM,
        out_shape=jax.ShapeDtypeStruct(left.shape, F32),
        compiler_params=pltpu.CompilerParams(vmem_limit_bytes=VMEM_BYTES),
        cost_estimate=cost,
        name="add",
    )(left, right)


def butterfly(shares, slabs, section):
    if slabs == 1:
        return shares[0], jnp.zeros_like(shares[0])
    for step in range(bit_count(slabs)):
        pairs = gz_pairs(lambda place, odd: place ^ (1 << step_bits(slabs, odd)[step]))
        if len(shares) == 2:
            return shares[0], lax.ppermute(shares[1], ("gz", "gy"), pairs)
        keep, send, stays, onward = shares
        if step == 0:
            keep, send = fetch(keep, send)
        onward = lax.ppermute(onward, ("gz", "gy"), pairs)
        stays = lax.ppermute(stays, ("gz", "gy"), pairs)
        send = add(send, onward)
        keep = add(keep, stays, pl.CostEstimate(flops=0, bytes_accessed=LATE_BYTES, transcendentals=0))
        half = keep.shape[0] // 2
        shares = [keep, send] if keep.shape[0] == section else [keep[:half], keep[half:], send[:half], send[half:]]


def join_kernel(small_ref, kept_ref, arrived_ref, message_ref, *, rows):
    cols = kept_ref.shape[1]
    total = kept_ref[...] + arrived_ref[...]
    planes = total[: CZ * rows].reshape(CZ, rows, cols)
    counts = total[CZ * rows :]
    fy, fx = small_ref[3:4], small_ref[4:5]
    row_at = lax.broadcasted_iota(jnp.int32, (rows, cols), 0)
    col_at = lax.broadcasted_iota(jnp.int32, (rows, cols), 1)
    for plane in range(CZ):
        part = planes[plane]
        follow = jnp.where(row_at == rows - 1, part, pltpu.roll(part, rows - 1, 0))
        part = (1.0 - fy) * part + fy * follow
        follow = jnp.where(col_at == cols - 1, part, pltpu.roll(part, cols - 1, 1))
        part = (1.0 - fx) * part + fx * follow
        part = jnp.maximum(part / (counts[plane : plane + 1] + 1.0), DATA_FLOOR)
        message_ref[plane * rows : (plane + 1) * rows] = part
    message_ref[CZ * rows :] = small_ref[...]


def join(small, kept, arrived, rows):
    return pl.pallas_call(
        functools.partial(join_kernel, rows=rows),
        in_specs=[VMEM] * 3,
        out_specs=VMEM,
        out_shape=jax.ShapeDtypeStruct(kept.shape, F32),
        compiler_params=pltpu.CompilerParams(vmem_limit_bytes=VMEM_BYTES),
        name="join",
    )(small, kept, arrived)


def taps_sum(values, weights):
    result = weights[0] * values[0]
    for offset in range(1, len(weights)):
        result = result + weights[offset] * values[offset]
    return result


def band_dot(values, high_part, low_part):
    cols = values.shape[1]
    top = values.astype(jnp.bfloat16)
    rest = (values - top.astype(F32)).astype(jnp.bfloat16)
    both = jnp.dot(top, jnp.concatenate([high_part, low_part], axis=1), preferred_element_type=F32)
    return both[:, :cols] + both[:, cols:] + jnp.dot(rest, high_part, preferred_element_type=F32)


def update_kernel(
    weight_ref, high_band_ref, low_band_ref, own_ref, below_ref, above_ref, low_rows_ref, high_rows_ref, *rest,
    views, margin, first
):
    if first:
        message_ref, out_ref, copied_hbm, *scratch, copied_sem = rest
        copied = pltpu.make_async_copy(message_ref.at[pl.ds(0, copied_hbm.shape[0])], copied_hbm, copied_sem)
        copied.start()
    else:
        est_ref, est_below_ref, est_above_ref, est_low_ref, est_high_ref, out_ref, *scratch = rest
    estimate, joined, first_pass, ratio, back_first = scratch
    _, planes, rows, cols = own_ref.shape
    taps = 2 * margin + 1
    wide = 2 * margin
    flag_low, flag_high = weight_ref[views * 3 * taps], weight_ref[views * 3 * taps + 1]
    low, body, high = slice(0, wide), slice(wide, wide + rows), slice(wide + rows, 2 * wide + rows)

    above_at = below_ref.shape[0]
    own_at = 2 * above_at
    for view in range(views):
        pieces = (
            (0, margin, below_ref, view * margin, view * margin),
            (margin, planes, own_ref.at[view], 0, own_at + view * planes),
            (margin + planes, margin, above_ref, view * margin, above_at + view * margin),
        )
        for to, length, source, at, edge_at in pieces:
            joined[view, to : to + length, body] = source[at : at + length]
            joined[view, to : to + length, low] = low_rows_ref[edge_at : edge_at + length] * flag_low
            joined[view, to : to + length, high] = high_rows_ref[edge_at : edge_at + length] * flag_high
    if first:
        inner = joined[0]
        for view in range(1, views):
            inner = inner + joined[view]
        estimate[margin : planes + 3 * margin] = inner / views
        at = views * margin
        for to, source, edge_at in ((0, below_ref, at), (planes + 3 * margin, above_ref, above_at + at)):
            estimate[to : to + margin, body] = source[at : at + margin]
            estimate[to : to + margin, low] = low_rows_ref[edge_at : edge_at + margin] * flag_low
            estimate[to : to + margin, high] = high_rows_ref[edge_at : edge_at + margin] * flag_high
    else:
        for index, source in enumerate((est_below_ref, est_ref, est_above_ref)):
            here = slice(index * planes, (index + 1) * planes)
            estimate[here, body] = source[...]
            estimate[here, low] = est_low_ref[here] * flag_low
            estimate[here, high] = est_high_ref[here] * flag_high

    mid_planes, mid_rows = planes + 2 * margin, rows + 2 * margin
    weights = [
        [[weight_ref[(view * 3 + dim) * taps + tap] for tap in range(taps)] for dim in range(3)] for view in range(views)
    ]

    def along_z(tile, carry):
        here = pl.ds(pl.multiple_of(tile * SUB, SUB), SUB)
        values = [estimate[plane, here, :] for plane in range(planes + 4 * margin)]
        for view in range(views):
            for plane in range(mid_planes):
                first_pass[view, plane, here, :] = taps_sum(values[plane : plane + taps], weights[view][0])
        return carry

    lax.fori_loop(0, (rows + 4 * margin) // SUB, along_z, 0)

    for view in range(views):
        values = [first_pass[view, :, tap : tap + mid_rows, :].reshape(-1, SUB, cols) for tap in range(taps)]
        blurred = band_dot(
            taps_sum(values, weights[view][1]).reshape(-1, cols), high_band_ref[view, 0], low_band_ref[view, 0]
        )
        ratio[view] = joined[view, :, margin : margin + mid_rows, :] / blurred.reshape(mid_planes, mid_rows, cols)

    def back_z(tile, carry):
        here = pl.ds(pl.multiple_of(tile * SUB, SUB), SUB)
        for view in range(views):
            values = [ratio[view, plane, here, :] for plane in range(mid_planes)]
            for plane in range(planes):
                back_first[view, plane, here, :] = taps_sum(values[plane : plane + taps], weights[view][0][::-1])
        return carry

    lax.fori_loop(0, mid_rows // SUB, back_z, 0)

    logs = None
    for view in range(views):
        values = [back_first[view, :, tap : tap + rows, :].reshape(-1, SUB, cols) for tap in range(taps)]
        correction = band_dot(
            taps_sum(values, weights[view][1][::-1]).reshape(-1, cols), high_band_ref[view, 1], low_band_ref[view, 1]
        )
        one = jnp.log(correction)
        logs = one if logs is None else logs + one
    out_ref[...] = estimate[wide : wide + planes, body] * jnp.exp(logs / views).reshape(planes, rows, cols)
    if first:
        copied.wait()


def update(weights, bands, own, below, above, low_rows, high_rows, message, later, margin):
    views, planes, rows, cols = own.shape
    first = not later
    arrays = [weights, *bands, own, below, above, low_rows, high_rows] + ([message] if first else list(later))
    mid_planes, mid_rows = planes + 2 * margin, rows + 2 * margin
    scratch = [
        (planes + 4 * margin, rows + 4 * margin),
        (views, mid_planes, rows + 4 * margin),
        (views, mid_planes, rows + 4 * margin),
        (views, mid_planes, mid_rows),
        (views, planes, mid_rows),
    ]
    out_shape = jax.ShapeDtypeStruct((planes, rows, cols), F32)
    copy_shape = jax.ShapeDtypeStruct((planes * rows, cols), F32)
    return pl.pallas_call(
        functools.partial(update_kernel, views=views, margin=margin, first=first),
        in_specs=[VMEM] * len(arrays),
        out_specs=[VMEM, HBM] if first else VMEM,
        out_shape=[out_shape, copy_shape] if first else out_shape,
        scratch_shapes=[pltpu.VMEM(shape + (cols,), F32) for shape in scratch] + [pltpu.SemaphoreType.DMA] * first,
        compiler_params=pltpu.CompilerParams(vmem_limit_bytes=VMEM_BYTES),
        name="update",
    )(*arrays)


def from_beside(axis, upward, downward):
    count = lax.axis_size(axis)
    up = [(i, i + 1) for i in range(count - 1)]
    down = [(target, source) for source, target in up]
    return lax.ppermute(upward, axis, up), lax.ppermute(downward, axis, down)


def from_slabs_beside(upward, downward):
    odd = lax.axis_index("gy") % 2 == 1
    if upward is downward:
        sends = (upward, downward)
    else:
        sends = (jnp.where(odd, downward, upward), jnp.where(odd, upward, downward))
    first = lax.ppermute(sends[0], ("gz", "gy"), gz_pairs(lambda place, odd: place - 1 if odd else place + 1))
    second = lax.ppermute(sends[1], ("gz", "gy"), gz_pairs(lambda place, odd: place + 1 if odd else place - 1))
    return jnp.where(odd, second, first), jnp.where(odd, first, second)


def edge_rows(pieces, width):
    count = lax.axis_size("gy")
    rows = pieces[0].shape[-2]
    if count == 2:
        at = jnp.where(lax.axis_index("gy") == 0, rows - width, 0)
        parts = [lax.dynamic_slice_in_dim(piece, at, width, axis=1) for piece in pieces]
        arrived = lax.ppermute(jnp.concatenate(parts), "gy", [(0, 1), (1, 0)])
        return arrived, arrived
    upward = jnp.concatenate([piece[:, rows - width :] for piece in pieces])
    downward = jnp.concatenate([piece[:, :width] for piece in pieces])
    return from_beside("gy", upward, downward)


def from_views(message):
    count = lax.axis_size("view")
    if count == 2:
        return jnp.stack([message, lax.ppermute(message, "view", [(0, 1), (1, 0)])])
    return lax.all_gather(message, "view")


def on_device(camera, background, destination, offsets, shift_frac, psf_taps):
    slabs = lax.axis_size("gz")
    views = lax.axis_size("view")
    _, blocks, _, rows, cols = camera.shape
    taps = psf_taps.shape[-1]
    margin = taps // 2
    section = CZ * rows + CZ
    fraction = shift_frac[0]
    shares = deposit(
        camera[0], destination.reshape(blocks), offsets.reshape(blocks), background.reshape(1), fraction, slabs,
        first_shares(slabs),
    )
    kept, arrived = butterfly(shares, slabs, section)
    small = jnp.concatenate(
        [
            jnp.pad(psf_taps[0], ((0, 0), (0, cols - taps))),
            jnp.broadcast_to(fraction[1:, None], (2, cols)),
            jnp.zeros((CZ - 5, cols), F32),
        ]
    )
    message = join(small, kept, arrived, rows)

    messages = from_views(message)
    all_joined = messages[:, : CZ * rows].reshape(views, CZ, rows, cols)
    estimate = jnp.sum(all_joined, axis=0) / views
    upward = jnp.concatenate([all_joined[:, CZ - margin :].reshape(views * margin, rows, cols), estimate[: CZ - margin]])
    downward = jnp.concatenate([all_joined[:, :margin].reshape(views * margin, rows, cols), estimate[margin:]])
    below, above = from_slabs_beside(upward, downward)
    wide = 2 * margin
    low_rows, high_rows = edge_rows([below, above, all_joined.reshape(views * CZ, rows, cols)], wide)

    all_taps = messages[:, CZ * rows : CZ * rows + 3, :taps]
    kernels = all_taps / jnp.sum(all_taps, axis=-1, keepdims=True)
    places = jnp.arange(cols, dtype=jnp.int32)
    shift = places[:, None] - places[None, :] + margin
    band = sum(jnp.where(shift == tap, kernels[:, 2, tap, None, None], 0.0) for tap in range(taps))
    band = jnp.stack([band, jnp.swapaxes(band, 1, 2)], axis=1)
    high_part = lax.reduce_precision(band, 8, 7)
    bands = (high_part.astype(jnp.bfloat16), (band - high_part).astype(jnp.bfloat16))
    row_band = lax.axis_index("gy")
    flags = jnp.stack([row_band > 0, row_band < lax.axis_size("gy") - 1]).astype(F32)
    weights = jnp.broadcast_to(jnp.concatenate([kernels.reshape(-1), flags])[:, None, None], (views * 3 * taps + 2, SUB, cols))

    later = ()
    for iteration in range(ITERS):
        if iteration:
            est_below, est_above = from_slabs_beside(estimate, estimate)
            later = (estimate, est_below, est_above) + edge_rows([est_below, estimate, est_above], wide)
        result = update(weights, bands, all_joined, below, above, low_rows, high_rows, message, later, margin)
        estimate = result if later else result[0]
        joined = joined if later else result[1]
    return (estimate, joined.reshape(1, CZ, rows, cols))


def solution(mesh):
    return jax.shard_map(
        on_device,
        mesh=mesh,
        in_specs=(
            P("view", ("groups", "gz"), None, "gy", None),
            P("view", "gy", ("groups", "gz")),
            P("view", "gy", ("groups", "gz"), None),
            P("view", "gy", ("groups", "gz")),
            P("view", None),
            P("view", None, None),
        ),
        out_specs=(P(("groups", "gz"), "gy", None), P("view", ("groups", "gz"), "gy", None)),
        check_vma=False,
    )
```

```python
import functools

import jax
import jax.numpy as jnp
from jax import lax
from jax.experimental import pallas as pl
from jax.experimental.pallas import tpu as pltpu
from jax.sharding import PartitionSpec as P

CZ = 8
HALF = CZ // 2
ITERS = 2


DATA_FLOOR = 0.25
PRECISE = lax.Precision.HIGHEST
F32 = jnp.float32
SUB = 8
VMEM = pl.BlockSpec(memory_space=pltpu.VMEM)
HBM = pl.BlockSpec(memory_space=pltpu.HBM)
VMEM_BYTES = 48 * 1024 * 1024
DEPOSIT_VMEM_BYTES = 60 * 1024 * 1024


def bit_count(count):
    bits = count.bit_length() - 1
    assert count == 1 << bits
    return bits


def step_bits(slabs, odd):
    order = list(range(bit_count(slabs)))
    if odd and len(order) > 1:
        order[:2] = [1, 0]
    return order


def section_of(value, order):
    result = 0
    for step, bit in enumerate(order):
        result = result | (((value >> bit) & 1) << (len(order) - 1 - step))
    return result


def deposit_kernel(
    target_hbm, first_hbm, level_hbm, fraction_hbm, camera_hbm, *rest, slabs, section, chunk
):
    *out_refs, sums_ref, target, first, level, fraction, camera, small_sems, camera_sems = rest
    blocks, planes, rows, cols = camera.shape
    sources = ((target_hbm, target), (first_hbm, first), (level_hbm, level), (fraction_hbm, fraction))
    smalls = [pltpu.make_async_copy(*pair, small_sems.at[i]) for i, pair in enumerate(sources)]
    parts = []
    for i in range(blocks // chunk):
        here = pl.ds(i * chunk, chunk)
        parts.append(pltpu.make_async_copy(camera_hbm.at[here], camera.at[here], camera_sems.at[i]))
    for copy in smalls + parts:
        copy.start()
    sums_ref[...] = jnp.zeros(sums_ref.shape, F32)
    for copy in smalls:
        copy.wait()
    place = lax.axis_index("gz").astype(jnp.int32)
    odd = lax.axis_index("gy") % 2 == 1
    base_level = level[0].astype(F32)
    upper_share = fraction[0]
    lower_share = 1.0 - upper_share
    count_at = lax.broadcasted_iota(jnp.int32, (SUB, cols), 0)

    def one(block, carry):
        away = target[block] ^ place
        slab = jnp.where(odd, section_of(away, step_bits(slabs, True)), section_of(away, step_bits(slabs, False)))
        at = first[block]
        lower = camera[block, 0] - base_level
        for plane in range(planes - 1):
            upper = camera[block, plane + 1] - base_level
            lands = at + plane
            half = lands // HALF
            start = (half * slabs + slab) * section
            here = pl.ds(pl.multiple_of(start + (lands - half * HALF) * rows, SUB), rows)
            sums_ref[here, :] += lower_share * lower + upper_share * upper
            counts = pl.ds(pl.multiple_of(start + HALF * rows, SUB), SUB)
            sums_ref[counts, :] += (count_at == lands - half * HALF).astype(F32)
            lower = upper
        return carry

    for i, copy in enumerate(parts):
        copy.wait()
        lax.fori_loop(i * chunk, (i + 1) * chunk, one, 0, unroll=True)
    at = 0
    for out_ref in out_refs:
        out_ref[...] = sums_ref[at : at + out_ref.shape[0]]
        at += out_ref.shape[0]


def deposit(camera, target, first, level, fraction, slabs, shares):
    blocks, planes, rows, cols = camera.shape
    section = HALF * rows + SUB
    chunk = SUB if blocks % SUB == 0 else blocks
    return pl.pallas_call(
        functools.partial(deposit_kernel, slabs=slabs, section=section, chunk=chunk),
        in_specs=[HBM] * 5,
        out_specs=[VMEM] * (2 * len(shares)),
        out_shape=[jax.ShapeDtypeStruct((share * section, cols), F32) for share in shares * 2],
        scratch_shapes=[
            pltpu.VMEM((2 * slabs * section, cols), F32),
            pltpu.SMEM(target.shape, jnp.int32),
            pltpu.SMEM(first.shape, jnp.int32),
            pltpu.SMEM(level.shape, jnp.int32),
            pltpu.SMEM(fraction.shape, F32),
            pltpu.VMEM(camera.shape, F32),
            pltpu.SemaphoreType.DMA((4,)),
            pltpu.SemaphoreType.DMA((blocks // chunk,)),
        ],
        compiler_params=pltpu.CompilerParams(vmem_limit_bytes=DEPOSIT_VMEM_BYTES),
        name="deposit",
    )(target, first, level, fraction, camera)


def gz_pairs(partner):
    count, bands = lax.axis_size("gz"), lax.axis_size("gy")
    pairs = []
    for place in range(count):
        for band in range(bands):
            other = partner(place, band % 2 == 1)
            if 0 <= other < count:
                pairs.append((place * bands + band, other * bands + band))
    return pairs


def first_shares(slabs):
    if slabs <= 2:
        return [1] * slabs
    return [slabs // 4] * 4


def fetch_kernel(*refs):
    sources, targets, sems = refs[: len(refs) // 2], refs[len(refs) // 2 : -1], refs[-1]
    copies = [pltpu.make_async_copy(*pair, sems.at[i]) for i, pair in enumerate(zip(sources, targets))]
    for copy in copies:
        copy.start()
    for copy in copies:
        copy.wait()


def fetch(*arrays):
    return pl.pallas_call(
        fetch_kernel,
        in_specs=[HBM] * len(arrays),
        out_specs=[VMEM] * len(arrays),
        out_shape=[jax.ShapeDtypeStruct(array.shape, array.dtype) for array in arrays],
        scratch_shapes=[pltpu.SemaphoreType.DMA((len(arrays),))],
        compiler_params=pltpu.CompilerParams(vmem_limit_bytes=VMEM_BYTES),
        name="fetch",
    )(*arrays)


def add_kernel(left_ref, right_ref, out_ref):
    out_ref[...] = left_ref[...] + right_ref[...]


def add(left, right):
    return pl.pallas_call(
        add_kernel,
        in_specs=[VMEM] * 2,
        out_specs=VMEM,
        out_shape=jax.ShapeDtypeStruct(left.shape, F32),
        compiler_params=pltpu.CompilerParams(vmem_limit_bytes=VMEM_BYTES),
        name="add",
    )(left, right)


def butterfly(halves, slabs, section):
    if slabs == 1:
        return [(shares[0], jnp.zeros_like(shares[0])) for shares in halves]
    for step in range(bit_count(slabs)):
        pairs = gz_pairs(lambda place, odd: place ^ (1 << step_bits(slabs, odd)[step]))

        def exchange(array):
            return lax.ppermute(array, ("gz", "gy"), pairs)

        if len(halves[0]) == 2:
            return [(shares[0], exchange(shares[1])) for shares in halves]
        if step == 0:
            fetched = fetch(*(shares[1] for shares in halves))
            halves = [[shares[0], array, *shares[2:]] for shares, array in zip(halves, fetched)]
        onward = [exchange(shares[3]) for shares in halves]
        stays = [exchange(shares[2]) for shares in halves]
        sends = [add(shares[1], array) for shares, array in zip(halves, onward)]
        keeps = [add(shares[0], array) for shares, array in zip(halves, stays)]
        half = keeps[0].shape[0] // 2
        if keeps[0].shape[0] == section:
            halves = [list(pair) for pair in zip(keeps, sends)]
        else:
            halves = [[keep[:half], keep[half:], send[:half], send[half:]] for keep, send in zip(keeps, sends)]


def join_kernel(small_ref, kept_ref, arrived_ref, message_ref, *, rows):
    cols = kept_ref.shape[1]
    total = kept_ref[...] + arrived_ref[...]
    planes = total[: HALF * rows].reshape(HALF, rows, cols)
    counts = total[HALF * rows :]
    fy, fx = small_ref[3:4], small_ref[4:5]
    row_at = lax.broadcasted_iota(jnp.int32, (rows, cols), 0)
    col_at = lax.broadcasted_iota(jnp.int32, (rows, cols), 1)
    for plane in range(HALF):
        part = planes[plane]
        follow = jnp.where(row_at == rows - 1, part, pltpu.roll(part, rows - 1, 0))
        part = (1.0 - fy) * part + fy * follow
        follow = jnp.where(col_at == cols - 1, part, pltpu.roll(part, cols - 1, 1))
        part = (1.0 - fx) * part + fx * follow
        part = jnp.maximum(part / (counts[plane : plane + 1] + 1.0), DATA_FLOOR)
        message_ref[plane * rows : (plane + 1) * rows] = part
    message_ref[HALF * rows :] = small_ref[...]


def join(small, kept, arrived, rows):
    return pl.pallas_call(
        functools.partial(join_kernel, rows=rows),
        in_specs=[VMEM] * 3,
        out_specs=VMEM,
        out_shape=jax.ShapeDtypeStruct(kept.shape, F32),
        compiler_params=pltpu.CompilerParams(vmem_limit_bytes=VMEM_BYTES),
        name="join",
    )(small, kept, arrived)


def taps_sum(values, weights):
    result = weights[0] * values[0]
    for offset in range(1, len(weights)):
        result = result + weights[offset] * values[offset]
    return result


def parts_of(values):
    top = values.astype(jnp.bfloat16)
    return top, (values - top.astype(F32)).astype(jnp.bfloat16)


def columns_blurred(values, bands):
    cols = values.shape[1]
    both = jnp.dot(jnp.concatenate(parts_of(values), axis=1), bands, preferred_element_type=F32)
    return both[:, :cols] + both[:, cols:]


def rows_blurred(planes, bands):
    results = []
    for at in range(0, len(planes), 2):
        stacks = []
        for plane in planes[at : at + 2]:
            top, rest = parts_of(plane)
            stacks.append(jnp.concatenate([top, rest, top], axis=0))
        both = jnp.dot(bands, jnp.concatenate(stacks, axis=1), preferred_element_type=F32)
        cols = planes[at].shape[1]
        results += [both[:, index * cols : (index + 1) * cols] for index in range(len(stacks))]
    return results


def update_kernel(
    weight_ref, row_band_ref, col_band_ref, below_ref, above_ref, low_rows_ref, high_rows_ref, *rest,
    views, margin, first
):
    halves, rest = rest[: 2 * views], rest[2 * views :]
    if first:
        *own_refs, out_ref, copied_hbm, estimate, joined, first_pass, ratio, back_first, sems = rest
    else:
        est_ref, est_below_ref, est_above_ref, est_low_ref, est_high_ref, out_ref, *scratch = rest
        estimate, joined, first_pass, ratio, back_first = scratch
    planes, rows, cols = out_ref.shape
    if first:
        length = HALF * rows
        copies = [
            pltpu.make_async_copy(ref.at[pl.ds(0, length)], copied_hbm.at[pl.ds(i * length, length)], sems.at[i])
            for i, ref in enumerate(own_refs)
        ]
        for copy in copies:
            copy.start()
    taps = 2 * margin + 1
    wide = 2 * margin
    flag_low, flag_high = weight_ref[views * taps], weight_ref[views * taps + 1]
    low, body, high = slice(0, wide), slice(wide, wide + rows), slice(wide + rows, 2 * wide + rows)

    above_at = below_ref.shape[0]
    own_at = 2 * above_at
    for view in range(views):
        here = slice(view * margin, (view + 1) * margin)
        pieces = [(0, margin, below_ref[here], view * margin)]
        for half in range(2):
            own = halves[2 * view + half][: HALF * rows].reshape(HALF, rows, cols)
            pieces.append((margin + half * HALF, HALF, own, own_at + (2 * view + half) * HALF))
        pieces.append((margin + planes, margin, above_ref[here], above_at + view * margin))
        for to, length, source, edge_at in pieces:
            joined[view, to : to + length, body] = source
            joined[view, to : to + length, low] = low_rows_ref[edge_at : edge_at + length] * flag_low
            joined[view, to : to + length, high] = high_rows_ref[edge_at : edge_at + length] * flag_high
    if first:
        inner = joined[0]
        for view in range(1, views):
            inner = inner + joined[view]
        estimate[margin : planes + 3 * margin] = inner / views
        at = views * margin
        for to, source, edge_at in ((0, below_ref, at), (planes + 3 * margin, above_ref, above_at + at)):
            estimate[to : to + margin, body] = source[at : at + margin]
            estimate[to : to + margin, low] = low_rows_ref[edge_at : edge_at + margin] * flag_low
            estimate[to : to + margin, high] = high_rows_ref[edge_at : edge_at + margin] * flag_high
    else:
        for index, source in enumerate((est_below_ref, est_ref, est_above_ref)):
            here = slice(index * planes, (index + 1) * planes)
            estimate[here, body] = source[...]
            estimate[here, low] = est_low_ref[here] * flag_low
            estimate[here, high] = est_high_ref[here] * flag_high

    mid_planes, mid_rows = planes + 2 * margin, rows + 2 * margin
    weights = [[weight_ref[view * taps + tap] for tap in range(taps)] for view in range(views)]

    def along_z(tile, carry):
        here = pl.ds(pl.multiple_of(tile * SUB, SUB), SUB)
        values = [estimate[plane, here, :] for plane in range(planes + 4 * margin)]
        for view in range(views):
            for plane in range(mid_planes):
                first_pass[view, plane, here, :] = taps_sum(values[plane : plane + taps], weights[view])
        return carry

    lax.fori_loop(0, (rows + 4 * margin) // SUB, along_z, 0, unroll=2)

    for view in range(views):
        blurred = rows_blurred([first_pass[view, plane] for plane in range(mid_planes)], row_band_ref[view, 0])
        blurred = columns_blurred(
            jnp.concatenate([plane[:mid_rows] for plane in blurred], axis=0), col_band_ref[view, 0]
        )
        ratio[view] = joined[view, :, margin : margin + mid_rows, :] / blurred.reshape(mid_planes, mid_rows, cols)

    def back_z(tile, carry):
        here = pl.ds(pl.multiple_of(tile * SUB, SUB), SUB)
        for view in range(views):
            values = [ratio[view, plane, here, :] for plane in range(mid_planes)]
            for plane in range(planes):
                back_first[view, plane, here, :] = taps_sum(values[plane : plane + taps], weights[view][::-1])
        return carry

    lax.fori_loop(0, mid_rows // SUB, back_z, 0, unroll=True)

    logs = None
    for view in range(views):
        back_first[view, :, mid_rows:, :] = jnp.zeros((planes, 2 * margin, cols), F32)
        blurred = rows_blurred([back_first[view, plane] for plane in range(planes)], row_band_ref[view, 1][:rows])
        correction = columns_blurred(jnp.concatenate(blurred, axis=0), col_band_ref[view, 1])
        one = jnp.log(correction)
        logs = one if logs is None else logs + one
    out_ref[...] = estimate[wide : wide + planes, body] * jnp.exp(logs / views).reshape(planes, rows, cols)
    if first:
        for copy in copies:
            copy.wait()


def update(weights, bands, halves, below, above, low_rows, high_rows, own, later, margin):
    first = not later
    arrays = [weights, *bands, below, above, low_rows, high_rows, *halves] + list(own if first else later)
    views = len(halves) // 2
    _, rows, cols = below.shape
    planes = CZ
    mid_planes, mid_rows = planes + 2 * margin, rows + 2 * margin
    scratch = [
        (planes + 4 * margin, rows + 4 * margin),
        (views, mid_planes, rows + 4 * margin),
        (views, mid_planes, rows + 4 * margin),
        (views, mid_planes, mid_rows),
        (views, planes, rows + 4 * margin),
    ]
    out_shape = jax.ShapeDtypeStruct((planes, rows, cols), F32)
    copy_shape = jax.ShapeDtypeStruct((planes * rows, cols), F32)
    return pl.pallas_call(
        functools.partial(update_kernel, views=views, margin=margin, first=first),
        in_specs=[VMEM] * len(arrays),
        out_specs=[VMEM, HBM] if first else VMEM,
        out_shape=[out_shape, copy_shape] if first else out_shape,
        scratch_shapes=[pltpu.VMEM(shape + (cols,), F32) for shape in scratch] + [pltpu.SemaphoreType.DMA((2,))] * first,
        compiler_params=pltpu.CompilerParams(vmem_limit_bytes=VMEM_BYTES),
        name="update",
    )(*arrays)


def from_beside(axis, upward, downward):
    count = lax.axis_size(axis)
    up = [(i, i + 1) for i in range(count - 1)]
    down = [(target, source) for source, target in up]
    return lax.ppermute(upward, axis, up), lax.ppermute(downward, axis, down)


def from_slabs_beside(upward, downward):
    odd = lax.axis_index("gy") % 2 == 1
    if upward is downward:
        sends = (upward, downward)
    else:
        sends = (jnp.where(odd, downward, upward), jnp.where(odd, upward, downward))
    first = lax.ppermute(sends[0], ("gz", "gy"), gz_pairs(lambda place, odd: place - 1 if odd else place + 1))
    second = lax.ppermute(sends[1], ("gz", "gy"), gz_pairs(lambda place, odd: place + 1 if odd else place - 1))
    return jnp.where(odd, second, first), jnp.where(odd, first, second)


def edge_rows(pieces, width):
    count = lax.axis_size("gy")
    rows = pieces[0].shape[-2]
    if count == 2:
        at = jnp.where(lax.axis_index("gy") == 0, rows - width, 0)
        parts = [lax.dynamic_slice_in_dim(piece, at, width, axis=1) for piece in pieces]
        arrived = lax.ppermute(jnp.concatenate(parts), "gy", [(0, 1), (1, 0)])
        return arrived, arrived
    upward = jnp.concatenate([piece[:, rows - width :] for piece in pieces])
    downward = jnp.concatenate([piece[:, :width] for piece in pieces])
    return from_beside("gy", upward, downward)


def band_matrix(kernels, length, margin):
    places = jnp.arange(length, dtype=jnp.int32)
    shift = places[None, :] - places[:, None] + margin
    taps = kernels.shape[-1]
    return sum(jnp.where(shift == tap, kernels[:, tap, None, None], 0.0) for tap in range(taps))


def from_views(message):
    count = lax.axis_size("view")
    if count == 2:
        return [message, lax.ppermute(message, "view", [(0, 1), (1, 0)])]
    gathered = lax.all_gather(message, "view")
    return [gathered[view] for view in range(count)]


def on_device(camera, background, destination, offsets, shift_frac, psf_taps):
    slabs = lax.axis_size("gz")
    views = lax.axis_size("view")
    _, blocks, _, rows, cols = camera.shape
    taps = psf_taps.shape[-1]
    margin = taps // 2
    assert margin == HALF
    section = HALF * rows + SUB
    fraction = shift_frac[0]
    shares = deposit(
        camera[0], destination.reshape(blocks), offsets.reshape(blocks), background.reshape(1), fraction, slabs,
        first_shares(slabs),
    )
    small = jnp.concatenate(
        [
            jnp.pad(psf_taps[0], ((0, 0), (0, cols - taps))),
            jnp.broadcast_to(fraction[1:, None], (2, cols)),
            jnp.zeros((SUB - 5, cols), F32),
        ]
    )
    per = len(shares) // 2
    own, messages = [], []
    for kept, arrived in butterfly([shares[:per], shares[per:]], slabs, section):
        own.append(join(small, kept, arrived, rows))
        messages.append(from_views(own[-1]))
    halves = [messages[half][view] for view in range(views) for half in range(2)]
    low_half, high_half = (
        [message[: HALF * rows].reshape(HALF, rows, cols) for message in messages[half]] for half in range(2)
    )
    upward = jnp.concatenate(high_half + [sum(low_half) / views])
    downward = jnp.concatenate(low_half + [sum(high_half) / views])
    below, above = from_slabs_beside(upward, downward)
    wide = 2 * margin
    pieces = [part for view in range(views) for part in (low_half[view], high_half[view])]
    low_rows, high_rows = edge_rows([below, above] + pieces, wide)

    all_taps = jnp.stack([message[HALF * rows : HALF * rows + 3, :taps] for message in messages[0]])
    kernels = all_taps / jnp.sum(all_taps, axis=-1, keepdims=True)
    row_bands = jnp.stack([band_matrix(kernels[:, 1, ::order], rows + 4 * margin, 0) for order in (1, -1)], axis=1)
    high_part = lax.reduce_precision(row_bands, 8, 7)
    row_bands = jnp.concatenate([high_part, high_part, row_bands - high_part], axis=-1).astype(jnp.bfloat16)
    col_bands = jnp.stack([band_matrix(kernels[:, 2, ::order], cols, margin) for order in (1, -1)], axis=1)
    col_bands = jnp.swapaxes(col_bands, -1, -2)
    high_part = lax.reduce_precision(col_bands, 8, 7)
    col_bands = jnp.concatenate([high_part, col_bands - high_part], axis=-1).astype(jnp.bfloat16)
    bands = (row_bands, jnp.concatenate([col_bands, col_bands], axis=-2))
    row_band = lax.axis_index("gy")
    flags = jnp.stack([row_band > 0, row_band < lax.axis_size("gy") - 1]).astype(F32)
    weights = jnp.concatenate([kernels[:, 0].reshape(-1), flags])
    weights = jnp.broadcast_to(weights[:, None, None], (views * taps + 2, SUB, cols))

    later = ()
    for iteration in range(ITERS):
        if iteration:
            est_below, est_above = from_slabs_beside(estimate, estimate)
            later = (estimate, est_below, est_above) + edge_rows([est_below, estimate, est_above], wide)
        result = update(weights, bands, halves, below, above, low_rows, high_rows, own, later, margin)
        estimate = result if later else result[0]
        joined = joined if later else result[1]
    return (estimate, joined.reshape(1, CZ, rows, cols))


def solution(mesh):
    return jax.shard_map(
        on_device,
        mesh=mesh,
        in_specs=(
            P("view", ("groups", "gz"), None, "gy", None),
            P("view", "gy", ("groups", "gz")),
            P("view", "gy", ("groups", "gz"), None),
            P("view", "gy", ("groups", "gz")),
            P("view", None),
            P("view", None, None),
        ),
        out_specs=(P(("groups", "gz"), "gy", None), P("view", ("groups", "gz"), "gy", None)),
        check_vma=False,
    )
```

```python
import functools

import jax
import jax.numpy as jnp
from jax import lax
from jax.experimental import pallas as pl
from jax.experimental.pallas import tpu as pltpu
from jax.sharding import PartitionSpec as P

CZ = 8
HALF = CZ // 2
ITERS = 2


DATA_FLOOR = 0.25
PRECISE = lax.Precision.HIGHEST
F32 = jnp.float32
SUB = 8
VMEM = pl.BlockSpec(memory_space=pltpu.VMEM)
HBM = pl.BlockSpec(memory_space=pltpu.HBM)
VMEM_BYTES = 48 * 1024 * 1024
DEPOSIT_VMEM_BYTES = 60 * 1024 * 1024


def bit_count(count):
    bits = count.bit_length() - 1
    assert count == 1 << bits
    return bits


def step_bits(slabs, odd):
    order = list(range(bit_count(slabs)))
    if odd and len(order) > 1:
        order[:2] = [1, 0]
    return order


def section_of(value, order):
    result = 0
    for step, bit in enumerate(order):
        result = result | (((value >> bit) & 1) << (len(order) - 1 - step))
    return result


def deposit_kernel(
    target_hbm, first_hbm, level_hbm, fraction_hbm, camera_hbm, *rest, slabs, section, chunk
):
    *out_refs, sums_ref, target, first, level, fraction, camera, small_sems, camera_sems = rest
    blocks, planes, rows, cols = camera.shape
    sources = ((target_hbm, target), (first_hbm, first), (level_hbm, level), (fraction_hbm, fraction))
    smalls = [pltpu.make_async_copy(*pair, small_sems.at[i]) for i, pair in enumerate(sources)]
    parts = []
    for i in range(blocks // chunk):
        here = pl.ds(i * chunk, chunk)
        parts.append(pltpu.make_async_copy(camera_hbm.at[here], camera.at[here], camera_sems.at[i]))
    for copy in smalls + parts:
        copy.start()
    sums_ref[...] = jnp.zeros(sums_ref.shape, F32)
    for copy in smalls:
        copy.wait()
    quarter = slabs // 4

    def section_row(half, slab):
        if not quarter:
            return (half * slabs + slab) * section
        ahead = jnp.where(slab < 3 * quarter, half * 3 * quarter, 3 * quarter + half * quarter)
        return (ahead + slab) * section

    place = lax.axis_index("gz").astype(jnp.int32)
    odd = lax.axis_index("gy") % 2 == 1
    base_level = level[0].astype(F32)
    upper_share = fraction[0]
    lower_share = 1.0 - upper_share
    count_at = lax.broadcasted_iota(jnp.int32, (SUB, cols), 0)

    def one(block, carry):
        away = target[block] ^ place
        slab = jnp.where(odd, section_of(away, step_bits(slabs, True)), section_of(away, step_bits(slabs, False)))
        at = first[block]
        lower = camera[block, 0] - base_level
        for plane in range(planes - 1):
            upper = camera[block, plane + 1] - base_level
            lands = at + plane
            half = lands // HALF
            start = section_row(half, slab)
            here = pl.ds(pl.multiple_of(start + (lands - half * HALF) * rows, SUB), rows)
            sums_ref[here, :] += lower_share * lower + upper_share * upper
            counts = pl.ds(pl.multiple_of(start + HALF * rows, SUB), SUB)
            sums_ref[counts, :] += (count_at == lands - half * HALF).astype(F32)
            lower = upper
        return carry

    for i, copy in enumerate(parts):
        copy.wait()
        lax.fori_loop(i * chunk, (i + 1) * chunk, one, 0, unroll=True)
    at = 0
    for out_ref in out_refs:
        out_ref[...] = sums_ref[at : at + out_ref.shape[0]]
        at += out_ref.shape[0]


def deposit(camera, target, first, level, fraction, slabs, shares):
    blocks, planes, rows, cols = camera.shape
    section = HALF * rows + SUB
    chunk = HALF if blocks % HALF == 0 else blocks
    return pl.pallas_call(
        functools.partial(deposit_kernel, slabs=slabs, section=section, chunk=chunk),
        in_specs=[HBM] * 5,
        out_specs=[VMEM] * len(shares),
        out_shape=[jax.ShapeDtypeStruct((share * section, cols), F32) for share in shares],
        scratch_shapes=[
            pltpu.VMEM((2 * slabs * section, cols), F32),
            pltpu.SMEM(target.shape, jnp.int32),
            pltpu.SMEM(first.shape, jnp.int32),
            pltpu.SMEM(level.shape, jnp.int32),
            pltpu.SMEM(fraction.shape, F32),
            pltpu.VMEM(camera.shape, F32),
            pltpu.SemaphoreType.DMA((4,)),
            pltpu.SemaphoreType.DMA((blocks // chunk,)),
        ],
        compiler_params=pltpu.CompilerParams(vmem_limit_bytes=DEPOSIT_VMEM_BYTES),
        name="deposit",
    )(target, first, level, fraction, camera)


def gz_pairs(partner):
    count, bands = lax.axis_size("gz"), lax.axis_size("gy")
    pairs = []
    for place in range(count):
        for band in range(bands):
            other = partner(place, band % 2 == 1)
            if 0 <= other < count:
                pairs.append((place * bands + band, other * bands + band))
    return pairs


def first_shares(slabs):
    if slabs <= 2:
        return [1] * (2 * slabs)
    return [slabs // 4] * 6 + [slabs // 2]


def fetch_kernel(*refs):
    sources, targets, sems = refs[: len(refs) // 2], refs[len(refs) // 2 : -1], refs[-1]
    copies = [pltpu.make_async_copy(*pair, sems.at[i]) for i, pair in enumerate(zip(sources, targets))]
    for copy in copies:
        copy.start()
    for copy in copies:
        copy.wait()


def fetch(*arrays):
    return pl.pallas_call(
        fetch_kernel,
        in_specs=[HBM] * len(arrays),
        out_specs=[VMEM] * len(arrays),
        out_shape=[jax.ShapeDtypeStruct(array.shape, array.dtype) for array in arrays],
        scratch_shapes=[pltpu.SemaphoreType.DMA((len(arrays),))],
        compiler_params=pltpu.CompilerParams(vmem_limit_bytes=VMEM_BYTES),
        name="fetch",
    )(*arrays)


def add_kernel(left_ref, right_ref, out_ref):
    out_ref[...] = left_ref[...] + right_ref[...]


def add(left, right):
    return pl.pallas_call(
        add_kernel,
        in_specs=[VMEM] * 2,
        out_specs=VMEM,
        out_shape=jax.ShapeDtypeStruct(left.shape, F32),
        compiler_params=pltpu.CompilerParams(vmem_limit_bytes=VMEM_BYTES),
        name="add",
    )(left, right)


def butterfly(shares, slabs, section):
    if slabs == 1:
        return [(share,) for share in shares]
    if slabs == 2:
        halves = [shares[:2], shares[2:]]
    else:
        halves, onward = [shares[:3], shares[3:6]], shares[6]
    for step in range(bit_count(slabs)):
        pairs = gz_pairs(lambda place, odd: place ^ (1 << step_bits(slabs, odd)[step]))

        def exchange(array):
            return lax.ppermute(array, ("gz", "gy"), pairs)

        if step == bit_count(slabs) - 1:
            return [(*keeps, exchange(send)) for *keeps, send in halves]
        if step == 0:
            fetched = fetch(*(half[1] for half in halves), *(half[0] for half in halves))
            halves = [[fetched[2 + i], fetched[i], half[2]] for i, half in enumerate(halves)]
        onward = exchange(onward)
        stays = [exchange(half[2]) for half in halves]
        cut = onward.shape[0] // 2
        sends = [add(half[1], array) for half, array in zip(halves, (onward[:cut], onward[cut:]))]
        if stays[0].shape[0] == section:
            halves = [(half[0], array, send) for half, array, send in zip(halves, stays, sends)]
        else:
            keeps = [add(half[0], array) for half, array in zip(halves, stays)]
            cut //= 2
            halves = [(keep[:cut], keep[cut:], send[:cut]) for keep, send in zip(keeps, sends)]
            onward = jnp.concatenate([send[cut:] for send in sends])


def join_kernel(small_ref, *rest, rows):
    *term_refs, message_ref = rest
    cols = message_ref.shape[1]
    total = term_refs[0][...]
    for term_ref in term_refs[1:]:
        total = total + term_ref[...]
    planes = total[: HALF * rows].reshape(HALF, rows, cols)
    counts = total[HALF * rows :]
    fy, fx = small_ref[3:4], small_ref[4:5]
    row_at = lax.broadcasted_iota(jnp.int32, (rows, cols), 0)
    col_at = lax.broadcasted_iota(jnp.int32, (rows, cols), 1)
    for plane in range(HALF):
        part = planes[plane]
        follow = jnp.where(row_at == rows - 1, part, pltpu.roll(part, rows - 1, 0))
        part = (1.0 - fy) * part + fy * follow
        follow = jnp.where(col_at == cols - 1, part, pltpu.roll(part, cols - 1, 1))
        part = (1.0 - fx) * part + fx * follow
        part = jnp.maximum(part / (counts[plane : plane + 1] + 1.0), DATA_FLOOR)
        message_ref[plane * rows : (plane + 1) * rows] = part
    message_ref[HALF * rows :] = small_ref[...]


def join(small, terms, rows):
    return pl.pallas_call(
        functools.partial(join_kernel, rows=rows),
        in_specs=[VMEM] * (1 + len(terms)),
        out_specs=VMEM,
        out_shape=jax.ShapeDtypeStruct(terms[0].shape, F32),
        compiler_params=pltpu.CompilerParams(vmem_limit_bytes=VMEM_BYTES),
        name="join",
    )(small, *terms)


def taps_sum(values, weights):
    result = weights[0] * values[0]
    for offset in range(1, len(weights)):
        result = result + weights[offset] * values[offset]
    return result


def parts_of(values):
    top = values.astype(jnp.bfloat16)
    return top, (values - top.astype(F32)).astype(jnp.bfloat16)


def columns_blurred(values, bands):
    cols = values.shape[1]
    both = jnp.dot(jnp.concatenate(parts_of(values), axis=1), bands, preferred_element_type=F32)
    return both[:, :cols] + both[:, cols:]


def rows_blurred(planes, bands):
    results = []
    for at in range(0, len(planes), 2):
        stacks = []
        for plane in planes[at : at + 2]:
            top, rest = parts_of(plane)
            stacks.append(jnp.concatenate([top, rest, top], axis=0))
        both = jnp.dot(bands, jnp.concatenate(stacks, axis=1), preferred_element_type=F32)
        cols = planes[at].shape[1]
        results += [both[:, index * cols : (index + 1) * cols] for index in range(len(stacks))]
    return results


def update_kernel(
    weight_ref, row_band_ref, col_band_ref, below_ref, above_ref, low_rows_ref, high_rows_ref, *rest,
    views, margin, first
):
    halves, rest = rest[: 2 * views], rest[2 * views :]
    if first:
        *own_refs, out_ref, copied_hbm, estimate, joined, first_pass, ratio, back_first, sems = rest
    else:
        est_ref, est_below_ref, est_above_ref, est_low_ref, est_high_ref, out_ref, *scratch = rest
        estimate, joined, first_pass, ratio, back_first = scratch
    planes, rows, cols = out_ref.shape
    if first:
        length = HALF * rows
        copies = [
            pltpu.make_async_copy(ref.at[pl.ds(0, length)], copied_hbm.at[pl.ds(i * length, length)], sems.at[i])
            for i, ref in enumerate(own_refs)
        ]
        for copy in copies:
            copy.start()
    taps = 2 * margin + 1
    wide = 2 * margin
    flag_low, flag_high = weight_ref[views * taps], weight_ref[views * taps + 1]
    low, body, high = slice(0, wide), slice(wide, wide + rows), slice(wide + rows, 2 * wide + rows)

    above_at = below_ref.shape[0]
    own_at = 2 * above_at
    for view in range(views):
        here = slice(view * margin, (view + 1) * margin)
        pieces = [(0, margin, below_ref[here], view * margin)]
        for half in range(2):
            own = halves[2 * view + half][: HALF * rows].reshape(HALF, rows, cols)
            pieces.append((margin + half * HALF, HALF, own, own_at + (2 * view + half) * HALF))
        pieces.append((margin + planes, margin, above_ref[here], above_at + view * margin))
        for to, length, source, edge_at in pieces:
            joined[view, to : to + length, body] = source
            joined[view, to : to + length, low] = low_rows_ref[edge_at : edge_at + length] * flag_low
            joined[view, to : to + length, high] = high_rows_ref[edge_at : edge_at + length] * flag_high
    if first:
        inner = joined[0]
        for view in range(1, views):
            inner = inner + joined[view]
        estimate[margin : planes + 3 * margin] = inner / views
        at = views * margin
        for to, source, edge_at in ((0, below_ref, at), (planes + 3 * margin, above_ref, above_at + at)):
            estimate[to : to + margin, body] = source[at : at + margin]
            estimate[to : to + margin, low] = low_rows_ref[edge_at : edge_at + margin] * flag_low
            estimate[to : to + margin, high] = high_rows_ref[edge_at : edge_at + margin] * flag_high
    else:
        for index, source in enumerate((est_below_ref, est_ref, est_above_ref)):
            here = slice(index * planes, (index + 1) * planes)
            estimate[here, body] = source[...]
            estimate[here, low] = est_low_ref[here] * flag_low
            estimate[here, high] = est_high_ref[here] * flag_high

    mid_planes, mid_rows = planes + 2 * margin, rows + 2 * margin
    weights = [[weight_ref[view * taps + tap] for tap in range(taps)] for view in range(views)]

    def along_z(tile, carry):
        here = pl.ds(pl.multiple_of(tile * SUB, SUB), SUB)
        values = [estimate[plane, here, :] for plane in range(planes + 4 * margin)]
        for view in range(views):
            for plane in range(mid_planes):
                first_pass[view, plane, here, :] = taps_sum(values[plane : plane + taps], weights[view])
        return carry

    lax.fori_loop(0, (rows + 4 * margin) // SUB, along_z, 0, unroll=2)

    for view in range(views):
        blurred = rows_blurred([first_pass[view, plane] for plane in range(mid_planes)], row_band_ref[view, 0])
        blurred = columns_blurred(
            jnp.concatenate([plane[:mid_rows] for plane in blurred], axis=0), col_band_ref[view, 0]
        )
        ratio[view] = joined[view, :, margin : margin + mid_rows, :] / blurred.reshape(mid_planes, mid_rows, cols)

    def back_z(tile, carry):
        here = pl.ds(pl.multiple_of(tile * SUB, SUB), SUB)
        for view in range(views):
            values = [ratio[view, plane, here, :] for plane in range(mid_planes)]
            for plane in range(planes):
                back_first[view, plane, here, :] = taps_sum(values[plane : plane + taps], weights[view][::-1])
        return carry

    lax.fori_loop(0, mid_rows // SUB, back_z, 0, unroll=True)

    logs = None
    for view in range(views):
        back_first[view, :, mid_rows:, :] = jnp.zeros((planes, 2 * margin, cols), F32)
        blurred = rows_blurred([back_first[view, plane] for plane in range(planes)], row_band_ref[view, 1][:rows])
        correction = columns_blurred(jnp.concatenate(blurred, axis=0), col_band_ref[view, 1])
        one = jnp.log(correction)
        logs = one if logs is None else logs + one
    out_ref[...] = estimate[wide : wide + planes, body] * jnp.exp(logs / views).reshape(planes, rows, cols)
    if first:
        for copy in copies:
            copy.wait()


def update(weights, bands, halves, below, above, low_rows, high_rows, own, later, margin):
    first = not later
    arrays = [weights, *bands, below, above, low_rows, high_rows, *halves] + list(own if first else later)
    views = len(halves) // 2
    _, rows, cols = below.shape
    planes = CZ
    mid_planes, mid_rows = planes + 2 * margin, rows + 2 * margin
    scratch = [
        (planes + 4 * margin, rows + 4 * margin),
        (views, mid_planes, rows + 4 * margin),
        (views, mid_planes, rows + 4 * margin),
        (views, mid_planes, mid_rows),
        (views, planes, rows + 4 * margin),
    ]
    out_shape = jax.ShapeDtypeStruct((planes, rows, cols), F32)
    copy_shape = jax.ShapeDtypeStruct((planes * rows, cols), F32)
    return pl.pallas_call(
        functools.partial(update_kernel, views=views, margin=margin, first=first),
        in_specs=[VMEM] * len(arrays),
        out_specs=[VMEM, HBM] if first else VMEM,
        out_shape=[out_shape, copy_shape] if first else out_shape,
        scratch_shapes=[pltpu.VMEM(shape + (cols,), F32) for shape in scratch] + [pltpu.SemaphoreType.DMA((2,))] * first,
        compiler_params=pltpu.CompilerParams(vmem_limit_bytes=VMEM_BYTES),
        name="update",
    )(*arrays)


def from_beside(axis, upward, downward):
    count = lax.axis_size(axis)
    up = [(i, i + 1) for i in range(count - 1)]
    down = [(target, source) for source, target in up]
    return lax.ppermute(upward, axis, up), lax.ppermute(downward, axis, down)


def from_slabs_beside(upward, downward):
    odd = lax.axis_index("gy") % 2 == 1
    if upward is downward:
        sends = (upward, downward)
    else:
        sends = (jnp.where(odd, downward, upward), jnp.where(odd, upward, downward))
    first = lax.ppermute(sends[0], ("gz", "gy"), gz_pairs(lambda place, odd: place - 1 if odd else place + 1))
    second = lax.ppermute(sends[1], ("gz", "gy"), gz_pairs(lambda place, odd: place + 1 if odd else place - 1))
    return jnp.where(odd, second, first), jnp.where(odd, first, second)


def edge_rows(pieces, width):
    count = lax.axis_size("gy")
    rows = pieces[0].shape[-2]
    if count == 2:
        at = jnp.where(lax.axis_index("gy") == 0, rows - width, 0)
        parts = [lax.dynamic_slice_in_dim(piece, at, width, axis=1) for piece in pieces]
        arrived = lax.ppermute(jnp.concatenate(parts), "gy", [(0, 1), (1, 0)])
        return arrived, arrived
    upward = jnp.concatenate([piece[:, rows - width :] for piece in pieces])
    downward = jnp.concatenate([piece[:, :width] for piece in pieces])
    return from_beside("gy", upward, downward)


def band_matrix(kernels, length, margin):
    places = jnp.arange(length, dtype=jnp.int32)
    shift = places[None, :] - places[:, None] + margin
    taps = kernels.shape[-1]
    return sum(jnp.where(shift == tap, kernels[:, tap, None, None], 0.0) for tap in range(taps))


def from_views(message):
    count = lax.axis_size("view")
    if count == 2:
        return [message, lax.ppermute(message, "view", [(0, 1), (1, 0)])]
    gathered = lax.all_gather(message, "view")
    return [gathered[view] for view in range(count)]


def on_device(camera, background, destination, offsets, shift_frac, psf_taps):
    slabs = lax.axis_size("gz")
    views = lax.axis_size("view")
    _, blocks, _, rows, cols = camera.shape
    taps = psf_taps.shape[-1]
    margin = taps // 2
    assert margin == HALF
    section = HALF * rows + SUB
    fraction = shift_frac[0]
    shares = deposit(
        camera[0], destination.reshape(blocks), offsets.reshape(blocks), background.reshape(1), fraction, slabs,
        first_shares(slabs),
    )
    small = jnp.concatenate(
        [
            jnp.pad(psf_taps[0], ((0, 0), (0, cols - taps))),
            jnp.broadcast_to(fraction[1:, None], (2, cols)),
            jnp.zeros((SUB - 5, cols), F32),
        ]
    )
    own, messages = [], []
    for terms in butterfly(shares, slabs, section):
        own.append(join(small, terms, rows))
        messages.append(from_views(own[-1]))
    halves = [messages[half][view] for view in range(views) for half in range(2)]
    low_half, high_half = (
        [message[: HALF * rows].reshape(HALF, rows, cols) for message in messages[half]] for half in range(2)
    )
    upward = jnp.concatenate(high_half + [sum(low_half) / views])
    downward = jnp.concatenate(low_half + [sum(high_half) / views])
    below, above = from_slabs_beside(upward, downward)
    wide = 2 * margin
    pieces = [part for view in range(views) for part in (low_half[view], high_half[view])]
    low_rows, high_rows = edge_rows([below, above] + pieces, wide)

    all_taps = jnp.stack([message[HALF * rows : HALF * rows + 3, :taps] for message in messages[0]])
    kernels = all_taps / jnp.sum(all_taps, axis=-1, keepdims=True)
    row_bands = jnp.stack([band_matrix(kernels[:, 1, ::order], rows + 4 * margin, 0) for order in (1, -1)], axis=1)
    high_part = lax.reduce_precision(row_bands, 8, 7)
    row_bands = jnp.concatenate([high_part, high_part, row_bands - high_part], axis=-1).astype(jnp.bfloat16)
    col_bands = jnp.stack([band_matrix(kernels[:, 2, ::order], cols, margin) for order in (1, -1)], axis=1)
    col_bands = jnp.swapaxes(col_bands, -1, -2)
    high_part = lax.reduce_precision(col_bands, 8, 7)
    col_bands = jnp.concatenate([high_part, col_bands - high_part], axis=-1).astype(jnp.bfloat16)
    bands = (row_bands, jnp.concatenate([col_bands, col_bands], axis=-2))
    row_band = lax.axis_index("gy")
    flags = jnp.stack([row_band > 0, row_band < lax.axis_size("gy") - 1]).astype(F32)
    weights = jnp.concatenate([kernels[:, 0].reshape(-1), flags])
    weights = jnp.broadcast_to(weights[:, None, None], (views * taps + 2, SUB, cols))

    later = ()
    for iteration in range(ITERS):
        if iteration:
            est_below, est_above = from_slabs_beside(estimate, estimate)
            later = (estimate, est_below, est_above) + edge_rows([est_below, estimate, est_above], wide)
        result = update(weights, bands, halves, below, above, low_rows, high_rows, own, later, margin)
        estimate = result if later else result[0]
        joined = joined if later else result[1]
    return (estimate, joined.reshape(1, CZ, rows, cols))


def solution(mesh):
    return jax.shard_map(
        on_device,
        mesh=mesh,
        in_specs=(
            P("view", ("groups", "gz"), None, "gy", None),
            P("view", "gy", ("groups", "gz")),
            P("view", "gy", ("groups", "gz"), None),
            P("view", "gy", ("groups", "gz")),
            P("view", None),
            P("view", None, None),
        ),
        out_specs=(P(("groups", "gz"), "gy", None), P("view", ("groups", "gz"), "gy", None)),
        check_vma=False,
    )
```

```python
import functools

import jax
import jax.numpy as jnp
from jax import lax
from jax.experimental import pallas as pl
from jax.experimental.pallas import tpu as pltpu
from jax.sharding import PartitionSpec as P

CZ = 8
HALF = CZ // 2
ITERS = 2


DATA_FLOOR = 0.25
PRECISE = lax.Precision.HIGHEST
F32 = jnp.float32
SUB = 8
VMEM = pl.BlockSpec(memory_space=pltpu.VMEM)
HBM = pl.BlockSpec(memory_space=pltpu.HBM)
VMEM_BYTES = 48 * 1024 * 1024
DEPOSIT_VMEM_BYTES = 60 * 1024 * 1024


def bit_count(count):
    bits = count.bit_length() - 1
    assert count == 1 << bits
    return bits


def step_bits(slabs, odd):
    order = list(range(bit_count(slabs)))
    if odd and len(order) > 1:
        order[:2] = [1, 0]
    return order


def section_of(value, order):
    result = 0
    for step, bit in enumerate(order):
        result = result | (((value >> bit) & 1) << (len(order) - 1 - step))
    return result


def deposit_kernel(
    target_hbm, first_hbm, level_hbm, fraction_hbm, camera_hbm, *rest, slabs, section, chunk
):
    *out_refs, sums_ref, target, first, level, fraction, camera, small_sems, camera_sems = rest
    blocks, planes, rows, cols = camera.shape
    sources = ((target_hbm, target), (first_hbm, first), (level_hbm, level), (fraction_hbm, fraction))
    smalls = [pltpu.make_async_copy(*pair, small_sems.at[i]) for i, pair in enumerate(sources)]
    parts = []
    for i in range(blocks // chunk):
        here = pl.ds(i * chunk, chunk)
        parts.append(pltpu.make_async_copy(camera_hbm.at[here], camera.at[here], camera_sems.at[i]))
    for copy in smalls + parts:
        copy.start()
    sums_ref[...] = jnp.zeros(sums_ref.shape, F32)
    for copy in smalls:
        copy.wait()
    quarter = slabs // 4

    def section_row(half, slab):
        if not quarter:
            return (half * slabs + slab) * section
        ahead = jnp.where(slab < 3 * quarter, half * 3 * quarter, 3 * quarter + half * quarter)
        return (ahead + slab) * section

    place = lax.axis_index("gz").astype(jnp.int32)
    odd = lax.axis_index("gy") % 2 == 1
    base_level = level[0].astype(F32)
    upper_share = fraction[0]
    lower_share = 1.0 - upper_share
    count_at = lax.broadcasted_iota(jnp.int32, (SUB, cols), 0)

    def one(block, carry):
        away = target[block] ^ place
        slab = jnp.where(odd, section_of(away, step_bits(slabs, True)), section_of(away, step_bits(slabs, False)))
        at = first[block]
        lower = camera[block, 0] - base_level
        for plane in range(planes - 1):
            upper = camera[block, plane + 1] - base_level
            lands = at + plane
            half = lands // HALF
            start = section_row(half, slab)
            here = pl.ds(pl.multiple_of(start + (lands - half * HALF) * rows, SUB), rows)
            sums_ref[here, :] += lower_share * lower + upper_share * upper
            counts = pl.ds(pl.multiple_of(start + HALF * rows, SUB), SUB)
            sums_ref[counts, :] += (count_at == lands - half * HALF).astype(F32)
            lower = upper
        return carry

    for i, copy in enumerate(parts):
        copy.wait()
        lax.fori_loop(i * chunk, (i + 1) * chunk, one, 0, unroll=True)
    at = 0
    for out_ref in out_refs:
        out_ref[...] = sums_ref[at : at + out_ref.shape[0]]
        at += out_ref.shape[0]


def deposit(camera, target, first, level, fraction, slabs, shares):
    blocks, planes, rows, cols = camera.shape
    section = HALF * rows + SUB
    chunk = HALF if blocks % HALF == 0 else blocks
    return pl.pallas_call(
        functools.partial(deposit_kernel, slabs=slabs, section=section, chunk=chunk),
        in_specs=[HBM] * 5,
        out_specs=[VMEM] * len(shares),
        out_shape=[jax.ShapeDtypeStruct((share * section, cols), F32) for share in shares],
        scratch_shapes=[
            pltpu.VMEM((2 * slabs * section, cols), F32),
            pltpu.SMEM(target.shape, jnp.int32),
            pltpu.SMEM(first.shape, jnp.int32),
            pltpu.SMEM(level.shape, jnp.int32),
            pltpu.SMEM(fraction.shape, F32),
            pltpu.VMEM(camera.shape, F32),
            pltpu.SemaphoreType.DMA((4,)),
            pltpu.SemaphoreType.DMA((blocks // chunk,)),
        ],
        compiler_params=pltpu.CompilerParams(vmem_limit_bytes=DEPOSIT_VMEM_BYTES),
        name="deposit",
    )(target, first, level, fraction, camera)


def gz_pairs(partner):
    count, bands = lax.axis_size("gz"), lax.axis_size("gy")
    pairs = []
    for place in range(count):
        for band in range(bands):
            other = partner(place, band % 2 == 1)
            if 0 <= other < count:
                pairs.append((place * bands + band, other * bands + band))
    return pairs


def first_shares(slabs):
    if slabs <= 2:
        return [1] * (2 * slabs)
    return [slabs // 4] * 6 + [slabs // 2]


def fetch_kernel(*refs):
    sources, targets, sems = refs[: len(refs) // 2], refs[len(refs) // 2 : -1], refs[-1]
    copies = [pltpu.make_async_copy(*pair, sems.at[i]) for i, pair in enumerate(zip(sources, targets))]
    for copy in copies:
        copy.start()
    for copy in copies:
        copy.wait()


def fetch(*arrays):
    return pl.pallas_call(
        fetch_kernel,
        in_specs=[HBM] * len(arrays),
        out_specs=[VMEM] * len(arrays),
        out_shape=[jax.ShapeDtypeStruct(array.shape, array.dtype) for array in arrays],
        scratch_shapes=[pltpu.SemaphoreType.DMA((len(arrays),))],
        compiler_params=pltpu.CompilerParams(vmem_limit_bytes=VMEM_BYTES),
        name="fetch",
    )(*arrays)


def add_kernel(left_ref, right_ref, out_ref):
    out_ref[...] = left_ref[...] + right_ref[...]


def add(left, right):
    return pl.pallas_call(
        add_kernel,
        in_specs=[VMEM] * 2,
        out_specs=VMEM,
        out_shape=jax.ShapeDtypeStruct(left.shape, F32),
        compiler_params=pltpu.CompilerParams(vmem_limit_bytes=VMEM_BYTES),
        name="add",
    )(left, right)


def butterfly(shares, slabs, section):
    if slabs == 1:
        return [(share,) for share in shares]
    if slabs == 2:
        halves = [shares[:2], shares[2:]]
    else:
        halves, onward = [shares[:3], shares[3:6]], shares[6]
    for step in range(bit_count(slabs)):
        pairs = gz_pairs(lambda place, odd: place ^ (1 << step_bits(slabs, odd)[step]))

        def exchange(array):
            return lax.ppermute(array, ("gz", "gy"), pairs)

        if step == bit_count(slabs) - 1:
            return [(*keeps, exchange(send)) for *keeps, send in halves]
        if step == 0:
            fetched = fetch(*(half[1] for half in halves), *(half[0] for half in halves))
            halves = [[fetched[2 + i], fetched[i], half[2]] for i, half in enumerate(halves)]
        onward = exchange(onward)
        stays = [exchange(half[2]) for half in halves]
        cut = onward.shape[0] // 2
        sends = [add(half[1], array) for half, array in zip(halves, (onward[:cut], onward[cut:]))]
        if stays[0].shape[0] == section:
            halves = [(half[0], array, send) for half, array, send in zip(halves, stays, sends)]
        else:
            keeps = [add(half[0], array) for half, array in zip(halves, stays)]
            cut //= 2
            halves = [(keep[:cut], keep[cut:], send[:cut]) for keep, send in zip(keeps, sends)]
            onward = jnp.concatenate([send[cut:] for send in sends])


def join_kernel(small_ref, *rest, rows):
    *term_refs, message_ref = rest
    cols = message_ref.shape[1]
    total = term_refs[0][...]
    for term_ref in term_refs[1:]:
        total = total + term_ref[...]
    planes = total[: HALF * rows].reshape(HALF, rows, cols)
    counts = total[HALF * rows :]
    fy, fx = small_ref[3:4], small_ref[4:5]
    row_at = lax.broadcasted_iota(jnp.int32, (rows, cols), 0)
    col_at = lax.broadcasted_iota(jnp.int32, (rows, cols), 1)
    for plane in range(HALF):
        part = planes[plane]
        follow = jnp.where(row_at == rows - 1, part, pltpu.roll(part, rows - 1, 0))
        part = (1.0 - fy) * part + fy * follow
        follow = jnp.where(col_at == cols - 1, part, pltpu.roll(part, cols - 1, 1))
        part = (1.0 - fx) * part + fx * follow
        part = jnp.maximum(part / (counts[plane : plane + 1] + 1.0), DATA_FLOOR)
        message_ref[plane * rows : (plane + 1) * rows] = part
    message_ref[HALF * rows :] = small_ref[...]


def join(small, terms, rows):
    return pl.pallas_call(
        functools.partial(join_kernel, rows=rows),
        in_specs=[VMEM] * (1 + len(terms)),
        out_specs=VMEM,
        out_shape=jax.ShapeDtypeStruct(terms[0].shape, F32),
        compiler_params=pltpu.CompilerParams(vmem_limit_bytes=VMEM_BYTES),
        name="join",
    )(small, *terms)


def taps_sum(values, weights):
    result = weights[0] * values[0]
    for offset in range(1, len(weights)):
        result = result + weights[offset] * values[offset]
    return result


def parts_of(values):
    top = values.astype(jnp.bfloat16)
    return top, (values - top.astype(F32)).astype(jnp.bfloat16)


def columns_blurred(values, bands):
    cols = values.shape[1]
    both = jnp.dot(jnp.concatenate(parts_of(values), axis=1), bands, preferred_element_type=F32)
    return both[:, :cols] + both[:, cols:]


def rows_blurred(planes, bands):
    results = []
    for at in range(0, len(planes), 2):
        stacks = []
        for plane in planes[at : at + 2]:
            top, rest = parts_of(plane)
            stacks.append(jnp.concatenate([top, rest, top], axis=0))
        both = jnp.dot(bands, jnp.concatenate(stacks, axis=1), preferred_element_type=F32)
        cols = planes[at].shape[1]
        results += [both[:, index * cols : (index + 1) * cols] for index in range(len(stacks))]
    return results


def prepare_kernel(weight_ref, *rest, views, margin, first):
    *sources, out_ref = rest
    _, mid_planes, rows, cols = out_ref.shape
    planes = mid_planes - 2 * margin
    taps = 2 * margin + 1
    weights = [[weight_ref[view * taps + tap] for tap in range(taps)] for view in range(views)]

    def one(tile, carry):
        here = pl.ds(pl.multiple_of(tile * SUB, SUB), SUB)
        values = []
        for plane in range(planes):
            if first:
                start = plane % HALF * rows + tile * SUB
                there = pl.ds(pl.multiple_of(start, SUB), SUB)
                value = sources[plane // HALF][there, :]
                for view in range(1, views):
                    value = value + sources[2 * view + plane // HALF][there, :]
                values.append(value / views)
            else:
                values.append(sources[0][plane, here, :])
        for view in range(views):
            for plane in range(mid_planes):
                pairs = [(tap, plane + tap - 2 * margin) for tap in range(taps) if 0 <= plane + tap - 2 * margin < planes]
                out_ref[view, plane, here, :] = taps_sum(
                    [values[at] for _, at in pairs], [weights[view][tap] for tap, _ in pairs]
                )
        return carry

    lax.fori_loop(0, rows // SUB, one, 0, unroll=2)


def prepare(weights, sources, views, margin, rows):
    first = len(sources) > 1
    cols = weights.shape[-1]
    return pl.pallas_call(
        functools.partial(prepare_kernel, views=views, margin=margin, first=first),
        in_specs=[VMEM] * (1 + len(sources)),
        out_specs=VMEM,
        out_shape=jax.ShapeDtypeStruct((views, CZ + 2 * margin, rows, cols), F32),
        compiler_params=pltpu.CompilerParams(vmem_limit_bytes=VMEM_BYTES),
        name="prepare",
    )(weights, *sources)


def update_kernel(
    weight_ref, row_band_ref, col_band_ref, below_ref, above_ref, low_rows_ref, high_rows_ref, *rest,
    views, margin, first, prepared
):
    if prepared:
        partial_ref, *rest = rest
    halves, rest = rest[: 2 * views], rest[2 * views :]
    if first:
        *own_refs, out_ref, copied_hbm, estimate, joined, first_pass, ratio, back_first, sems = rest
    else:
        est_ref, est_below_ref, est_above_ref, est_low_ref, est_high_ref, out_ref, *scratch = rest
        estimate, joined, first_pass, ratio, back_first = scratch
    planes, rows, cols = out_ref.shape
    if first:
        length = HALF * rows
        copies = [
            pltpu.make_async_copy(ref.at[pl.ds(0, length)], copied_hbm.at[pl.ds(i * length, length)], sems.at[i])
            for i, ref in enumerate(own_refs)
        ]
        for copy in copies:
            copy.start()
    taps = 2 * margin + 1
    wide = 2 * margin
    flag_low, flag_high = weight_ref[views * taps], weight_ref[views * taps + 1]
    low, body, high = slice(0, wide), slice(wide, wide + rows), slice(wide + rows, 2 * wide + rows)

    above_at = below_ref.shape[0]
    own_at = 2 * above_at
    for view in range(views):
        here = slice(view * margin, (view + 1) * margin)
        pieces = [(0, margin, below_ref[here], view * margin)]
        for half in range(2):
            own = halves[2 * view + half][: HALF * rows].reshape(HALF, rows, cols)
            pieces.append((margin + half * HALF, HALF, own, own_at + (2 * view + half) * HALF))
        pieces.append((margin + planes, margin, above_ref[here], above_at + view * margin))
        for to, length, source, edge_at in pieces:
            joined[view, to : to + length, body] = source
            joined[view, to : to + length, low] = low_rows_ref[edge_at : edge_at + length] * flag_low
            joined[view, to : to + length, high] = high_rows_ref[edge_at : edge_at + length] * flag_high
    if first:
        inner = joined[0]
        for view in range(1, views):
            inner = inner + joined[view]
        estimate[margin : planes + 3 * margin] = inner / views
        at = views * margin
        for to, source, edge_at in ((0, below_ref, at), (planes + 3 * margin, above_ref, above_at + at)):
            estimate[to : to + margin, body] = source[at : at + margin]
            estimate[to : to + margin, low] = low_rows_ref[edge_at : edge_at + margin] * flag_low
            estimate[to : to + margin, high] = high_rows_ref[edge_at : edge_at + margin] * flag_high
    else:
        for index, source in enumerate((est_below_ref, est_ref, est_above_ref)):
            here = slice(index * planes, (index + 1) * planes)
            estimate[here, body] = source[...]
            estimate[here, low] = est_low_ref[here] * flag_low
            estimate[here, high] = est_high_ref[here] * flag_high

    mid_planes, mid_rows = planes + 2 * margin, rows + 2 * margin
    weights = [[weight_ref[view * taps + tap] for tap in range(taps)] for view in range(views)]

    near = range(2 * margin, 2 * margin + planes) if prepared else ()

    def along_z(tile, carry):
        here = pl.ds(pl.multiple_of(wide + tile * SUB, SUB), SUB)
        there = pl.ds(pl.multiple_of(tile * SUB, SUB), SUB)
        values = [None if plane in near else estimate[plane, here, :] for plane in range(planes + 4 * margin)]
        for view in range(views):
            for plane in range(mid_planes):
                if prepared:
                    part = partial_ref[view, plane, there, :]
                    for tap in range(taps):
                        if plane + tap not in near:
                            part = part + weights[view][tap] * values[plane + tap]
                else:
                    part = taps_sum(values[plane : plane + taps], weights[view])
                first_pass[view, plane, here, :] = part
        return carry

    lax.fori_loop(0, rows // SUB, along_z, 0, unroll=2)

    for start in [*range(0, wide, SUB), *range(wide + rows, 2 * wide + rows, SUB)]:
        here = slice(start, start + SUB)
        values = [estimate[plane, here, :] for plane in range(planes + 4 * margin)]
        for view in range(views):
            for plane in range(mid_planes):
                first_pass[view, plane, here, :] = taps_sum(values[plane : plane + taps], weights[view])

    for view in range(views):
        blurred = rows_blurred([first_pass[view, plane] for plane in range(mid_planes)], row_band_ref[view, 0])
        blurred = columns_blurred(
            jnp.concatenate([plane[:mid_rows] for plane in blurred], axis=0), col_band_ref[view, 0]
        )
        ratio[view] = joined[view, :, margin : margin + mid_rows, :] / blurred.reshape(mid_planes, mid_rows, cols)

    def back_z(tile, carry):
        here = pl.ds(pl.multiple_of(tile * SUB, SUB), SUB)
        for view in range(views):
            values = [ratio[view, plane, here, :] for plane in range(mid_planes)]
            for plane in range(planes):
                back_first[view, plane, here, :] = taps_sum(values[plane : plane + taps], weights[view][::-1])
        return carry

    lax.fori_loop(0, mid_rows // SUB, back_z, 0, unroll=True)

    logs = None
    for view in range(views):
        back_first[view, :, mid_rows:, :] = jnp.zeros((planes, 2 * margin, cols), F32)
        blurred = rows_blurred([back_first[view, plane] for plane in range(planes)], row_band_ref[view, 1][:rows])
        correction = columns_blurred(jnp.concatenate(blurred, axis=0), col_band_ref[view, 1])
        one = jnp.log(correction)
        logs = one if logs is None else logs + one
    out_ref[...] = estimate[wide : wide + planes, body] * jnp.exp(logs / views).reshape(planes, rows, cols)
    if first:
        for copy in copies:
            copy.wait()


def update(weights, bands, partial, halves, below, above, low_rows, high_rows, own, later, margin):
    first = not later
    arrays = [weights, *bands, below, above, low_rows, high_rows, *partial, *halves] + list(own if first else later)
    views = len(halves) // 2
    _, rows, cols = below.shape
    planes = CZ
    mid_planes, mid_rows = planes + 2 * margin, rows + 2 * margin
    scratch = [
        (planes + 4 * margin, rows + 4 * margin),
        (views, mid_planes, rows + 4 * margin),
        (views, mid_planes, rows + 4 * margin),
        (views, mid_planes, mid_rows),
        (views, planes, rows + 4 * margin),
    ]
    out_shape = jax.ShapeDtypeStruct((planes, rows, cols), F32)
    copy_shape = jax.ShapeDtypeStruct((planes * rows, cols), F32)
    return pl.pallas_call(
        functools.partial(update_kernel, views=views, margin=margin, first=first, prepared=bool(partial)),
        in_specs=[VMEM] * len(arrays),
        out_specs=[VMEM, HBM] if first else VMEM,
        out_shape=[out_shape, copy_shape] if first else out_shape,
        scratch_shapes=[pltpu.VMEM(shape + (cols,), F32) for shape in scratch] + [pltpu.SemaphoreType.DMA((2,))] * first,
        compiler_params=pltpu.CompilerParams(vmem_limit_bytes=VMEM_BYTES),
        name="update",
    )(*arrays)


def from_beside(axis, upward, downward):
    count = lax.axis_size(axis)
    up = [(i, i + 1) for i in range(count - 1)]
    down = [(target, source) for source, target in up]
    return lax.ppermute(upward, axis, up), lax.ppermute(downward, axis, down)


def from_slabs_beside(upward, downward):
    turned = (lax.axis_index("gz") + lax.axis_index("gy")) % 2 == 1
    if upward is downward:
        sends = (upward, downward)
    else:
        sends = (jnp.where(turned, downward, upward), jnp.where(turned, upward, downward))
    ahead = gz_pairs(lambda place, odd: place - 1 if (place + odd) % 2 else place + 1)
    behind = gz_pairs(lambda place, odd: place + 1 if (place + odd) % 2 else place - 1)
    first = lax.ppermute(sends[0], ("gz", "gy"), ahead)
    second = lax.ppermute(sends[1], ("gz", "gy"), behind)
    return jnp.where(turned, first, second), jnp.where(turned, second, first)


def from_slabs_shifted(upward, downward):
    odd = lax.axis_index("gy") % 2 == 1
    if upward is downward:
        sends = (upward, downward)
    else:
        sends = (jnp.where(odd, downward, upward), jnp.where(odd, upward, downward))
    first = lax.ppermute(sends[0], ("gz", "gy"), gz_pairs(lambda place, odd: place - 1 if odd else place + 1))
    second = lax.ppermute(sends[1], ("gz", "gy"), gz_pairs(lambda place, odd: place + 1 if odd else place - 1))
    return jnp.where(odd, second, first), jnp.where(odd, first, second)


def edge_rows(pieces, width):
    count = lax.axis_size("gy")
    rows = pieces[0].shape[-2]
    if count == 2:
        at = jnp.where(lax.axis_index("gy") == 0, rows - width, 0)
        parts = [lax.dynamic_slice_in_dim(piece, at, width, axis=1) for piece in pieces]
        arrived = lax.ppermute(jnp.concatenate(parts), "gy", [(0, 1), (1, 0)])
        return arrived, arrived
    upward = jnp.concatenate([piece[:, rows - width :] for piece in pieces])
    downward = jnp.concatenate([piece[:, :width] for piece in pieces])
    return from_beside("gy", upward, downward)


def band_matrix(kernels, length, margin):
    places = jnp.arange(length, dtype=jnp.int32)
    shift = places[None, :] - places[:, None] + margin
    taps = kernels.shape[-1]
    return sum(jnp.where(shift == tap, kernels[:, tap, None, None], 0.0) for tap in range(taps))


def from_views(message):
    count = lax.axis_size("view")
    if count == 2:
        return [message, lax.ppermute(message, "view", [(0, 1), (1, 0)])]
    gathered = lax.all_gather(message, "view")
    return [gathered[view] for view in range(count)]


def on_device(camera, background, destination, offsets, shift_frac, psf_taps):
    slabs = lax.axis_size("gz")
    views = lax.axis_size("view")
    _, blocks, _, rows, cols = camera.shape
    taps = psf_taps.shape[-1]
    margin = taps // 2
    assert margin == HALF
    section = HALF * rows + SUB
    fraction = shift_frac[0]
    shares = deposit(
        camera[0], destination.reshape(blocks), offsets.reshape(blocks), background.reshape(1), fraction, slabs,
        first_shares(slabs),
    )
    small = jnp.concatenate(
        [
            jnp.pad(psf_taps[0], ((0, 0), (0, cols - taps))),
            jnp.broadcast_to(fraction[1:, None], (2, cols)),
            jnp.zeros((SUB - 5, cols), F32),
        ]
    )
    own, messages = [], []
    for terms in butterfly(shares, slabs, section):
        own.append(join(small, terms, rows))
        messages.append(from_views(own[-1]))
    halves = [messages[half][view] for view in range(views) for half in range(2)]
    low_half, high_half = (
        [message[: HALF * rows].reshape(HALF, rows, cols) for message in messages[half]] for half in range(2)
    )
    upward = jnp.concatenate(high_half + [sum(low_half) / views])
    downward = jnp.concatenate(low_half + [sum(high_half) / views])
    below, above = from_slabs_shifted(upward, downward)
    wide = 2 * margin
    pieces = [part for view in range(views) for part in (low_half[view], high_half[view])]
    low_rows, high_rows = edge_rows([below, above] + pieces, wide)

    all_taps = jnp.stack([message[HALF * rows : HALF * rows + 3, :taps] for message in messages[0]])
    kernels = all_taps / jnp.sum(all_taps, axis=-1, keepdims=True)
    row_bands = jnp.stack([band_matrix(kernels[:, 1, ::order], rows + 4 * margin, 0) for order in (1, -1)], axis=1)
    high_part = lax.reduce_precision(row_bands, 8, 7)
    row_bands = jnp.concatenate([high_part, high_part, row_bands - high_part], axis=-1).astype(jnp.bfloat16)
    col_bands = jnp.stack([band_matrix(kernels[:, 2, ::order], cols, margin) for order in (1, -1)], axis=1)
    col_bands = jnp.swapaxes(col_bands, -1, -2)
    high_part = lax.reduce_precision(col_bands, 8, 7)
    col_bands = jnp.concatenate([high_part, col_bands - high_part], axis=-1).astype(jnp.bfloat16)
    bands = (row_bands, jnp.concatenate([col_bands, col_bands], axis=-2))
    row_band = lax.axis_index("gy")
    flags = jnp.stack([row_band > 0, row_band < lax.axis_size("gy") - 1]).astype(F32)
    weights = jnp.concatenate([kernels[:, 0].reshape(-1), flags])
    weights = jnp.broadcast_to(weights[:, None, None], (views * taps + 2, SUB, cols))

    later = ()
    for iteration in range(ITERS):
        if iteration:
            est_below, est_above = from_slabs_beside(estimate, estimate)
            later = (estimate, est_below, est_above) + edge_rows([est_below, estimate, est_above], wide)
        partial = [] if iteration else [prepare(weights, halves, views, margin, rows)]
        result = update(weights, bands, partial, halves, below, above, low_rows, high_rows, own, later, margin)
        estimate = result if later else result[0]
        joined = joined if later else result[1]
    return (estimate, joined.reshape(1, CZ, rows, cols))


def solution(mesh):
    return jax.shard_map(
        on_device,
        mesh=mesh,
        in_specs=(
            P("view", ("groups", "gz"), None, "gy", None),
            P("view", "gy", ("groups", "gz")),
            P("view", "gy", ("groups", "gz"), None),
            P("view", "gy", ("groups", "gz")),
            P("view", None),
            P("view", None, None),
        ),
        out_specs=(P(("groups", "gz"), "gy", None), P("view", ("groups", "gz"), "gy", None)),
        check_vma=False,
    )
```

```python
import functools

import jax
import jax.numpy as jnp
from jax import lax
from jax.experimental import pallas as pl
from jax.experimental.pallas import tpu as pltpu
from jax.sharding import PartitionSpec as P

CZ = 8
HALF = CZ // 2
ITERS = 2


DATA_FLOOR = 0.25
PRECISE = lax.Precision.HIGHEST
F32 = jnp.float32
SUB = 8
VMEM = pl.BlockSpec(memory_space=pltpu.VMEM)
HBM = pl.BlockSpec(memory_space=pltpu.HBM)
VMEM_BYTES = 48 * 1024 * 1024
DEPOSIT_VMEM_BYTES = 60 * 1024 * 1024


def bit_count(count):
    bits = count.bit_length() - 1
    assert count == 1 << bits
    return bits


def step_bits(slabs, odd):
    order = list(range(bit_count(slabs)))
    if odd and len(order) > 1:
        order[:2] = [1, 0]
    return order


def section_of(value, order):
    result = 0
    for step, bit in enumerate(order):
        result = result | (((value >> bit) & 1) << (len(order) - 1 - step))
    return result


def deposit_kernel(
    target_hbm, first_hbm, level_hbm, fraction_hbm, camera_hbm, *rest, slabs, sections, chunk
):
    *out_refs, sums_ref, target, first, level, fraction, camera, small_sems, camera_sems = rest
    blocks, planes, rows, cols = camera.shape
    sources = ((target_hbm, target), (first_hbm, first), (level_hbm, level), (fraction_hbm, fraction))
    smalls = [pltpu.make_async_copy(*pair, small_sems.at[i]) for i, pair in enumerate(sources)]
    parts = []
    for i in range(blocks // chunk):
        here = pl.ds(i * chunk, chunk)
        parts.append(pltpu.make_async_copy(camera_hbm.at[here], camera.at[here], camera_sems.at[i]))
    for copy in smalls + parts:
        copy.start()
    sums_ref[...] = jnp.zeros(sums_ref.shape, F32)
    for copy in smalls:
        copy.wait()
    quarter = slabs // 4

    def section_row(half, slab):
        size = jnp.where(half == 0, sections[0], sections[1])
        if not quarter:
            return half * slabs * sections[0] + slab * size
        last = 3 * quarter * sum(sections) + half * quarter * sections[0] + (slab - 3 * quarter) * size
        return jnp.where(slab < 3 * quarter, half * 3 * quarter * sections[0] + slab * size, last)

    place = lax.axis_index("gz").astype(jnp.int32)
    odd = lax.axis_index("gy") % 2 == 1
    base_level = level[0].astype(F32)
    upper_share = fraction[0]
    lower_share = 1.0 - upper_share
    count_at = lax.broadcasted_iota(jnp.int32, (CZ, cols), 0)

    def one(block, carry):
        away = target[block] ^ place
        slab = jnp.where(odd, section_of(away, step_bits(slabs, True)), section_of(away, step_bits(slabs, False)))
        at = first[block]
        lower = camera[block, 0] - base_level
        for plane in range(planes - 1):
            upper = camera[block, plane + 1] - base_level
            lands = at + plane
            half = lands // HALF
            start = section_row(half, slab)
            here = pl.ds(pl.multiple_of(start + (lands - half * HALF) * rows, SUB), rows)
            sums_ref[here, :] += lower_share * lower + upper_share * upper
            lower = upper
        counts = pl.ds(pl.multiple_of(section_row(0, slab) + HALF * rows, SUB), CZ)
        sums_ref[counts, :] += ((count_at >= at) & (count_at < at + planes - 1)).astype(F32)
        return carry

    for i, copy in enumerate(parts):
        copy.wait()
        lax.fori_loop(i * chunk, (i + 1) * chunk, one, 0, unroll=True)
    at = 0
    for out_ref in out_refs:
        out_ref[...] = sums_ref[at : at + out_ref.shape[0]]
        at += out_ref.shape[0]


def deposit(camera, target, first, level, fraction, slabs):
    blocks, planes, rows, cols = camera.shape
    sections = section_sizes(rows)
    chunk = HALF if blocks % HALF == 0 else blocks
    return pl.pallas_call(
        functools.partial(deposit_kernel, slabs=slabs, sections=sections, chunk=chunk),
        in_specs=[HBM] * 5,
        out_specs=[VMEM] * len(first_shares(slabs, sections)),
        out_shape=[jax.ShapeDtypeStruct((size, cols), F32) for size in first_shares(slabs, sections)],
        scratch_shapes=[
            pltpu.VMEM((slabs * sum(sections), cols), F32),
            pltpu.SMEM(target.shape, jnp.int32),
            pltpu.SMEM(first.shape, jnp.int32),
            pltpu.SMEM(level.shape, jnp.int32),
            pltpu.SMEM(fraction.shape, F32),
            pltpu.VMEM(camera.shape, F32),
            pltpu.SemaphoreType.DMA((4,)),
            pltpu.SemaphoreType.DMA((blocks // chunk,)),
        ],
        compiler_params=pltpu.CompilerParams(vmem_limit_bytes=DEPOSIT_VMEM_BYTES),
        name="deposit",
    )(target, first, level, fraction, camera)


def gz_pairs(partner):
    count, bands = lax.axis_size("gz"), lax.axis_size("gy")
    pairs = []
    for place in range(count):
        for band in range(bands):
            other = partner(place, band % 2 == 1)
            if 0 <= other < count:
                pairs.append((place * bands + band, other * bands + band))
    return pairs


def section_sizes(rows):
    return HALF * rows + CZ, HALF * rows


def first_shares(slabs, sections):
    if slabs <= 2:
        return [size for size in sections for _ in range(slabs)]
    quarter = slabs // 4
    return [quarter * size for size in sections for _ in range(3)] + [quarter * sum(sections)]


def fetch_kernel(*refs):
    sources, targets, sems = refs[: len(refs) // 2], refs[len(refs) // 2 : -1], refs[-1]
    copies = [pltpu.make_async_copy(*pair, sems.at[i]) for i, pair in enumerate(zip(sources, targets))]
    for copy in copies:
        copy.start()
    for copy in copies:
        copy.wait()


def fetch(*arrays):
    return pl.pallas_call(
        fetch_kernel,
        in_specs=[HBM] * len(arrays),
        out_specs=[VMEM] * len(arrays),
        out_shape=[jax.ShapeDtypeStruct(array.shape, array.dtype) for array in arrays],
        scratch_shapes=[pltpu.SemaphoreType.DMA((len(arrays),))],
        compiler_params=pltpu.CompilerParams(vmem_limit_bytes=VMEM_BYTES),
        name="fetch",
    )(*arrays)


def add_kernel(left_ref, right_ref, out_ref):
    out_ref[...] = left_ref[...] + right_ref[...]


def add(left, right):
    return pl.pallas_call(
        add_kernel,
        in_specs=[VMEM] * 2,
        out_specs=VMEM,
        out_shape=jax.ShapeDtypeStruct(left.shape, F32),
        compiler_params=pltpu.CompilerParams(vmem_limit_bytes=VMEM_BYTES),
        name="add",
    )(left, right)


def butterfly(shares, slabs, sections):
    if slabs == 1:
        return [(share,) for share in shares]
    if slabs == 2:
        halves = [shares[:2], shares[2:]]
    else:
        halves, onward = [shares[:3], shares[3:6]], shares[6]
    for step in range(bit_count(slabs)):
        pairs = gz_pairs(lambda place, odd: place ^ (1 << step_bits(slabs, odd)[step]))

        def exchange(array):
            return lax.ppermute(array, ("gz", "gy"), pairs)

        if step == bit_count(slabs) - 1:
            return [(*keeps, exchange(send)) for *keeps, send in halves]
        if step == 0:
            fetched = fetch(*(half[1] for half in halves), *(half[0] for half in halves))
            halves = [[fetched[2 + i], fetched[i], half[2]] for i, half in enumerate(halves)]
        onward = exchange(onward)
        stays = [exchange(half[2]) for half in halves]
        cut = stays[0].shape[0]
        sends = [add(half[1], array) for half, array in zip(halves, (onward[:cut], onward[cut:]))]
        if cut == sections[0]:
            halves = [(half[0], array, send) for half, array, send in zip(halves, stays, sends)]
        else:
            keeps = [add(half[0], array) for half, array in zip(halves, stays)]
            cuts = [keep.shape[0] // 2 for keep in keeps]
            halves = [(keep[:cut], keep[cut:], send[:cut]) for cut, keep, send in zip(cuts, keeps, sends)]
            onward = jnp.concatenate([send[cut:] for cut, send in zip(cuts, sends)])


def join_kernel(small_ref, *rest, rows, half):
    if half == 0:
        *term_refs, message_ref, count_ref = rest
    else:
        count_ref, *term_refs, message_ref = rest
    cols = message_ref.shape[1]
    total = term_refs[0][...]
    for term_ref in term_refs[1:]:
        total = total + term_ref[...]
    planes = total[: HALF * rows].reshape(HALF, rows, cols)
    if half == 0:
        counts = total[HALF * rows :]
        count_ref[...] = counts
    else:
        counts = count_ref[HALF:]
    fy, fx = small_ref[3:4], small_ref[4:5]
    row_at = lax.broadcasted_iota(jnp.int32, (rows, cols), 0)
    col_at = lax.broadcasted_iota(jnp.int32, (rows, cols), 1)
    for plane in range(HALF):
        part = planes[plane]
        follow = jnp.where(row_at == rows - 1, part, pltpu.roll(part, rows - 1, 0))
        part = (1.0 - fy) * part + fy * follow
        follow = jnp.where(col_at == cols - 1, part, pltpu.roll(part, cols - 1, 1))
        part = (1.0 - fx) * part + fx * follow
        part = jnp.maximum(part / (counts[plane : plane + 1] + 1.0), DATA_FLOOR)
        message_ref[plane * rows : (plane + 1) * rows] = part
    if half == 0:
        message_ref[HALF * rows :] = small_ref[...]


def join(small, counts, terms, rows):
    half = 0 if counts is None else 1
    arrays = [small, *terms] if half == 0 else [small, counts, *terms]
    message = jax.ShapeDtypeStruct(terms[0].shape, F32)
    return pl.pallas_call(
        functools.partial(join_kernel, rows=rows, half=half),
        in_specs=[VMEM] * len(arrays),
        out_specs=[VMEM] * 2 if half == 0 else VMEM,
        out_shape=[message, jax.ShapeDtypeStruct(small.shape, F32)] if half == 0 else message,
        compiler_params=pltpu.CompilerParams(vmem_limit_bytes=VMEM_BYTES),
        name="join",
    )(*arrays)


def taps_sum(values, weights):
    result = weights[0] * values[0]
    for offset in range(1, len(weights)):
        result = result + weights[offset] * values[offset]
    return result


def parts_of(values):
    top = values.astype(jnp.bfloat16)
    return top, (values - top.astype(F32)).astype(jnp.bfloat16)


def columns_blurred(values, bands):
    cols = values.shape[1]
    both = jnp.dot(jnp.concatenate(parts_of(values), axis=1), bands, preferred_element_type=F32)
    return both[:, :cols] + both[:, cols:]


def rows_blurred(planes, bands):
    results = []
    for at in range(0, len(planes), 2):
        stacks = []
        for plane in planes[at : at + 2]:
            top, rest = parts_of(plane)
            stacks.append(jnp.concatenate([top, rest, top], axis=0))
        both = jnp.dot(bands, jnp.concatenate(stacks, axis=1), preferred_element_type=F32)
        cols = planes[at].shape[1]
        results += [both[:, index * cols : (index + 1) * cols] for index in range(len(stacks))]
    return results


def prepare_kernel(weight_ref, *rest, views, margin, first):
    *sources, out_ref = rest
    _, mid_planes, rows, cols = out_ref.shape
    planes = mid_planes - 2 * margin
    taps = 2 * margin + 1
    weights = [[weight_ref[view * taps + tap] for tap in range(taps)] for view in range(views)]

    def one(tile, carry):
        here = pl.ds(pl.multiple_of(tile * SUB, SUB), SUB)
        values = []
        for plane in range(planes):
            if first:
                start = plane % HALF * rows + tile * SUB
                there = pl.ds(pl.multiple_of(start, SUB), SUB)
                value = sources[plane // HALF][there, :]
                for view in range(1, views):
                    value = value + sources[2 * view + plane // HALF][there, :]
                values.append(value / views)
            else:
                values.append(sources[0][plane, here, :])
        for view in range(views):
            for plane in range(mid_planes):
                pairs = [(tap, plane + tap - 2 * margin) for tap in range(taps) if 0 <= plane + tap - 2 * margin < planes]
                out_ref[view, plane, here, :] = taps_sum(
                    [values[at] for _, at in pairs], [weights[view][tap] for tap, _ in pairs]
                )
        return carry

    lax.fori_loop(0, rows // SUB, one, 0, unroll=2)


def prepare(weights, sources, views, margin, rows):
    first = len(sources) > 1
    cols = weights.shape[-1]
    return pl.pallas_call(
        functools.partial(prepare_kernel, views=views, margin=margin, first=first),
        in_specs=[VMEM] * (1 + len(sources)),
        out_specs=VMEM,
        out_shape=jax.ShapeDtypeStruct((views, CZ + 2 * margin, rows, cols), F32),
        compiler_params=pltpu.CompilerParams(vmem_limit_bytes=VMEM_BYTES),
        name="prepare",
    )(weights, *sources)


def update_kernel(
    weight_ref, row_band_ref, col_band_ref, below_ref, above_ref, low_rows_ref, high_rows_ref, *rest,
    views, margin, first, prepared
):
    if prepared:
        partial_ref, *rest = rest
    halves, rest = rest[: 2 * views], rest[2 * views :]
    if first:
        *own_refs, out_ref, copied_hbm, estimate, joined, first_pass, ratio, back_first, sems = rest
    else:
        est_ref, est_below_ref, est_above_ref, est_low_ref, est_high_ref, out_ref, *scratch = rest
        estimate, joined, first_pass, ratio, back_first = scratch
    planes, rows, cols = out_ref.shape
    if first:
        length = HALF * rows
        copies = [
            pltpu.make_async_copy(ref.at[pl.ds(0, length)], copied_hbm.at[pl.ds(i * length, length)], sems.at[i])
            for i, ref in enumerate(own_refs)
        ]
        for copy in copies:
            copy.start()
    taps = 2 * margin + 1
    wide = 2 * margin
    flag_low, flag_high = weight_ref[views * taps], weight_ref[views * taps + 1]
    low, body, high = slice(0, wide), slice(wide, wide + rows), slice(wide + rows, 2 * wide + rows)

    above_at = below_ref.shape[0]
    own_at = 2 * above_at
    for view in range(views):
        here = slice(view * margin, (view + 1) * margin)
        pieces = [(0, margin, below_ref[here], view * margin)]
        for half in range(2):
            own = halves[2 * view + half][: HALF * rows].reshape(HALF, rows, cols)
            pieces.append((margin + half * HALF, HALF, own, own_at + (2 * view + half) * HALF))
        pieces.append((margin + planes, margin, above_ref[here], above_at + view * margin))
        for to, length, source, edge_at in pieces:
            joined[view, to : to + length, body] = source
            joined[view, to : to + length, low] = low_rows_ref[edge_at : edge_at + length] * flag_low
            joined[view, to : to + length, high] = high_rows_ref[edge_at : edge_at + length] * flag_high
    if first:
        inner = joined[0]
        for view in range(1, views):
            inner = inner + joined[view]
        estimate[margin : planes + 3 * margin] = inner / views
        at = views * margin
        for to, source, edge_at in ((0, below_ref, at), (planes + 3 * margin, above_ref, above_at + at)):
            estimate[to : to + margin, body] = source[at : at + margin]
            estimate[to : to + margin, low] = low_rows_ref[edge_at : edge_at + margin] * flag_low
            estimate[to : to + margin, high] = high_rows_ref[edge_at : edge_at + margin] * flag_high
    else:
        for index, source in enumerate((est_below_ref, est_ref, est_above_ref)):
            here = slice(index * planes, (index + 1) * planes)
            estimate[here, body] = source[...]
            estimate[here, low] = est_low_ref[here] * flag_low
            estimate[here, high] = est_high_ref[here] * flag_high

    mid_planes, mid_rows = planes + 2 * margin, rows + 2 * margin
    weights = [[weight_ref[view * taps + tap] for tap in range(taps)] for view in range(views)]

    near = range(2 * margin, 2 * margin + planes) if prepared else ()

    def along_z(tile, carry):
        here = pl.ds(pl.multiple_of(wide + tile * SUB, SUB), SUB)
        there = pl.ds(pl.multiple_of(tile * SUB, SUB), SUB)
        values = [None if plane in near else estimate[plane, here, :] for plane in range(planes + 4 * margin)]
        for view in range(views):
            for plane in range(mid_planes):
                if prepared:
                    part = partial_ref[view, plane, there, :]
                    for tap in range(taps):
                        if plane + tap not in near:
                            part = part + weights[view][tap] * values[plane + tap]
                else:
                    part = taps_sum(values[plane : plane + taps], weights[view])
                first_pass[view, plane, here, :] = part
        return carry

    lax.fori_loop(0, rows // SUB, along_z, 0, unroll=2)

    for start in [*range(0, wide, SUB), *range(wide + rows, 2 * wide + rows, SUB)]:
        here = slice(start, start + SUB)
        values = [estimate[plane, here, :] for plane in range(planes + 4 * margin)]
        for view in range(views):
            for plane in range(mid_planes):
                first_pass[view, plane, here, :] = taps_sum(values[plane : plane + taps], weights[view])

    for view in range(views):
        blurred = rows_blurred([first_pass[view, plane] for plane in range(mid_planes)], row_band_ref[view, 0])
        blurred = columns_blurred(
            jnp.concatenate([plane[:mid_rows] for plane in blurred], axis=0), col_band_ref[view, 0]
        )
        ratio[view] = joined[view, :, margin : margin + mid_rows, :] / blurred.reshape(mid_planes, mid_rows, cols)

    def back_z(tile, carry):
        here = pl.ds(pl.multiple_of(tile * SUB, SUB), SUB)
        for view in range(views):
            values = [ratio[view, plane, here, :] for plane in range(mid_planes)]
            for plane in range(planes):
                back_first[view, plane, here, :] = taps_sum(values[plane : plane + taps], weights[view][::-1])
        return carry

    lax.fori_loop(0, mid_rows // SUB, back_z, 0, unroll=True)

    logs = None
    for view in range(views):
        back_first[view, :, mid_rows:, :] = jnp.zeros((planes, 2 * margin, cols), F32)
        blurred = rows_blurred([back_first[view, plane] for plane in range(planes)], row_band_ref[view, 1][:rows])
        correction = columns_blurred(jnp.concatenate(blurred, axis=0), col_band_ref[view, 1])
        one = jnp.log(correction)
        logs = one if logs is None else logs + one
    out_ref[...] = estimate[wide : wide + planes, body] * jnp.exp(logs / views).reshape(planes, rows, cols)
    if first:
        for copy in copies:
            copy.wait()


def update(weights, bands, partial, halves, below, above, low_rows, high_rows, own, later, margin):
    first = not later
    arrays = [weights, *bands, below, above, low_rows, high_rows, *partial, *halves] + list(own if first else later)
    views = len(halves) // 2
    _, rows, cols = below.shape
    planes = CZ
    mid_planes, mid_rows = planes + 2 * margin, rows + 2 * margin
    scratch = [
        (planes + 4 * margin, rows + 4 * margin),
        (views, mid_planes, rows + 4 * margin),
        (views, mid_planes, rows + 4 * margin),
        (views, mid_planes, mid_rows),
        (views, planes, rows + 4 * margin),
    ]
    out_shape = jax.ShapeDtypeStruct((planes, rows, cols), F32)
    copy_shape = jax.ShapeDtypeStruct((planes * rows, cols), F32)
    return pl.pallas_call(
        functools.partial(update_kernel, views=views, margin=margin, first=first, prepared=bool(partial)),
        in_specs=[VMEM] * len(arrays),
        out_specs=[VMEM, HBM] if first else VMEM,
        out_shape=[out_shape, copy_shape] if first else out_shape,
        scratch_shapes=[pltpu.VMEM(shape + (cols,), F32) for shape in scratch] + [pltpu.SemaphoreType.DMA((2,))] * first,
        compiler_params=pltpu.CompilerParams(vmem_limit_bytes=VMEM_BYTES),
        name="update",
    )(*arrays)


def from_beside(axis, upward, downward):
    count = lax.axis_size(axis)
    up = [(i, i + 1) for i in range(count - 1)]
    down = [(target, source) for source, target in up]
    return lax.ppermute(upward, axis, up), lax.ppermute(downward, axis, down)


def from_slabs_beside(upward, downward):
    turned = (lax.axis_index("gz") + lax.axis_index("gy")) % 2 == 1
    if upward is downward:
        sends = (upward, downward)
    else:
        sends = (jnp.where(turned, downward, upward), jnp.where(turned, upward, downward))
    ahead = gz_pairs(lambda place, odd: place - 1 if (place + odd) % 2 else place + 1)
    behind = gz_pairs(lambda place, odd: place + 1 if (place + odd) % 2 else place - 1)
    first = lax.ppermute(sends[0], ("gz", "gy"), ahead)
    second = lax.ppermute(sends[1], ("gz", "gy"), behind)
    return jnp.where(turned, first, second), jnp.where(turned, second, first)


def from_slabs_shifted(upward, downward):
    odd = lax.axis_index("gy") % 2 == 1
    if upward is downward:
        sends = (upward, downward)
    else:
        sends = (jnp.where(odd, downward, upward), jnp.where(odd, upward, downward))
    first = lax.ppermute(sends[0], ("gz", "gy"), gz_pairs(lambda place, odd: place - 1 if odd else place + 1))
    second = lax.ppermute(sends[1], ("gz", "gy"), gz_pairs(lambda place, odd: place + 1 if odd else place - 1))
    return jnp.where(odd, second, first), jnp.where(odd, first, second)


def edge_rows(pieces, width):
    count = lax.axis_size("gy")
    rows = pieces[0].shape[-2]
    if count == 2:
        at = jnp.where(lax.axis_index("gy") == 0, rows - width, 0)
        parts = [lax.dynamic_slice_in_dim(piece, at, width, axis=1) for piece in pieces]
        arrived = lax.ppermute(jnp.concatenate(parts), "gy", [(0, 1), (1, 0)])
        return arrived, arrived
    upward = jnp.concatenate([piece[:, rows - width :] for piece in pieces])
    downward = jnp.concatenate([piece[:, :width] for piece in pieces])
    return from_beside("gy", upward, downward)


def band_matrix(kernels, length, margin):
    places = jnp.arange(length, dtype=jnp.int32)
    shift = places[None, :] - places[:, None] + margin
    taps = kernels.shape[-1]
    return sum(jnp.where(shift == tap, kernels[:, tap, None, None], 0.0) for tap in range(taps))


def from_views(message):
    count = lax.axis_size("view")
    if count == 2:
        return [message, lax.ppermute(message, "view", [(0, 1), (1, 0)])]
    gathered = lax.all_gather(message, "view")
    return [gathered[view] for view in range(count)]


def on_device(camera, background, destination, offsets, shift_frac, psf_taps):
    slabs = lax.axis_size("gz")
    views = lax.axis_size("view")
    _, blocks, _, rows, cols = camera.shape
    taps = psf_taps.shape[-1]
    margin = taps // 2
    assert margin == HALF
    fraction = shift_frac[0]
    shares = deposit(
        camera[0], destination.reshape(blocks), offsets.reshape(blocks), background.reshape(1), fraction, slabs
    )
    small = jnp.concatenate(
        [
            jnp.pad(psf_taps[0], ((0, 0), (0, cols - taps))),
            jnp.broadcast_to(fraction[1:, None], (2, cols)),
            jnp.zeros((SUB - 5, cols), F32),
        ]
    )
    own, messages = [], []
    counts = None
    for terms in butterfly(shares, slabs, section_sizes(rows)):
        if counts is None:
            message, counts = join(small, counts, terms, rows)
        else:
            message = join(small, counts, terms, rows)
        own.append(message)
        messages.append(from_views(message))
    halves = [messages[half][view] for view in range(views) for half in range(2)]
    low_half, high_half = (
        [message[: HALF * rows].reshape(HALF, rows, cols) for message in messages[half]] for half in range(2)
    )
    upward = jnp.concatenate(high_half + [sum(low_half) / views])
    downward = jnp.concatenate(low_half + [sum(high_half) / views])
    below, above = from_slabs_shifted(upward, downward)
    wide = 2 * margin
    pieces = [part for view in range(views) for part in (low_half[view], high_half[view])]
    low_rows, high_rows = edge_rows([below, above] + pieces, wide)

    all_taps = jnp.stack([message[HALF * rows : HALF * rows + 3, :taps] for message in messages[0]])
    kernels = all_taps / jnp.sum(all_taps, axis=-1, keepdims=True)
    row_bands = jnp.stack([band_matrix(kernels[:, 1, ::order], rows + 4 * margin, 0) for order in (1, -1)], axis=1)
    high_part = lax.reduce_precision(row_bands, 8, 7)
    row_bands = jnp.concatenate([high_part, high_part, row_bands - high_part], axis=-1).astype(jnp.bfloat16)
    col_bands = jnp.stack([band_matrix(kernels[:, 2, ::order], cols, margin) for order in (1, -1)], axis=1)
    col_bands = jnp.swapaxes(col_bands, -1, -2)
    high_part = lax.reduce_precision(col_bands, 8, 7)
    col_bands = jnp.concatenate([high_part, col_bands - high_part], axis=-1).astype(jnp.bfloat16)
    bands = (row_bands, jnp.concatenate([col_bands, col_bands], axis=-2))
    row_band = lax.axis_index("gy")
    flags = jnp.stack([row_band > 0, row_band < lax.axis_size("gy") - 1]).astype(F32)
    weights = jnp.concatenate([kernels[:, 0].reshape(-1), flags])
    weights = jnp.broadcast_to(weights[:, None, None], (views * taps + 2, SUB, cols))

    later = ()
    for iteration in range(ITERS):
        if iteration:
            est_below, est_above = from_slabs_beside(estimate, estimate)
            later = (estimate, est_below, est_above) + edge_rows([est_below, estimate, est_above], wide)
        partial = [] if iteration else [prepare(weights, halves, views, margin, rows)]
        result = update(weights, bands, partial, halves, below, above, low_rows, high_rows, own, later, margin)
        estimate = result if later else result[0]
        joined = joined if later else result[1]
    return (estimate, joined.reshape(1, CZ, rows, cols))


def solution(mesh):
    return jax.shard_map(
        on_device,
        mesh=mesh,
        in_specs=(
            P("view", ("groups", "gz"), None, "gy", None),
            P("view", "gy", ("groups", "gz")),
            P("view", "gy", ("groups", "gz"), None),
            P("view", "gy", ("groups", "gz")),
            P("view", None),
            P("view", None, None),
        ),
        out_specs=(P(("groups", "gz"), "gy", None), P("view", ("groups", "gz"), "gy", None)),
        check_vma=False,
    )
```

```python
import functools

import jax
import jax.numpy as jnp
from jax import lax
from jax.experimental import pallas as pl
from jax.experimental.pallas import tpu as pltpu
from jax.sharding import PartitionSpec as P

CZ = 8
HALF = CZ // 2
ITERS = 2


DATA_FLOOR = 0.25
PRECISE = lax.Precision.HIGHEST
F32 = jnp.float32
SUB = 8
VMEM = pl.BlockSpec(memory_space=pltpu.VMEM)
HBM = pl.BlockSpec(memory_space=pltpu.HBM)
VMEM_BYTES = 48 * 1024 * 1024
DEPOSIT_VMEM_BYTES = 60 * 1024 * 1024


def bit_count(count):
    bits = count.bit_length() - 1
    assert count == 1 << bits
    return bits


def step_bits(slabs, odd):
    order = list(range(bit_count(slabs)))
    if odd and len(order) > 1:
        order[:2] = [1, 0]
    return order


def section_of(value, order):
    result = 0
    for step, bit in enumerate(order):
        result = result | (((value >> bit) & 1) << (len(order) - 1 - step))
    return result


def deposit_kernel(
    target_hbm, first_hbm, level_hbm, fraction_hbm, camera_hbm, *rest, slabs, sections, chunk
):
    *out_refs, sums_ref, target, first, level, fraction, camera, small_sems, camera_sems = rest
    blocks, planes, rows, cols = camera.shape
    sources = ((target_hbm, target), (first_hbm, first), (level_hbm, level), (fraction_hbm, fraction))
    smalls = [pltpu.make_async_copy(*pair, small_sems.at[i]) for i, pair in enumerate(sources)]
    parts = []
    for i in range(blocks // chunk):
        here = pl.ds(i * chunk, chunk)
        parts.append(pltpu.make_async_copy(camera_hbm.at[here], camera.at[here], camera_sems.at[i]))
    for copy in smalls + parts:
        copy.start()
    sums_ref[...] = jnp.zeros(sums_ref.shape, F32)
    for copy in smalls:
        copy.wait()
    quarter = slabs // 4

    def section_row(half, slab):
        size = jnp.where(half == 0, sections[0], sections[1])
        if not quarter:
            return half * slabs * sections[0] + slab * size
        last = 3 * quarter * sum(sections) + half * quarter * sections[0] + (slab - 3 * quarter) * size
        return jnp.where(slab < 3 * quarter, half * 3 * quarter * sections[0] + slab * size, last)

    place = lax.axis_index("gz").astype(jnp.int32)
    odd = lax.axis_index("gy") % 2 == 1
    base_level = level[0].astype(F32)
    upper_share = fraction[0]
    lower_share = 1.0 - upper_share
    count_at = lax.broadcasted_iota(jnp.int32, (CZ, cols), 0)

    def one(block, carry):
        away = target[block] ^ place
        slab = jnp.where(odd, section_of(away, step_bits(slabs, True)), section_of(away, step_bits(slabs, False)))
        at = first[block]
        lower = camera[block, 0] - base_level
        landings = []
        for plane in range(planes - 1):
            upper = camera[block, plane + 1] - base_level
            lands = at + plane
            half = lands // HALF
            start = section_row(half, slab)
            here = pl.ds(pl.multiple_of(start + (lands - half * HALF) * rows, SUB), rows)
            landings.append((here, lower_share * lower + upper_share * upper))
            lower = upper
        counts = pl.ds(pl.multiple_of(section_row(0, slab) + HALF * rows, SUB), CZ)
        landings.append((counts, ((count_at >= at) & (count_at < at + planes - 1)).astype(F32)))
        sums = [sums_ref[here, :] + value for here, value in landings]
        for (here, _), value in zip(landings, sums):
            sums_ref[here, :] = value
        return carry

    for i, copy in enumerate(parts):
        copy.wait()
        lax.fori_loop(i * chunk, (i + 1) * chunk, one, 0, unroll=True)
    at = 0
    for out_ref in out_refs:
        out_ref[...] = sums_ref[at : at + out_ref.shape[0]]
        at += out_ref.shape[0]


def deposit(camera, target, first, level, fraction, slabs):
    blocks, planes, rows, cols = camera.shape
    sections = section_sizes(rows)
    chunk = HALF if blocks % HALF == 0 else blocks
    return pl.pallas_call(
        functools.partial(deposit_kernel, slabs=slabs, sections=sections, chunk=chunk),
        in_specs=[HBM] * 5,
        out_specs=[VMEM] * len(first_shares(slabs, sections)),
        out_shape=[jax.ShapeDtypeStruct((size, cols), F32) for size in first_shares(slabs, sections)],
        scratch_shapes=[
            pltpu.VMEM((slabs * sum(sections), cols), F32),
            pltpu.SMEM(target.shape, jnp.int32),
            pltpu.SMEM(first.shape, jnp.int32),
            pltpu.SMEM(level.shape, jnp.int32),
            pltpu.SMEM(fraction.shape, F32),
            pltpu.VMEM(camera.shape, F32),
            pltpu.SemaphoreType.DMA((4,)),
            pltpu.SemaphoreType.DMA((blocks // chunk,)),
        ],
        compiler_params=pltpu.CompilerParams(vmem_limit_bytes=DEPOSIT_VMEM_BYTES),
        name="deposit",
    )(target, first, level, fraction, camera)


def gz_pairs(partner):
    count, bands = lax.axis_size("gz"), lax.axis_size("gy")
    pairs = []
    for place in range(count):
        for band in range(bands):
            other = partner(place, band % 2 == 1)
            if 0 <= other < count:
                pairs.append((place * bands + band, other * bands + band))
    return pairs


def section_sizes(rows):
    return HALF * rows + CZ, HALF * rows


def first_shares(slabs, sections):
    if slabs <= 2:
        return [size for size in sections for _ in range(slabs)]
    quarter = slabs // 4
    return [quarter * size for size in sections for _ in range(3)] + [quarter * sum(sections)]


def fetch_kernel(*refs):
    sources, targets, sems = refs[: len(refs) // 2], refs[len(refs) // 2 : -1], refs[-1]
    copies = [pltpu.make_async_copy(*pair, sems.at[i]) for i, pair in enumerate(zip(sources, targets))]
    for copy in copies:
        copy.start()
    for copy in copies:
        copy.wait()


def fetch(*arrays):
    return pl.pallas_call(
        fetch_kernel,
        in_specs=[HBM] * len(arrays),
        out_specs=[VMEM] * len(arrays),
        out_shape=[jax.ShapeDtypeStruct(array.shape, array.dtype) for array in arrays],
        scratch_shapes=[pltpu.SemaphoreType.DMA((len(arrays),))],
        compiler_params=pltpu.CompilerParams(vmem_limit_bytes=VMEM_BYTES),
        name="fetch",
    )(*arrays)


def add_kernel(left_ref, right_ref, out_ref):
    out_ref[...] = left_ref[...] + right_ref[...]


def add(left, right):
    return pl.pallas_call(
        add_kernel,
        in_specs=[VMEM] * 2,
        out_specs=VMEM,
        out_shape=jax.ShapeDtypeStruct(left.shape, F32),
        compiler_params=pltpu.CompilerParams(vmem_limit_bytes=VMEM_BYTES),
        name="add",
    )(left, right)


def butterfly(shares, slabs, sections):
    if slabs == 1:
        return [(share,) for share in shares]
    if slabs == 2:
        halves = [shares[:2], shares[2:]]
    else:
        halves, onward = [shares[:3], shares[3:6]], shares[6]
    for step in range(bit_count(slabs)):
        pairs = gz_pairs(lambda place, odd: place ^ (1 << step_bits(slabs, odd)[step]))

        def exchange(array):
            return lax.ppermute(array, ("gz", "gy"), pairs)

        if step == bit_count(slabs) - 1:
            return [(*keeps, exchange(send)) for *keeps, send in halves]
        if step == 0:
            fetched = fetch(*(half[1] for half in halves), *(half[0] for half in halves))
            halves = [[fetched[2 + i], fetched[i], half[2]] for i, half in enumerate(halves)]
        onward = exchange(onward)
        stays = [exchange(half[2]) for half in halves]
        cut = stays[0].shape[0]
        sends = [add(half[1], array) for half, array in zip(halves, (onward[:cut], onward[cut:]))]
        if cut == sections[0]:
            halves = [(half[0], array, send) for half, array, send in zip(halves, stays, sends)]
        else:
            keeps = [add(half[0], array) for half, array in zip(halves, stays)]
            cuts = [keep.shape[0] // 2 for keep in keeps]
            halves = [(keep[:cut], keep[cut:], send[:cut]) for cut, keep, send in zip(cuts, keeps, sends)]
            onward = jnp.concatenate([send[cut:] for cut, send in zip(cuts, sends)])


def join_kernel(small_ref, *rest, rows, half):
    if half == 0:
        *term_refs, message_ref, count_ref = rest
    else:
        count_ref, *term_refs, message_ref = rest
    cols = message_ref.shape[1]
    total = term_refs[0][...]
    for term_ref in term_refs[1:]:
        total = total + term_ref[...]
    planes = total[: HALF * rows].reshape(HALF, rows, cols)
    if half == 0:
        counts = total[HALF * rows :]
        count_ref[...] = counts
    else:
        counts = count_ref[HALF:]
    fy, fx = small_ref[3:4], small_ref[4:5]
    row_at = lax.broadcasted_iota(jnp.int32, (rows, cols), 0)
    col_at = lax.broadcasted_iota(jnp.int32, (rows, cols), 1)
    for plane in range(HALF):
        part = planes[plane]
        follow = jnp.where(row_at == rows - 1, part, pltpu.roll(part, rows - 1, 0))
        part = (1.0 - fy) * part + fy * follow
        follow = jnp.where(col_at == cols - 1, part, pltpu.roll(part, cols - 1, 1))
        part = (1.0 - fx) * part + fx * follow
        part = jnp.maximum(part / (counts[plane : plane + 1] + 1.0), DATA_FLOOR)
        message_ref[plane * rows : (plane + 1) * rows] = part
    if half == 0:
        message_ref[HALF * rows :] = small_ref[...]


def join(small, counts, terms, rows):
    half = 0 if counts is None else 1
    arrays = [small, *terms] if half == 0 else [small, counts, *terms]
    message = jax.ShapeDtypeStruct(terms[0].shape, F32)
    return pl.pallas_call(
        functools.partial(join_kernel, rows=rows, half=half),
        in_specs=[VMEM] * len(arrays),
        out_specs=[VMEM] * 2 if half == 0 else VMEM,
        out_shape=[message, jax.ShapeDtypeStruct(small.shape, F32)] if half == 0 else message,
        compiler_params=pltpu.CompilerParams(vmem_limit_bytes=VMEM_BYTES),
        name="join",
    )(*arrays)


def taps_sum(values, weights):
    result = weights[0] * values[0]
    for offset in range(1, len(weights)):
        result = result + weights[offset] * values[offset]
    return result


def parts_of(values):
    top = values.astype(jnp.bfloat16)
    return top, (values - top.astype(F32)).astype(jnp.bfloat16)


def columns_blurred(values, bands):
    cols = values.shape[1]
    both = jnp.dot(jnp.concatenate(parts_of(values), axis=1), bands, preferred_element_type=F32)
    return both[:, :cols] + both[:, cols:]


def rows_blurred(planes, bands):
    results = []
    for at in range(0, len(planes), 2):
        stacks = []
        for plane in planes[at : at + 2]:
            top, rest = parts_of(plane)
            stacks.append(jnp.concatenate([top, rest, top], axis=0))
        both = jnp.dot(bands, jnp.concatenate(stacks, axis=1), preferred_element_type=F32)
        cols = planes[at].shape[1]
        results += [both[:, index * cols : (index + 1) * cols] for index in range(len(stacks))]
    return results


def prepare_kernel(weight_ref, *rest, views, margin, first):
    *sources, out_ref = rest
    _, mid_planes, rows, cols = out_ref.shape
    planes = mid_planes - 2 * margin
    taps = 2 * margin + 1
    weights = [[weight_ref[view * taps + tap] for tap in range(taps)] for view in range(views)]

    def one(tile, carry):
        here = pl.ds(pl.multiple_of(tile * SUB, SUB), SUB)
        values = []
        for plane in range(planes):
            if first:
                start = plane % HALF * rows + tile * SUB
                there = pl.ds(pl.multiple_of(start, SUB), SUB)
                value = sources[plane // HALF][there, :]
                for view in range(1, views):
                    value = value + sources[2 * view + plane // HALF][there, :]
                values.append(value / views)
            else:
                values.append(sources[0][plane, here, :])
        for view in range(views):
            for plane in range(mid_planes):
                pairs = [(tap, plane + tap - 2 * margin) for tap in range(taps) if 0 <= plane + tap - 2 * margin < planes]
                out_ref[view, plane, here, :] = taps_sum(
                    [values[at] for _, at in pairs], [weights[view][tap] for tap, _ in pairs]
                )
        return carry

    lax.fori_loop(0, rows // SUB, one, 0, unroll=2)


def prepare(weights, sources, views, margin, rows):
    first = len(sources) > 1
    cols = weights.shape[-1]
    return pl.pallas_call(
        functools.partial(prepare_kernel, views=views, margin=margin, first=first),
        in_specs=[VMEM] * (1 + len(sources)),
        out_specs=VMEM,
        out_shape=jax.ShapeDtypeStruct((views, CZ + 2 * margin, rows, cols), F32),
        compiler_params=pltpu.CompilerParams(vmem_limit_bytes=VMEM_BYTES),
        name="prepare",
    )(weights, *sources)


def update_kernel(
    weight_ref, row_band_ref, col_band_ref, below_ref, above_ref, low_rows_ref, high_rows_ref, *rest,
    views, margin, first, prepared
):
    if prepared:
        partial_ref, *rest = rest
    halves, rest = rest[: 2 * views], rest[2 * views :]
    if first:
        *own_refs, out_ref, copied_hbm, estimate, joined, first_pass, ratio, back_first, sems = rest
    else:
        est_ref, est_below_ref, est_above_ref, est_low_ref, est_high_ref, out_ref, *scratch = rest
        estimate, joined, first_pass, ratio, back_first = scratch
    planes, rows, cols = out_ref.shape
    if first:
        length = HALF * rows
        copies = [
            pltpu.make_async_copy(ref.at[pl.ds(0, length)], copied_hbm.at[pl.ds(i * length, length)], sems.at[i])
            for i, ref in enumerate(own_refs)
        ]
        for copy in copies:
            copy.start()
    taps = 2 * margin + 1
    wide = 2 * margin
    flag_low, flag_high = weight_ref[views * taps], weight_ref[views * taps + 1]
    low, body, high = slice(0, wide), slice(wide, wide + rows), slice(wide + rows, 2 * wide + rows)

    above_at = below_ref.shape[0]
    own_at = 2 * above_at
    for view in range(views):
        here = slice(view * margin, (view + 1) * margin)
        pieces = [(0, margin, below_ref[here], view * margin)]
        for half in range(2):
            own = halves[2 * view + half][: HALF * rows].reshape(HALF, rows, cols)
            pieces.append((margin + half * HALF, HALF, own, own_at + (2 * view + half) * HALF))
        pieces.append((margin + planes, margin, above_ref[here], above_at + view * margin))
        for to, length, source, edge_at in pieces:
            joined[view, to : to + length, body] = source
            joined[view, to : to + length, low] = low_rows_ref[edge_at : edge_at + length] * flag_low
            joined[view, to : to + length, high] = high_rows_ref[edge_at : edge_at + length] * flag_high
    if first:
        inner = joined[0]
        for view in range(1, views):
            inner = inner + joined[view]
        estimate[margin : planes + 3 * margin] = inner / views
        at = views * margin
        for to, source, edge_at in ((0, below_ref, at), (planes + 3 * margin, above_ref, above_at + at)):
            estimate[to : to + margin, body] = source[at : at + margin]
            estimate[to : to + margin, low] = low_rows_ref[edge_at : edge_at + margin] * flag_low
            estimate[to : to + margin, high] = high_rows_ref[edge_at : edge_at + margin] * flag_high
    else:
        for index, source in enumerate((est_below_ref, est_ref, est_above_ref)):
            here = slice(index * planes, (index + 1) * planes)
            estimate[here, body] = source[...]
            estimate[here, low] = est_low_ref[here] * flag_low
            estimate[here, high] = est_high_ref[here] * flag_high

    mid_planes, mid_rows = planes + 2 * margin, rows + 2 * margin
    weights = [[weight_ref[view * taps + tap] for tap in range(taps)] for view in range(views)]

    near = range(2 * margin, 2 * margin + planes) if prepared else ()

    def along_z(tile, carry):
        here = pl.ds(pl.multiple_of(wide + tile * SUB, SUB), SUB)
        there = pl.ds(pl.multiple_of(tile * SUB, SUB), SUB)
        values = [None if plane in near else estimate[plane, here, :] for plane in range(planes + 4 * margin)]
        for view in range(views):
            for plane in range(mid_planes):
                if prepared:
                    part = partial_ref[view, plane, there, :]
                    for tap in range(taps):
                        if plane + tap not in near:
                            part = part + weights[view][tap] * values[plane + tap]
                else:
                    part = taps_sum(values[plane : plane + taps], weights[view])
                first_pass[view, plane, here, :] = part
        return carry

    lax.fori_loop(0, rows // SUB, along_z, 0, unroll=2)

    for start in [*range(0, wide, SUB), *range(wide + rows, 2 * wide + rows, SUB)]:
        here = slice(start, start + SUB)
        values = [estimate[plane, here, :] for plane in range(planes + 4 * margin)]
        for view in range(views):
            for plane in range(mid_planes):
                first_pass[view, plane, here, :] = taps_sum(values[plane : plane + taps], weights[view])

    for view in range(views):
        blurred = rows_blurred([first_pass[view, plane] for plane in range(mid_planes)], row_band_ref[view, 0])
        blurred = columns_blurred(
            jnp.concatenate([plane[:mid_rows] for plane in blurred], axis=0), col_band_ref[view, 0]
        )
        ratio[view] = joined[view, :, margin : margin + mid_rows, :] / blurred.reshape(mid_planes, mid_rows, cols)

    def back_z(tile, carry):
        here = pl.ds(pl.multiple_of(tile * SUB, SUB), SUB)
        for view in range(views):
            values = [ratio[view, plane, here, :] for plane in range(mid_planes)]
            for plane in range(planes):
                back_first[view, plane, here, :] = taps_sum(values[plane : plane + taps], weights[view][::-1])
        return carry

    lax.fori_loop(0, mid_rows // SUB, back_z, 0, unroll=True)

    logs = None
    for view in range(views):
        back_first[view, :, mid_rows:, :] = jnp.zeros((planes, 2 * margin, cols), F32)
        blurred = rows_blurred([back_first[view, plane] for plane in range(planes)], row_band_ref[view, 1][:rows])
        correction = columns_blurred(jnp.concatenate(blurred, axis=0), col_band_ref[view, 1])
        one = jnp.log(correction)
        logs = one if logs is None else logs + one
    out_ref[...] = estimate[wide : wide + planes, body] * jnp.exp(logs / views).reshape(planes, rows, cols)
    if first:
        for copy in copies:
            copy.wait()


def update(weights, bands, partial, halves, below, above, low_rows, high_rows, own, later, margin):
    first = not later
    arrays = [weights, *bands, below, above, low_rows, high_rows, *partial, *halves] + list(own if first else later)
    views = len(halves) // 2
    _, rows, cols = below.shape
    planes = CZ
    mid_planes, mid_rows = planes + 2 * margin, rows + 2 * margin
    scratch = [
        (planes + 4 * margin, rows + 4 * margin),
        (views, mid_planes, rows + 4 * margin),
        (views, mid_planes, rows + 4 * margin),
        (views, mid_planes, mid_rows),
        (views, planes, rows + 4 * margin),
    ]
    out_shape = jax.ShapeDtypeStruct((planes, rows, cols), F32)
    copy_shape = jax.ShapeDtypeStruct((planes * rows, cols), F32)
    return pl.pallas_call(
        functools.partial(update_kernel, views=views, margin=margin, first=first, prepared=bool(partial)),
        in_specs=[VMEM] * len(arrays),
        out_specs=[VMEM, HBM] if first else VMEM,
        out_shape=[out_shape, copy_shape] if first else out_shape,
        scratch_shapes=[pltpu.VMEM(shape + (cols,), F32) for shape in scratch] + [pltpu.SemaphoreType.DMA((2,))] * first,
        compiler_params=pltpu.CompilerParams(vmem_limit_bytes=VMEM_BYTES),
        name="update",
    )(*arrays)


def from_beside(axis, upward, downward):
    count = lax.axis_size(axis)
    up = [(i, i + 1) for i in range(count - 1)]
    down = [(target, source) for source, target in up]
    return lax.ppermute(upward, axis, up), lax.ppermute(downward, axis, down)


def from_slabs_beside(upward, downward):
    turned = (lax.axis_index("gz") + lax.axis_index("gy")) % 2 == 1
    if upward is downward:
        sends = (upward, downward)
    else:
        sends = (jnp.where(turned, downward, upward), jnp.where(turned, upward, downward))
    ahead = gz_pairs(lambda place, odd: place - 1 if (place + odd) % 2 else place + 1)
    behind = gz_pairs(lambda place, odd: place + 1 if (place + odd) % 2 else place - 1)
    first = lax.ppermute(sends[0], ("gz", "gy"), ahead)
    second = lax.ppermute(sends[1], ("gz", "gy"), behind)
    return jnp.where(turned, first, second), jnp.where(turned, second, first)


def from_slabs_shifted(upward, downward):
    odd = lax.axis_index("gy") % 2 == 1
    if upward is downward:
        sends = (upward, downward)
    else:
        sends = (jnp.where(odd, downward, upward), jnp.where(odd, upward, downward))
    first = lax.ppermute(sends[0], ("gz", "gy"), gz_pairs(lambda place, odd: place - 1 if odd else place + 1))
    second = lax.ppermute(sends[1], ("gz", "gy"), gz_pairs(lambda place, odd: place + 1 if odd else place - 1))
    return jnp.where(odd, second, first), jnp.where(odd, first, second)


def edge_rows(pieces, width):
    count = lax.axis_size("gy")
    rows = pieces[0].shape[-2]
    if count == 2:
        at = jnp.where(lax.axis_index("gy") == 0, rows - width, 0)
        parts = [lax.dynamic_slice_in_dim(piece, at, width, axis=1) for piece in pieces]
        arrived = lax.ppermute(jnp.concatenate(parts), "gy", [(0, 1), (1, 0)])
        return arrived, arrived
    upward = jnp.concatenate([piece[:, rows - width :] for piece in pieces])
    downward = jnp.concatenate([piece[:, :width] for piece in pieces])
    return from_beside("gy", upward, downward)


def band_matrix(kernels, length, margin):
    places = jnp.arange(length, dtype=jnp.int32)
    shift = places[None, :] - places[:, None] + margin
    taps = kernels.shape[-1]
    return sum(jnp.where(shift == tap, kernels[:, tap, None, None], 0.0) for tap in range(taps))


def from_views(message):
    count = lax.axis_size("view")
    if count == 2:
        return [message, lax.ppermute(message, "view", [(0, 1), (1, 0)])]
    gathered = lax.all_gather(message, "view")
    return [gathered[view] for view in range(count)]


def on_device(camera, background, destination, offsets, shift_frac, psf_taps):
    slabs = lax.axis_size("gz")
    views = lax.axis_size("view")
    _, blocks, _, rows, cols = camera.shape
    taps = psf_taps.shape[-1]
    margin = taps // 2
    assert margin == HALF
    fraction = shift_frac[0]
    shares = deposit(
        camera[0], destination.reshape(blocks), offsets.reshape(blocks), background.reshape(1), fraction, slabs
    )
    small = jnp.concatenate(
        [
            jnp.pad(psf_taps[0], ((0, 0), (0, cols - taps))),
            jnp.broadcast_to(fraction[1:, None], (2, cols)),
            jnp.zeros((SUB - 5, cols), F32),
        ]
    )
    own, messages = [], []
    counts = None
    for terms in butterfly(shares, slabs, section_sizes(rows)):
        if counts is None:
            message, counts = join(small, counts, terms, rows)
        else:
            message = join(small, counts, terms, rows)
        own.append(message)
        messages.append(from_views(message))
    halves = [messages[half][view] for view in range(views) for half in range(2)]
    low_half, high_half = (
        [message[: HALF * rows].reshape(HALF, rows, cols) for message in messages[half]] for half in range(2)
    )
    upward = jnp.concatenate(high_half + [sum(low_half) / views])
    downward = jnp.concatenate(low_half + [sum(high_half) / views])
    below, above = from_slabs_shifted(upward, downward)
    wide = 2 * margin
    pieces = [part for view in range(views) for part in (low_half[view], high_half[view])]
    low_rows, high_rows = edge_rows([below, above] + pieces, wide)

    all_taps = jnp.stack([message[HALF * rows : HALF * rows + 3, :taps] for message in messages[0]])
    kernels = all_taps / jnp.sum(all_taps, axis=-1, keepdims=True)
    row_bands = jnp.stack([band_matrix(kernels[:, 1, ::order], rows + 4 * margin, 0) for order in (1, -1)], axis=1)
    high_part = lax.reduce_precision(row_bands, 8, 7)
    row_bands = jnp.concatenate([high_part, high_part, row_bands - high_part], axis=-1).astype(jnp.bfloat16)
    col_bands = jnp.stack([band_matrix(kernels[:, 2, ::order], cols, margin) for order in (1, -1)], axis=1)
    col_bands = jnp.swapaxes(col_bands, -1, -2)
    high_part = lax.reduce_precision(col_bands, 8, 7)
    col_bands = jnp.concatenate([high_part, col_bands - high_part], axis=-1).astype(jnp.bfloat16)
    bands = (row_bands, jnp.concatenate([col_bands, col_bands], axis=-2))
    row_band = lax.axis_index("gy")
    flags = jnp.stack([row_band > 0, row_band < lax.axis_size("gy") - 1]).astype(F32)
    weights = jnp.concatenate([kernels[:, 0].reshape(-1), flags])
    weights = jnp.broadcast_to(weights[:, None, None], (views * taps + 2, SUB, cols))

    later = ()
    for iteration in range(ITERS):
        if iteration:
            est_below, est_above = from_slabs_beside(estimate, estimate)
            later = (estimate, est_below, est_above) + edge_rows([est_below, estimate, est_above], wide)
        partial = [] if iteration else [prepare(weights, halves, views, margin, rows)]
        result = update(weights, bands, partial, halves, below, above, low_rows, high_rows, own, later, margin)
        estimate = result if later else result[0]
        joined = joined if later else result[1]
    return (estimate, joined.reshape(1, CZ, rows, cols))


def solution(mesh):
    return jax.shard_map(
        on_device,
        mesh=mesh,
        in_specs=(
            P("view", ("groups", "gz"), None, "gy", None),
            P("view", "gy", ("groups", "gz")),
            P("view", "gy", ("groups", "gz"), None),
            P("view", "gy", ("groups", "gz")),
            P("view", None),
            P("view", None, None),
        ),
        out_specs=(P(("groups", "gz"), "gy", None), P("view", ("groups", "gz"), "gy", None)),
        check_vma=False,
    )
```

```python
import functools

import jax
import jax.numpy as jnp
from jax import lax
from jax.experimental import pallas as pl
from jax.experimental.pallas import tpu as pltpu
from jax.sharding import PartitionSpec as P

CZ = 8
HALF = CZ // 2
ITERS = 2


DATA_FLOOR = 0.25
PRECISE = lax.Precision.HIGHEST
F32 = jnp.float32
SUB = 8
VMEM = pl.BlockSpec(memory_space=pltpu.VMEM)
HBM = pl.BlockSpec(memory_space=pltpu.HBM)
VMEM_BYTES = 48 * 1024 * 1024
DEPOSIT_VMEM_BYTES = 60 * 1024 * 1024


def bit_count(count):
    bits = count.bit_length() - 1
    assert count == 1 << bits
    return bits


def step_bits(slabs, odd):
    order = list(range(bit_count(slabs)))
    if odd and len(order) > 1:
        order[:2] = [1, 0]
    return order


def section_of(value, order):
    result = 0
    for step, bit in enumerate(order):
        result = result | (((value >> bit) & 1) << (len(order) - 1 - step))
    return result


def deposit_kernel(
    target_hbm, first_hbm, level_hbm, fraction_hbm, camera_hbm, *rest, slabs, sections, chunk
):
    *out_refs, sums_ref, target, first, level, fraction, camera, small_sems, camera_sems = rest
    blocks, planes, rows, cols = camera.shape
    sources = ((target_hbm, target), (first_hbm, first), (level_hbm, level), (fraction_hbm, fraction))
    smalls = [pltpu.make_async_copy(*pair, small_sems.at[i]) for i, pair in enumerate(sources)]
    parts = []
    for i in range(blocks // chunk):
        here = pl.ds(i * chunk, chunk)
        parts.append(pltpu.make_async_copy(camera_hbm.at[here], camera.at[here], camera_sems.at[i]))
    for copy in smalls + parts:
        copy.start()
    sums_ref[...] = jnp.zeros(sums_ref.shape, F32)
    for copy in smalls:
        copy.wait()
    quarter = slabs // 4

    def section_row(half, slab):
        size = jnp.where(half == 0, sections[0], sections[1])
        if not quarter:
            return half * slabs * sections[0] + slab * size
        last = 3 * quarter * sum(sections) + half * quarter * sections[0] + (slab - 3 * quarter) * size
        return jnp.where(slab < 3 * quarter, half * 3 * quarter * sections[0] + slab * size, last)

    place = lax.axis_index("gz").astype(jnp.int32)
    odd = lax.axis_index("gy") % 2 == 1
    base_level = level[0].astype(F32)
    upper_share = fraction[0]
    lower_share = 1.0 - upper_share
    count_at = lax.broadcasted_iota(jnp.int32, (CZ, cols), 0)

    def one(block, carry):
        away = target[block] ^ place
        slab = jnp.where(odd, section_of(away, step_bits(slabs, True)), section_of(away, step_bits(slabs, False)))
        at = first[block]
        lower = camera[block, 0] - base_level
        landings = []
        for plane in range(planes - 1):
            upper = camera[block, plane + 1] - base_level
            lands = at + plane
            half = lands // HALF
            start = section_row(half, slab)
            here = pl.ds(pl.multiple_of(start + (lands - half * HALF) * rows, SUB), rows)
            landings.append((here, lower_share * lower + upper_share * upper))
            lower = upper
        counts = pl.ds(pl.multiple_of(section_row(0, slab) + HALF * rows, SUB), CZ)
        landings.append((counts, ((count_at >= at) & (count_at < at + planes - 1)).astype(F32)))
        sums = [sums_ref[here, :] + value for here, value in landings]
        for (here, _), value in zip(landings, sums):
            sums_ref[here, :] = value
        return carry

    for i, copy in enumerate(parts):
        copy.wait()
        lax.fori_loop(i * chunk, (i + 1) * chunk, one, 0, unroll=True)
    at = 0
    for out_ref in out_refs:
        out_ref[...] = sums_ref[at : at + out_ref.shape[0]]
        at += out_ref.shape[0]


def deposit(camera, target, first, level, fraction, slabs):
    blocks, planes, rows, cols = camera.shape
    sections = section_sizes(rows)
    chunk = HALF if blocks % HALF == 0 else blocks
    return pl.pallas_call(
        functools.partial(deposit_kernel, slabs=slabs, sections=sections, chunk=chunk),
        in_specs=[HBM] * 5,
        out_specs=[VMEM] * len(first_shares(slabs, sections)),
        out_shape=[jax.ShapeDtypeStruct((size, cols), F32) for size in first_shares(slabs, sections)],
        scratch_shapes=[
            pltpu.VMEM((slabs * sum(sections), cols), F32),
            pltpu.SMEM(target.shape, jnp.int32),
            pltpu.SMEM(first.shape, jnp.int32),
            pltpu.SMEM(level.shape, jnp.int32),
            pltpu.SMEM(fraction.shape, F32),
            pltpu.VMEM(camera.shape, F32),
            pltpu.SemaphoreType.DMA((4,)),
            pltpu.SemaphoreType.DMA((blocks // chunk,)),
        ],
        compiler_params=pltpu.CompilerParams(vmem_limit_bytes=DEPOSIT_VMEM_BYTES),
        name="deposit",
    )(target, first, level, fraction, camera)


def gz_pairs(partner):
    count, bands = lax.axis_size("gz"), lax.axis_size("gy")
    pairs = []
    for place in range(count):
        for band in range(bands):
            other = partner(place, band % 2 == 1)
            if 0 <= other < count:
                pairs.append((place * bands + band, other * bands + band))
    return pairs


def section_sizes(rows):
    return HALF * rows + CZ, HALF * rows


def first_shares(slabs, sections):
    if slabs <= 2:
        return [size for size in sections for _ in range(slabs)]
    quarter = slabs // 4
    return [quarter * size for size in sections for _ in range(3)] + [quarter * sum(sections)]


def fetch_kernel(*refs):
    sources, targets, sems = refs[: len(refs) // 2], refs[len(refs) // 2 : -1], refs[-1]
    copies = [pltpu.make_async_copy(*pair, sems.at[i]) for i, pair in enumerate(zip(sources, targets))]
    for copy in copies:
        copy.start()
    for copy in copies:
        copy.wait()


def fetch(*arrays):
    return pl.pallas_call(
        fetch_kernel,
        in_specs=[HBM] * len(arrays),
        out_specs=[VMEM] * len(arrays),
        out_shape=[jax.ShapeDtypeStruct(array.shape, array.dtype) for array in arrays],
        scratch_shapes=[pltpu.SemaphoreType.DMA((len(arrays),))],
        compiler_params=pltpu.CompilerParams(vmem_limit_bytes=VMEM_BYTES),
        name="fetch",
    )(*arrays)


def add_kernel(left_ref, right_ref, out_ref):
    out_ref[...] = left_ref[...] + right_ref[...]


def add(left, right):
    return pl.pallas_call(
        add_kernel,
        in_specs=[VMEM] * 2,
        out_specs=VMEM,
        out_shape=jax.ShapeDtypeStruct(left.shape, F32),
        compiler_params=pltpu.CompilerParams(vmem_limit_bytes=VMEM_BYTES),
        name="add",
    )(left, right)


def butterfly(shares, slabs, sections):
    if slabs == 1:
        return [(share,) for share in shares]
    if slabs == 2:
        halves = [shares[:2], shares[2:]]
    else:
        halves, onward = [shares[:3], shares[3:6]], shares[6]
    for step in range(bit_count(slabs)):
        pairs = gz_pairs(lambda place, odd: place ^ (1 << step_bits(slabs, odd)[step]))

        def exchange(array):
            return lax.ppermute(array, ("gz", "gy"), pairs)

        if step == bit_count(slabs) - 1:
            return [(*keeps, exchange(send)) for *keeps, send in halves]
        if step == 0:
            fetched = fetch(*(half[1] for half in halves), *(half[0] for half in halves))
            halves = [[fetched[2 + i], fetched[i], half[2]] for i, half in enumerate(halves)]
        onward = exchange(onward)
        stays = [exchange(half[2]) for half in halves]
        cut = stays[0].shape[0]
        sends = [add(half[1], array) for half, array in zip(halves, (onward[:cut], onward[cut:]))]
        if cut == sections[0]:
            halves = [(half[0], array, send) for half, array, send in zip(halves, stays, sends)]
        else:
            keeps = [add(half[0], array) for half, array in zip(halves, stays)]
            cuts = [keep.shape[0] // 2 for keep in keeps]
            halves = [(keep[:cut], keep[cut:], send[:cut]) for cut, keep, send in zip(cuts, keeps, sends)]
            onward = jnp.concatenate([send[cut:] for cut, send in zip(cuts, sends)])


def join_kernel(small_ref, *rest, rows, half):
    if half == 0:
        *term_refs, message_ref, count_ref = rest
    else:
        count_ref, *term_refs, message_ref = rest
    cols = message_ref.shape[1]
    total = term_refs[0][...]
    for term_ref in term_refs[1:]:
        total = total + term_ref[...]
    planes = total[: HALF * rows].reshape(HALF, rows, cols)
    if half == 0:
        counts = total[HALF * rows :]
        count_ref[...] = counts
    else:
        counts = count_ref[HALF:]
    fy, fx = small_ref[3:4], small_ref[4:5]
    row_at = lax.broadcasted_iota(jnp.int32, (rows, cols), 0)
    col_at = lax.broadcasted_iota(jnp.int32, (rows, cols), 1)
    for plane in range(HALF):
        part = planes[plane]
        follow = jnp.where(row_at == rows - 1, part, pltpu.roll(part, rows - 1, 0))
        part = (1.0 - fy) * part + fy * follow
        follow = jnp.where(col_at == cols - 1, part, pltpu.roll(part, cols - 1, 1))
        part = (1.0 - fx) * part + fx * follow
        part = jnp.maximum(part * (1.0 / (counts[plane : plane + 1] + 1.0)), DATA_FLOOR)
        message_ref[plane * rows : (plane + 1) * rows] = part
    if half == 0:
        message_ref[HALF * rows :] = small_ref[...]


def join(small, counts, terms, rows):
    half = 0 if counts is None else 1
    arrays = [small, *terms] if half == 0 else [small, counts, *terms]
    message = jax.ShapeDtypeStruct(terms[0].shape, F32)
    return pl.pallas_call(
        functools.partial(join_kernel, rows=rows, half=half),
        in_specs=[VMEM] * len(arrays),
        out_specs=[VMEM] * 2 if half == 0 else VMEM,
        out_shape=[message, jax.ShapeDtypeStruct(small.shape, F32)] if half == 0 else message,
        compiler_params=pltpu.CompilerParams(vmem_limit_bytes=VMEM_BYTES),
        name="join",
    )(*arrays)


def taps_sum(values, weights):
    result = weights[0] * values[0]
    for offset in range(1, len(weights)):
        result = result + weights[offset] * values[offset]
    return result


def parts_of(values):
    top = values.astype(jnp.bfloat16)
    return top, (values - top.astype(F32)).astype(jnp.bfloat16)


def columns_blurred(values, bands):
    cols = values.shape[1]
    both = jnp.dot(jnp.concatenate(parts_of(values), axis=1), bands, preferred_element_type=F32)
    return both[:, :cols] + both[:, cols:]


def rows_blurred(planes, bands):
    results = []
    for at in range(0, len(planes), 2):
        stacks = []
        for plane in planes[at : at + 2]:
            top, rest = parts_of(plane)
            stacks.append(jnp.concatenate([top, rest, top], axis=0))
        both = jnp.dot(bands, jnp.concatenate(stacks, axis=1), preferred_element_type=F32)
        cols = planes[at].shape[1]
        results += [both[:, index * cols : (index + 1) * cols] for index in range(len(stacks))]
    return results


def prepare_kernel(weight_ref, *rest, views, margin, first):
    *sources, out_ref = rest
    _, mid_planes, rows, cols = out_ref.shape
    planes = mid_planes - 2 * margin
    taps = 2 * margin + 1
    weights = [[weight_ref[view * taps + tap] for tap in range(taps)] for view in range(views)]

    def one(tile, carry):
        here = pl.ds(pl.multiple_of(tile * SUB, SUB), SUB)
        values = []
        for plane in range(planes):
            if first:
                start = plane % HALF * rows + tile * SUB
                there = pl.ds(pl.multiple_of(start, SUB), SUB)
                value = sources[plane // HALF][there, :]
                for view in range(1, views):
                    value = value + sources[2 * view + plane // HALF][there, :]
                values.append(value / views)
            else:
                values.append(sources[0][plane, here, :])
        for view in range(views):
            for plane in range(mid_planes):
                pairs = [(tap, plane + tap - 2 * margin) for tap in range(taps) if 0 <= plane + tap - 2 * margin < planes]
                out_ref[view, plane, here, :] = taps_sum(
                    [values[at] for _, at in pairs], [weights[view][tap] for tap, _ in pairs]
                )
        return carry

    lax.fori_loop(0, rows // SUB, one, 0, unroll=2)


def prepare(weights, sources, views, margin, rows):
    first = len(sources) > 1
    cols = weights.shape[-1]
    return pl.pallas_call(
        functools.partial(prepare_kernel, views=views, margin=margin, first=first),
        in_specs=[VMEM] * (1 + len(sources)),
        out_specs=VMEM,
        out_shape=jax.ShapeDtypeStruct((views, CZ + 2 * margin, rows, cols), F32),
        compiler_params=pltpu.CompilerParams(vmem_limit_bytes=VMEM_BYTES),
        name="prepare",
    )(weights, *sources)


def update_kernel(
    weight_ref, row_band_ref, col_band_ref, below_ref, above_ref, low_rows_ref, high_rows_ref, *rest,
    views, margin, first, prepared
):
    if prepared:
        partial_ref, *rest = rest
    halves, rest = rest[: 2 * views], rest[2 * views :]
    if first:
        *own_refs, out_ref, copied_hbm, estimate, joined, first_pass, ratio, back_first, sems = rest
    else:
        est_ref, est_below_ref, est_above_ref, est_low_ref, est_high_ref, out_ref, *scratch = rest
        estimate, joined, first_pass, ratio, back_first = scratch
    planes, rows, cols = out_ref.shape
    if first:
        length = HALF * rows
        copies = [
            pltpu.make_async_copy(ref.at[pl.ds(0, length)], copied_hbm.at[pl.ds(i * length, length)], sems.at[i])
            for i, ref in enumerate(own_refs)
        ]
        for copy in copies:
            copy.start()
    taps = 2 * margin + 1
    wide = 2 * margin
    flag_low, flag_high = weight_ref[views * taps], weight_ref[views * taps + 1]
    low, body, high = slice(0, wide), slice(wide, wide + rows), slice(wide + rows, 2 * wide + rows)

    above_at = below_ref.shape[0]
    own_at = 2 * above_at
    for view in range(views):
        here = slice(view * margin, (view + 1) * margin)
        pieces = [(0, margin, below_ref[here], view * margin)]
        for half in range(2):
            own = halves[2 * view + half][: HALF * rows].reshape(HALF, rows, cols)
            pieces.append((margin + half * HALF, HALF, own, own_at + (2 * view + half) * HALF))
        pieces.append((margin + planes, margin, above_ref[here], above_at + view * margin))
        for to, length, source, edge_at in pieces:
            joined[view, to : to + length, body] = source
            joined[view, to : to + length, low] = low_rows_ref[edge_at : edge_at + length] * flag_low
            joined[view, to : to + length, high] = high_rows_ref[edge_at : edge_at + length] * flag_high
    if first:
        inner = joined[0]
        for view in range(1, views):
            inner = inner + joined[view]
        estimate[margin : planes + 3 * margin] = inner / views
        at = views * margin
        for to, source, edge_at in ((0, below_ref, at), (planes + 3 * margin, above_ref, above_at + at)):
            estimate[to : to + margin, body] = source[at : at + margin]
            estimate[to : to + margin, low] = low_rows_ref[edge_at : edge_at + margin] * flag_low
            estimate[to : to + margin, high] = high_rows_ref[edge_at : edge_at + margin] * flag_high
    else:
        for index, source in enumerate((est_below_ref, est_ref, est_above_ref)):
            here = slice(index * planes, (index + 1) * planes)
            estimate[here, body] = source[...]
            estimate[here, low] = est_low_ref[here] * flag_low
            estimate[here, high] = est_high_ref[here] * flag_high

    mid_planes, mid_rows = planes + 2 * margin, rows + 2 * margin
    weights = [[weight_ref[view * taps + tap] for tap in range(taps)] for view in range(views)]

    near = range(2 * margin, 2 * margin + planes) if prepared else ()

    def along_z(tile, carry):
        here = pl.ds(pl.multiple_of(wide + tile * SUB, SUB), SUB)
        there = pl.ds(pl.multiple_of(tile * SUB, SUB), SUB)
        values = [None if plane in near else estimate[plane, here, :] for plane in range(planes + 4 * margin)]
        for view in range(views):
            for plane in range(mid_planes):
                if prepared:
                    part = partial_ref[view, plane, there, :]
                    for tap in range(taps):
                        if plane + tap not in near:
                            part = part + weights[view][tap] * values[plane + tap]
                else:
                    part = taps_sum(values[plane : plane + taps], weights[view])
                first_pass[view, plane, here, :] = part
        return carry

    lax.fori_loop(0, rows // SUB, along_z, 0, unroll=2)

    for start in [*range(0, wide, SUB), *range(wide + rows, 2 * wide + rows, SUB)]:
        here = slice(start, start + SUB)
        values = [estimate[plane, here, :] for plane in range(planes + 4 * margin)]
        for view in range(views):
            for plane in range(mid_planes):
                first_pass[view, plane, here, :] = taps_sum(values[plane : plane + taps], weights[view])

    for view in range(views):
        blurred = rows_blurred([first_pass[view, plane] for plane in range(mid_planes)], row_band_ref[view, 0])
        blurred = columns_blurred(
            jnp.concatenate([plane[:mid_rows] for plane in blurred], axis=0), col_band_ref[view, 0]
        )
        ratio[view] = joined[view, :, margin : margin + mid_rows, :] / blurred.reshape(mid_planes, mid_rows, cols)

    def back_z(tile, carry):
        here = pl.ds(pl.multiple_of(tile * SUB, SUB), SUB)
        for view in range(views):
            values = [ratio[view, plane, here, :] for plane in range(mid_planes)]
            for plane in range(planes):
                back_first[view, plane, here, :] = taps_sum(values[plane : plane + taps], weights[view][::-1])
        return carry

    lax.fori_loop(0, mid_rows // SUB, back_z, 0, unroll=True)

    logs = None
    for view in range(views):
        back_first[view, :, mid_rows:, :] = jnp.zeros((planes, 2 * margin, cols), F32)
        blurred = rows_blurred([back_first[view, plane] for plane in range(planes)], row_band_ref[view, 1][:rows])
        correction = columns_blurred(jnp.concatenate(blurred, axis=0), col_band_ref[view, 1])
        one = jnp.log(correction)
        logs = one if logs is None else logs + one
    out_ref[...] = estimate[wide : wide + planes, body] * jnp.exp(logs / views).reshape(planes, rows, cols)
    if first:
        for copy in copies:
            copy.wait()


def update(weights, bands, partial, halves, below, above, low_rows, high_rows, own, later, margin):
    first = not later
    arrays = [weights, *bands, below, above, low_rows, high_rows, *partial, *halves] + list(own if first else later)
    views = len(halves) // 2
    _, rows, cols = below.shape
    planes = CZ
    mid_planes, mid_rows = planes + 2 * margin, rows + 2 * margin
    scratch = [
        (planes + 4 * margin, rows + 4 * margin),
        (views, mid_planes, rows + 4 * margin),
        (views, mid_planes, rows + 4 * margin),
        (views, mid_planes, mid_rows),
        (views, planes, rows + 4 * margin),
    ]
    out_shape = jax.ShapeDtypeStruct((planes, rows, cols), F32)
    copy_shape = jax.ShapeDtypeStruct((planes * rows, cols), F32)
    return pl.pallas_call(
        functools.partial(update_kernel, views=views, margin=margin, first=first, prepared=bool(partial)),
        in_specs=[VMEM] * len(arrays),
        out_specs=[VMEM, HBM] if first else VMEM,
        out_shape=[out_shape, copy_shape] if first else out_shape,
        scratch_shapes=[pltpu.VMEM(shape + (cols,), F32) for shape in scratch] + [pltpu.SemaphoreType.DMA((2,))] * first,
        compiler_params=pltpu.CompilerParams(vmem_limit_bytes=VMEM_BYTES),
        name="update",
    )(*arrays)


def from_beside(axis, upward, downward):
    count = lax.axis_size(axis)
    up = [(i, i + 1) for i in range(count - 1)]
    down = [(target, source) for source, target in up]
    return lax.ppermute(upward, axis, up), lax.ppermute(downward, axis, down)


def from_slabs_beside(upward, downward):
    turned = (lax.axis_index("gz") + lax.axis_index("gy")) % 2 == 1
    if upward is downward:
        sends = (upward, downward)
    else:
        sends = (jnp.where(turned, downward, upward), jnp.where(turned, upward, downward))
    ahead = gz_pairs(lambda place, odd: place - 1 if (place + odd) % 2 else place + 1)
    behind = gz_pairs(lambda place, odd: place + 1 if (place + odd) % 2 else place - 1)
    first = lax.ppermute(sends[0], ("gz", "gy"), ahead)
    second = lax.ppermute(sends[1], ("gz", "gy"), behind)
    return jnp.where(turned, first, second), jnp.where(turned, second, first)


def from_slabs_shifted(upward, downward):
    odd = lax.axis_index("gy") % 2 == 1
    if upward is downward:
        sends = (upward, downward)
    else:
        sends = (jnp.where(odd, downward, upward), jnp.where(odd, upward, downward))
    first = lax.ppermute(sends[0], ("gz", "gy"), gz_pairs(lambda place, odd: place - 1 if odd else place + 1))
    second = lax.ppermute(sends[1], ("gz", "gy"), gz_pairs(lambda place, odd: place + 1 if odd else place - 1))
    return jnp.where(odd, second, first), jnp.where(odd, first, second)


def edge_rows(pieces, width):
    count = lax.axis_size("gy")
    rows = pieces[0].shape[-2]
    if count == 2:
        at = jnp.where(lax.axis_index("gy") == 0, rows - width, 0)
        parts = [lax.dynamic_slice_in_dim(piece, at, width, axis=1) for piece in pieces]
        arrived = lax.ppermute(jnp.concatenate(parts), "gy", [(0, 1), (1, 0)])
        return arrived, arrived
    upward = jnp.concatenate([piece[:, rows - width :] for piece in pieces])
    downward = jnp.concatenate([piece[:, :width] for piece in pieces])
    return from_beside("gy", upward, downward)


def band_matrix(kernels, length, margin):
    places = jnp.arange(length, dtype=jnp.int32)
    shift = places[None, :] - places[:, None] + margin
    taps = kernels.shape[-1]
    return sum(jnp.where(shift == tap, kernels[:, tap, None, None], 0.0) for tap in range(taps))


def from_views(message):
    count = lax.axis_size("view")
    if count == 2:
        return [message, lax.ppermute(message, "view", [(0, 1), (1, 0)])]
    gathered = lax.all_gather(message, "view")
    return [gathered[view] for view in range(count)]


def on_device(camera, background, destination, offsets, shift_frac, psf_taps):
    slabs = lax.axis_size("gz")
    views = lax.axis_size("view")
    _, blocks, _, rows, cols = camera.shape
    taps = psf_taps.shape[-1]
    margin = taps // 2
    assert margin == HALF
    fraction = shift_frac[0]
    shares = deposit(
        camera[0], destination.reshape(blocks), offsets.reshape(blocks), background.reshape(1), fraction, slabs
    )
    small = jnp.concatenate(
        [
            jnp.pad(psf_taps[0], ((0, 0), (0, cols - taps))),
            jnp.broadcast_to(fraction[1:, None], (2, cols)),
            jnp.zeros((SUB - 5, cols), F32),
        ]
    )
    own, messages = [], []
    counts = None
    for terms in butterfly(shares, slabs, section_sizes(rows)):
        if counts is None:
            message, counts = join(small, counts, terms, rows)
        else:
            message = join(small, counts, terms, rows)
        own.append(message)
        messages.append(from_views(message))
    halves = [messages[half][view] for view in range(views) for half in range(2)]
    low_half, high_half = (
        [message[: HALF * rows].reshape(HALF, rows, cols) for message in messages[half]] for half in range(2)
    )
    upward = jnp.concatenate(high_half + [sum(low_half) / views])
    downward = jnp.concatenate(low_half + [sum(high_half) / views])
    below, above = from_slabs_shifted(upward, downward)
    wide = 2 * margin
    pieces = [part for view in range(views) for part in (low_half[view], high_half[view])]
    low_rows, high_rows = edge_rows([below, above] + pieces, wide)

    all_taps = jnp.stack([message[HALF * rows : HALF * rows + 3, :taps] for message in messages[0]])
    kernels = all_taps / jnp.sum(all_taps, axis=-1, keepdims=True)
    row_bands = jnp.stack([band_matrix(kernels[:, 1, ::order], rows + 4 * margin, 0) for order in (1, -1)], axis=1)
    high_part = lax.reduce_precision(row_bands, 8, 7)
    row_bands = jnp.concatenate([high_part, high_part, row_bands - high_part], axis=-1).astype(jnp.bfloat16)
    col_bands = jnp.stack([band_matrix(kernels[:, 2, ::order], cols, margin) for order in (1, -1)], axis=1)
    col_bands = jnp.swapaxes(col_bands, -1, -2)
    high_part = lax.reduce_precision(col_bands, 8, 7)
    col_bands = jnp.concatenate([high_part, col_bands - high_part], axis=-1).astype(jnp.bfloat16)
    bands = (row_bands, jnp.concatenate([col_bands, col_bands], axis=-2))
    row_band = lax.axis_index("gy")
    flags = jnp.stack([row_band > 0, row_band < lax.axis_size("gy") - 1]).astype(F32)
    weights = jnp.concatenate([kernels[:, 0].reshape(-1), flags])
    weights = jnp.broadcast_to(weights[:, None, None], (views * taps + 2, SUB, cols))

    later = ()
    for iteration in range(ITERS):
        if iteration:
            est_below, est_above = from_slabs_beside(estimate, estimate)
            later = (estimate, est_below, est_above) + edge_rows([est_below, estimate, est_above], wide)
        partial = [] if iteration else [prepare(weights, halves, views, margin, rows)]
        result = update(weights, bands, partial, halves, below, above, low_rows, high_rows, own, later, margin)
        estimate = result if later else result[0]
        joined = joined if later else result[1]
    return (estimate, joined.reshape(1, CZ, rows, cols))


def solution(mesh):
    return jax.shard_map(
        on_device,
        mesh=mesh,
        in_specs=(
            P("view", ("groups", "gz"), None, "gy", None),
            P("view", "gy", ("groups", "gz")),
            P("view", "gy", ("groups", "gz"), None),
            P("view", "gy", ("groups", "gz")),
            P("view", None),
            P("view", None, None),
        ),
        out_specs=(P(("groups", "gz"), "gy", None), P("view", ("groups", "gz"), "gy", None)),
        check_vma=False,
    )
```
